32 devices in a mesh: fsdp: 8 (over z, x), rep: 4 (over y, core).
Axes of the slice: x: 2, y: 2, z: 4, core: 2. Of those that a mesh axis runs over, the one named last changes fastest.
Arguments:
- tokens: bfloat16 [16384, 2048], P(('fsdp', 'rep')), may hold values from -6 to 6
- segments: int32 [16384], P(('fsdp', 'rep')), may hold values from 0 to 255, never falling along the last dimension, each value on 1 to 128 neighbouring positions
- cotangent: bfloat16 [16384, 2048], P(('fsdp', 'rep')), may hold values from -6 to 6
- gain_one: bfloat16 [2048], P(('fsdp', 'rep')), may hold values from 0.5 to 1.5
- w_query: bfloat16 [2048, 2048], P(('fsdp', 'rep')), may hold values from -0.125 to 0.125
- w_key: bfloat16 [2048, 2048], P(('fsdp', 'rep')), may hold values from -0.125 to 0.125
- w_value: bfloat16 [2048, 4096], P(('fsdp', 'rep')), may hold values from -0.125 to 0.125
- w_gate: bfloat16 [2048, 4096], P(('fsdp', 'rep')), may hold values from -0.125 to 0.125
- w_beta: bfloat16 [2048, 16], P(('fsdp', 'rep')), may hold values from -0.125 to 0.125
- w_alpha: bfloat16 [2048, 16], P(('fsdp', 'rep')), may hold values from -0.125 to 0.125
- conv_q: bfloat16 [4, 2048], P(None, ('fsdp', 'rep')), may hold values from -3 to 3
- conv_k: bfloat16 [4, 2048], P(None, ('fsdp', 'rep')), may hold values from -3 to 3
- conv_v: bfloat16 [4, 4096], P(None, ('fsdp', 'rep')), may hold values from -3 to 3
- a_log: float32 [16], replicated, may hold values from 0 to 2.77
- dt_bias: float32 [16], replicated, may hold values from -6 to -2
- norm_gain: bfloat16 [256], P(('fsdp', 'rep')), may hold values from 0.5 to 1.5
- w_out: bfloat16 [4096, 2048], P(None, ('fsdp', 'rep')), may hold values from -0.1875 to 0.1875
- gain_two: bfloat16 [2048], P(('fsdp', 'rep')), may hold values from 0.5 to 1.5
- w_ffgate: bfloat16 [2048, 5632], P(('fsdp', 'rep')), may hold values from -0.125 to 0.125
- w_ffup: bfloat16 [2048, 5632], P(('fsdp', 'rep')), may hold values from -0.125 to 0.125
- w_down: bfloat16 [5632, 2048], P(None, ('fsdp', 'rep')), may hold values from -0.15625 to 0.15625
Outputs:
- output: bfloat16 [16384, 2048], P(('fsdp', 'rep'))
- grad_tokens: float32 [16384, 2048], P(('fsdp', 'rep'))
- grad_gain_one: float32 [2048], P(('fsdp', 'rep'))
- grad_w_query: float32 [2048, 2048], P(('fsdp', 'rep'))
- grad_w_key: float32 [2048, 2048], P(('fsdp', 'rep'))
- grad_w_value: float32 [2048, 4096], P(('fsdp', 'rep'))
- grad_w_gate: float32 [2048, 4096], P(('fsdp', 'rep'))
- grad_w_beta: float32 [2048, 16], P(('fsdp', 'rep'))
- grad_w_alpha: float32 [2048, 16], P(('fsdp', 'rep'))
- grad_conv_q: float32 [4, 2048], P(None, ('fsdp', 'rep'))
- grad_conv_k: float32 [4, 2048], P(None, ('fsdp', 'rep'))
- grad_conv_v: float32 [4, 4096], P(None, ('fsdp', 'rep'))
- grad_a_log: float32 [16], replicated
- grad_dt_bias: float32 [16], replicated
- grad_norm_gain: float32 [256], P(('fsdp', 'rep'))
- grad_w_out: float32 [4096, 2048], P(None, ('fsdp', 'rep'))
- grad_gain_two: float32 [2048], P(('fsdp', 'rep'))
- grad_w_ffgate: float32 [2048, 5632], P(('fsdp', 'rep'))
- grad_w_ffup: float32 [2048, 5632], P(('fsdp', 'rep'))
- grad_w_down: float32 [5632, 2048], P(None, ('fsdp', 'rep'))
The draws below stay inside these ranges and needn't reach their ends.
Inputs may be any that keep to these rules, and one draw needn't show every extreme that they name: `segments`: document numbers never fall along the tokens; a document covers 1 to 128 consecutive tokens.
All inputs are finite; a program needn't handle non-finite values.
Results may differ from the reference program's by a relative error of at most 0.011.
Values may be sent and summed in bfloat16 or wider, within the bound.
No kernel may reach another device: no remote copies, remote signals or barrier semaphores. Data moves between devices by JAX's collectives and lax.ppermute only.
A program may use at most 640 MiB of HBM per device.

```python
import math
import jax
import jax.numpy as jnp
import numpy as np
from jax import lax

D = 2048
HEADS = 16
DV = 256
FF = 5632
CONV = 4
SPAN = 64
SEQ = 256
HK = 2048
HV = 4096
TOK_DEV = 512
TOKENS = 16384


def block_scale(rng, extent, shards, least, top_value):
    factor_of, own = 1.0, jax.random.fold_in(rng, 6)
    for axis_at, parts in shards:
        steps = jnp.exp(jax.random.uniform(jax.random.fold_in(own, axis_at), (parts,), jnp.float32, least / len(shards), top_value / len(shards)))
        factor_of = factor_of * jnp.repeat(steps, extent[axis_at] // parts).reshape([-1 if axis == axis_at else 1 for axis in range(len(extent))])
    return factor_of


def split_up(amount, total, reach, lean):
    loads = [(1 << 20) // math.isqrt(standing ** lean) + 1 for standing in range(2, amount + 1)]
    rest, holding = total - reach - (amount - 1), [1] * (amount - 1)
    while rest > 0:
        free = [i for i in range(amount - 1) if holding[i] < reach]
        whole, left = sum([loads[i] for i in free]), rest
        for i in free:
            more = min(reach - holding[i], max(1, left * loads[i] // whole), rest)
            holding[i] = holding[i] + more
            rest = rest - more
    return np.array([reach] + holding)


def ragged_sizes(rng, amount, total, reach, skew):
    if amount == 2:
        one = jax.random.randint(rng, (), max(1, total - reach), min(reach, total - 1) + 1)
        return jnp.stack([one, total - one])
    sizes = jnp.asarray(split_up(amount, total, reach, skew), jnp.int32)
    couples = (amount - 1) // 2
    source_of, receiver = sizes[1:1 + 2 * couples:2], sizes[2:2 + 2 * couples:2]
    slack = jnp.minimum(source_of - 1, reach - receiver)
    moved = jax.random.randint(jax.random.fold_in(rng, 1), (couples,), 0, 1 << 20) % (slack + 1)
    sizes = sizes.at[1:1 + 2 * couples:2].set(source_of - moved).at[2:2 + 2 * couples:2].set(receiver + moved)
    return sizes[jax.random.permutation(jax.random.fold_in(rng, 2), amount)]


def bell_draw(stream_key, shape, spread, limit, shards=(), held_as=jnp.bfloat16):
    factor_of = block_scale(stream_key, shape, shards, -0.22, 0.18) if shards else 1.0
    drawn = jax.random.normal(stream_key, shape, jnp.float32) * spread * factor_of
    return jnp.minimum(jnp.maximum(drawn, -limit), limit).astype(held_as)


def setup_inputs(seed: int = 0) -> dict:
    arg_keys = jax.random.split(jax.random.key(seed), 22)
    tokens = bell_draw(arg_keys[0], (TOKENS, D), 1.0, 6.0, ((0, 32),))
    segments = jnp.searchsorted(jnp.cumsum(ragged_sizes(arg_keys[1], TOKENS * 4 // SEQ, TOKENS, SEQ // 2, 0)), jnp.arange(TOKENS), side="right").astype(jnp.int32)
    cotangent = bell_draw(arg_keys[2], (TOKENS, D), 1.0, 6.0, ((0, 32),))
    gain_one = jnp.clip(1.0 + 0.1 * jax.random.normal(arg_keys[3], (D,), jnp.float32), 0.5, 1.5).astype(jnp.bfloat16)
    w_query = bell_draw(arg_keys[4], (D, HK), D ** -0.5, 0.125, ((0, 32),))
    w_key = bell_draw(arg_keys[5], (D, HK), D ** -0.5, 0.125, ((0, 32),))
    w_value = bell_draw(arg_keys[6], (D, HV), D ** -0.5, 0.125, ((0, 32),))
    w_gate = bell_draw(arg_keys[7], (D, HV), D ** -0.5, 0.125, ((0, 32),))
    w_beta = bell_draw(arg_keys[8], (D, HEADS), D ** -0.5, 0.125, ((0, 32),))
    w_alpha = bell_draw(arg_keys[9], (D, HEADS), D ** -0.5, 0.125, ((0, 32),))
    conv_q = bell_draw(arg_keys[10], (CONV, HK), CONV ** -0.5, 3.0, ((1, 32),))
    conv_k = bell_draw(arg_keys[11], (CONV, HK), CONV ** -0.5, 3.0, ((1, 32),))
    conv_v = bell_draw(arg_keys[12], (CONV, HV), CONV ** -0.5, 3.0, ((1, 32),))
    a_log = jnp.clip(jax.random.uniform(arg_keys[13], (HEADS,), jnp.float32, 0.0, 2.77), 0.0, 2.77)
    dt_bias = jnp.clip(jax.random.uniform(arg_keys[14], (HEADS,), jnp.float32, -6.0, -2.0), -6.0, -2.0)
    norm_gain = jnp.clip(1.0 + 0.1 * jax.random.normal(arg_keys[15], (DV,), jnp.float32), 0.5, 1.5).astype(jnp.bfloat16)
    w_out = bell_draw(arg_keys[16], (HV, D), (HV // 4) ** -0.5, 0.1875, ((1, 32),))
    gain_two = jnp.clip(1.0 + 0.1 * jax.random.normal(arg_keys[17], (D,), jnp.float32), 0.5, 1.5).astype(jnp.bfloat16)
    w_ffgate = bell_draw(arg_keys[18], (D, FF), D ** -0.5, 0.125, ((0, 32),))
    w_ffup = bell_draw(arg_keys[19], (D, FF), D ** -0.5, 0.125, ((0, 32),))
    w_down = bell_draw(arg_keys[20], (FF, D), (FF // 4) ** -0.5, 0.15625, ((1, 32),))
    return dict(tokens=tokens, segments=segments, cotangent=cotangent, gain_one=gain_one, w_query=w_query, w_key=w_key, w_value=w_value, w_gate=w_gate, w_beta=w_beta, w_alpha=w_alpha, conv_q=conv_q, conv_k=conv_k, conv_v=conv_v, a_log=a_log, dt_bias=dt_bias, norm_gain=norm_gain, w_out=w_out, gain_two=gain_two, w_ffgate=w_ffgate, w_ffup=w_ffup, w_down=w_down)


@jax.custom_vjp
def low(v):
    return lax.optimization_barrier(v.astype(jnp.bfloat16)).astype(jnp.float32)

@jax.custom_vjp
def low_back(v):
    return v

def low_keep(v):
    return (low(v), None)

def low_pass(kept, grad):
    return (grad,)

def back_keep(v):
    return (v, None)

def back_low(kept, grad):
    return (low(grad),)
low.defvjp(low_keep, low_pass)
low_back.defvjp(back_keep, back_low)

def precise_dot(left, right):
    return jnp.dot(left, right, precision=lax.Precision.HIGHEST, preferred_element_type=jnp.float32)

def rms_norm(values, gain):
    return values * lax.rsqrt(lax.optimization_barrier(jnp.mean(values * values, axis=-1, keepdims=True)) + 1e-06) * gain

def short_conv(signal, conv_taps, doc_ids):
    width = conv_taps.shape[0]
    summed = signal * conv_taps[width - 1]
    for offset in range(1, width):
        shifted = jnp.pad(signal, ((0, 0), (offset, 0), (0, 0)))[:, :-offset]
        shifted_ids = jnp.pad(doc_ids, ((0, 0), (offset, 0)), constant_values=-1)[:, :-offset]
        same_doc = (shifted_ids == doc_ids).astype(signal.dtype)[..., None]
        summed = summed + shifted * same_doc * conv_taps[width - 1 - offset]
    return jax.nn.silu(summed)

def span_step(state_mat, block_in):
    query_part, key_part, value_part, beta_part, decay_part, start_part = block_in
    block_len = query_part.shape[2]
    highest = lax.Precision.HIGHEST
    log_decay = jnp.cumsum(decay_part, axis=-1)
    doc_count = jnp.cumsum(start_part, axis=-1)
    same_doc = doc_count[:, :, None] == doc_count[:, None, :]
    positions = jnp.arange(block_len)
    lower_incl = positions[:, None] >= positions[None, :]
    lower_strict = (positions[:, None] > positions[None, :]).astype(decay_part.dtype)
    linked = (same_doc & lower_incl)[:, None].astype(decay_part.dtype)
    log_gap = log_decay[..., :, None] - log_decay[..., None, :]
    decay_mat = jnp.exp(log_gap * linked) * linked
    carry_in = jnp.exp(log_decay) * (doc_count == 0)[:, None, :].astype(decay_part.dtype)
    key_gram = jnp.einsum('bhid,bhjd->bhij', key_part, key_part, precision=highest)
    nilpotent = -beta_part[..., :, None] * (decay_mat * key_gram * lower_strict)
    inverse = jnp.eye(block_len, dtype=decay_part.dtype) + nilpotent
    power_mat = nilpotent
    for section_num in range(block_len.bit_length() - 2):
        power_mat = jnp.matmul(power_mat, power_mat, precision=highest)
        inverse = inverse + jnp.matmul(inverse, power_mat, precision=highest)
    recalled = jnp.einsum('bhid,bhed->bhie', key_part, state_mat, precision=highest)
    target = beta_part[..., None] * (value_part - carry_in[..., None] * recalled)
    update = jnp.matmul(inverse, target, precision=highest)
    scores = jnp.einsum('bhid,bhjd->bhij', query_part, key_part, precision=highest) * decay_mat
    output = carry_in[..., None] * jnp.einsum('bhid,bhed->bhie', query_part, state_mat, precision=highest)
    output = output + jnp.matmul(scores, update, precision=highest)
    weighted = decay_mat[..., -1, :][..., None] * update
    new_state = carry_in[..., -1][..., None, None] * state_mat
    new_state = new_state + jnp.einsum('bhje,bhjd->bhed', weighted, key_part, precision=highest)
    return (new_state, output)

def mixer(projected, conv_q, conv_k, conv_v, a_log, dt_bias, norm_gain, doc_ids, head_count, block_size):
    batch_n = projected.shape[0]
    length = projected.shape[1]
    key_width = conv_q.shape[1]
    value_width = conv_v.shape[1]
    key_head = key_width // head_count
    value_head = value_width // head_count
    base = 2 * key_width + 2 * value_width
    queries = short_conv(projected[..., :key_width], conv_q, doc_ids).reshape(batch_n, length, head_count, key_head)
    key_vecs = short_conv(projected[..., key_width:2 * key_width], conv_k, doc_ids).reshape(batch_n, length, head_count, key_head)
    values = short_conv(projected[..., 2 * key_width:2 * key_width + value_width], conv_v, doc_ids).reshape(batch_n, length, head_count, value_head)
    out_gate = projected[..., 2 * key_width + value_width:base].reshape(batch_n, length, head_count, value_head)
    beta_rate = jax.nn.sigmoid(projected[..., base:base + head_count])
    decay = -jnp.exp(a_log) * jax.nn.softplus(projected[..., base + head_count:] + dt_bias)
    queries = queries * lax.rsqrt(lax.optimization_barrier(jnp.sum(queries * queries, axis=-1, keepdims=True)) + 1e-06) * key_head ** (-0.5)
    key_vecs = key_vecs * lax.rsqrt(lax.optimization_barrier(jnp.sum(key_vecs * key_vecs, axis=-1, keepdims=True)) + 1e-06)
    previous = jnp.pad(doc_ids, ((0, 0), (1, 0)), constant_values=-1)[:, :-1]
    doc_start = (doc_ids != previous).astype(decay.dtype)
    num_blocks = length // block_size

    def split_heads(array):
        return array.reshape(batch_n, num_blocks, block_size, head_count, array.shape[-1]).transpose(1, 0, 3, 2, 4)

    def split_rates(array):
        return array.reshape(batch_n, num_blocks, block_size, head_count).transpose(1, 0, 3, 2)
    starts = doc_start.reshape(batch_n, num_blocks, block_size).transpose(1, 0, 2)
    state_mat = jnp.zeros((batch_n, head_count, value_head, key_head), decay.dtype)
    final, outputs = lax.scan(jax.checkpoint(span_step), state_mat, (split_heads(queries), split_heads(key_vecs), split_heads(values), split_rates(beta_rate), split_rates(decay), starts))
    recur = outputs.transpose(1, 0, 3, 2, 4).reshape(batch_n, length, head_count, value_head)
    recur = recur * lax.rsqrt(lax.optimization_barrier(jnp.mean(recur * recur, axis=-1, keepdims=True)) + 1e-05) * norm_gain * jax.nn.silu(out_gate)
    return recur.reshape(batch_n, length, value_width)

def layer(inputs, doc_ids, gain_one, w_query, w_key, w_value, w_gate, w_beta, w_alpha, conv_q, conv_k, conv_v, a_log, dt_bias, norm_gain, w_out, gain_two, w_ffgate, w_ffup, w_down):
    seq_count = inputs.shape[0] // SEQ
    normed_one = low(rms_norm(inputs, gain_one))
    joined = jnp.concatenate((w_query, w_key, w_value, w_gate, w_beta, w_alpha), axis=1)
    projected = low_back(precise_dot(normed_one, joined))
    mixed = mixer(projected.reshape(seq_count, SEQ, -1), conv_q, conv_k, conv_v, a_log, dt_bias, norm_gain, doc_ids.reshape(seq_count, SEQ), HEADS, SPAN)
    mixed = low(mixed.reshape(inputs.shape[0], -1))
    middle = inputs + low_back(precise_dot(mixed, w_out))
    normed_two = low(rms_norm(middle, gain_two))
    gate_up = low_back(precise_dot(normed_two, jnp.concatenate((w_ffgate, w_ffup), axis=1)))
    hidden = low(jax.nn.silu(gate_up[:, :FF]) * gate_up[:, FF:])
    return middle + low_back(precise_dot(hidden, w_down))

def reference(tokens, segments, cotangent, gain_one, w_query, w_key, w_value, w_gate, w_beta, w_alpha, conv_q, conv_k, conv_v, a_log, dt_bias, norm_gain, w_out, gain_two, w_ffgate, w_ffup, w_down):
    float_params = tuple((parameter.astype(jnp.float32) for parameter in (gain_one, w_query, w_key, w_value, w_gate, w_beta, w_alpha, conv_q, conv_k, conv_v, a_log, dt_bias, norm_gain, w_out, gain_two, w_ffgate, w_ffup, w_down)))
    group_rows = TOK_DEV
    group_count = TOKENS // group_rows

    def one_group(totals, group_index):
        row_start = (group_index * group_rows).astype(jnp.int32)
        inputs = lax.dynamic_slice_in_dim(tokens, row_start, group_rows, 0).astype(jnp.float32)
        doc_ids = lax.dynamic_slice_in_dim(segments, row_start, group_rows, 0)
        incoming = lax.dynamic_slice_in_dim(cotangent, row_start, group_rows, 0).astype(jnp.float32)

        def forward(inner, *weights):
            return layer(inner, doc_ids, *weights)
        result, pullback = jax.vjp(forward, inputs, *float_params)
        gradients = pullback(incoming)
        totals = tuple((total + grad for total, grad in zip(totals, gradients[1:])))
        return (totals, (result.astype(jnp.bfloat16), gradients[0]))
    initial = tuple((jnp.zeros_like(parameter) for parameter in float_params))
    totals, (outputs, input_grads) = lax.scan(one_group, initial, jnp.arange(group_count, dtype=jnp.int32))
    return (outputs.reshape(TOKENS, D), input_grads.reshape(TOKENS, D), totals[0], totals[1], totals[2], totals[3], totals[4], totals[5], totals[6], totals[7], totals[8], totals[9], totals[10], totals[11], totals[12], totals[13], totals[14], totals[15], totals[16], totals[17])
```

```python
import functools

import jax
import jax.numpy as jnp
from jax import lax
from jax.experimental import pallas as pl
from jax.experimental.pallas import tpu as pltpu
from jax.sharding import PartitionSpec as P

SEQ = 256
SPLIT = 2
PAIR = 2
ROWS = PAIR * SEQ

f32 = jnp.float32
bf16 = jnp.bfloat16
NN = (((1,), (0,)), ((), ()))
NT = (((1,), (1,)), ((), ()))
TN = (((0,), (0,)), ((), ()))


def split(a):
    hi = a.astype(bf16)
    return hi, (a - hi.astype(f32)).astype(bf16)


def one(a, b, dims):
    return lax.dot_general(a.astype(bf16), b.astype(bf16), dims, preferred_element_type=f32)


def three(a, b, dims):
    ah, al = split(a)
    bh, bl = split(b)
    out = lax.dot_general(ah, bl, dims, preferred_element_type=f32)
    out = out + lax.dot_general(al, bh, dims, preferred_element_type=f32)
    return out + lax.dot_general(ah, bh, dims, preferred_element_type=f32)


def exact_left(a, b, dims):
    bh, bl = split(b)
    a = a.astype(bf16)
    return lax.dot_general(a, bh, dims, preferred_element_type=f32) + lax.dot_general(a, bl, dims, preferred_element_type=f32)


def exact_right(a, b, dims):
    ah, al = split(a)
    b = b.astype(bf16)
    return lax.dot_general(ah, b, dims, preferred_element_type=f32) + lax.dot_general(al, b, dims, preferred_element_type=f32)


def sigmoid(v):
    return 1.0 / (1.0 + jnp.exp(-v))


def conv(c, taps, pos):
    width = taps.shape[0]
    z = c * taps[width - 1 : width]
    for s in range(1, width):
        z = z + jnp.where(pos >= s, pltpu.roll(c, s, 0), 0.0) * taps[width - 1 - s : width - s]
    return z


def unit(c):
    r = lax.rsqrt(jnp.sum(c * c, axis=-1, keepdims=True) + 1e-6)
    return c * r, r


def inverses(n_list, iota_r, iota_c):
    size = n_list[0].shape[0]
    eye = (iota_r == iota_c).astype(f32)
    xs = None
    b = 1
    while b < size:
        mask = ((iota_r // (2 * b)) == (iota_c // (2 * b))) & ((iota_r // b) % 2 == 1) & ((iota_c // b) % 2 == 0)
        cs = [jnp.where(mask, n, 0.0) for n in n_list]
        if xs is None:
            xs = [eye - c for c in cs]
        else:
            low = [x.astype(bf16) for x in xs]
            t = [one(c, x, NN) for c, x in zip(cs, low)]
            xs = [x - one(y, z, NN) for x, y, z in zip(xs, low, t)]
        b *= 2
    left = [(eye - x) - three(n, x, NN) for n, x in zip(n_list, xs)]
    return [x + one(x, r, NN) for x, r in zip(xs, left)]


def rates(pba, prm, tri):
    beta = sigmoid(pba)
    rate = pba + prm[1:2]
    decay = -prm[0:1] * (jnp.maximum(rate, 0.0) + jnp.log1p(jnp.exp(-jnp.abs(rate))))
    return beta, rate, decay, exact_left(tri, decay, NN), exact_right(decay, tri, (((0,), (1,)), ((), ())))


class Sequence:
    def __init__(self, dims, half, refs, rows, iota_r, iota_c, tri):
        pq_ref, pk_ref, pv_ref, pg_ref, ba_ref, pos_ref, taps_ref, gain_ref, prm_ref = refs
        nh, dk, dv = dims
        hs = nh // SPLIT
        wq = hs * dk
        at = half * hs
        H = range(hs)
        self.rows = rows
        self.pos = pos_ref[rows, :]
        taps = taps_ref[...]
        self.taps = (taps[:, :wq], taps[:, wq : 2 * wq], taps[:, 2 * wq :])
        self.raw = (pq_ref[rows, :], pk_ref[rows, :], pv_ref[rows, :])
        self.beta, self.rate, self.decay, gcol, grow = rates(ba_ref[rows, :], prm_ref[...], tri)
        self.z = tuple(conv(c, t, self.pos) for c, t in zip(self.raw, self.taps))
        self.sig = tuple(sigmoid(z) for z in self.z)
        qc, kc, self.v = (z * g for z, g in zip(self.z, self.sig))
        live = (iota_c <= iota_r) & (iota_c >= iota_r - self.pos.astype(jnp.int32))
        self.bs = [self.beta[:, at + h : at + h + 1] for h in H]
        self.uq = [unit(qc[:, h * dk : (h + 1) * dk]) for h in H]
        self.uk = [unit(kc[:, h * dk : (h + 1) * dk]) for h in H]
        self.qs = [a * dk ** -0.5 for a, _ in self.uq]
        self.ks = [a for a, _ in self.uk]
        lane = nh + at
        self.ls = [
            jnp.where(live, jnp.exp(jnp.where(live, gcol[:, lane + h : lane + h + 1] - grow[lane + h : lane + h + 1, :], 0.0)), 0.0)
            for h in H]


def planes(n):
    iota_r = lax.broadcasted_iota(jnp.int32, (n, n), 0)
    iota_c = lax.broadcasted_iota(jnp.int32, (n, n), 1)
    return iota_r, iota_c, (iota_c <= iota_r).astype(f32), iota_c < iota_r


def fwd_kernel(dims, half, *refs):
    shared, (out_ref, x_ref, u_ref, o_ref) = refs[:9], refs[-4:]
    pg_ref, gain_ref = refs[3], refs[7]
    nh, dk, dv = dims
    hs = nh // SPLIT
    iota_r, iota_c, tri, strict = planes(SEQ)
    gain = gain_ref[...]
    seqs = [Sequence(dims, half, shared, slice(i * SEQ, (i + 1) * SEQ), iota_r, iota_c, tri) for i in range(out_ref.shape[0] // SEQ)]
    units = [(i, h) for i in range(len(seqs)) for h in range(hs)]
    ms = [three(seqs[i].ks[h], seqs[i].ks[h], NT) for i, h in units]
    ns = [jnp.where(strict, seqs[i].bs[h] * seqs[i].ls[h] * m, 0.0) for (i, h), m in zip(units, ms)]
    xs = inverses(ns, iota_r, iota_c)
    us = [three(x, seqs[i].bs[h] * seqs[i].v[:, h * dv : (h + 1) * dv], NN) for (i, h), x in zip(units, xs)]
    ps = [seqs[i].ls[h] * three(seqs[i].qs[h], seqs[i].ks[h], NT) for i, h in units]
    os = [three(p, u, NN) for p, u in zip(ps, us)]
    for (i, h), x, u, o in zip(units, xs, us, os):
        rows, sl = seqs[i].rows, slice(h * dv, (h + 1) * dv)
        x_ref[i * hs + h] = x
        u_ref[rows, sl] = u
        o_ref[rows, sl] = o
        r = lax.rsqrt(jnp.mean(o * o, axis=-1, keepdims=True) + 1e-5)
        pg = pg_ref[rows, sl]
        out_ref[rows, sl] = (o * r * gain * (pg * sigmoid(pg))).astype(bf16)


def bwd_kernel(dims, half, has_before, *refs):
    shared, (x_ref, u_ref, o_ref, dm_ref) = refs[:9], refs[9:13]
    dp_ref, dba_ref, dtaps_ref, dgain_ref, dprm_ref = refs[-5:]
    pg_ref, gain_ref, prm_ref = refs[3], refs[7], refs[8]
    nh, dk, dv = dims
    hs = nh // SPLIT
    wq, wv = hs * dk, hs * dv
    at = half * hs
    iota_r, iota_c, tri, strict = planes(SEQ)
    gain = gain_ref[...]
    prm = prm_ref[...]
    seqs = [Sequence(dims, half, shared, slice(i * SEQ, (i + 1) * SEQ), iota_r, iota_c, tri) for i in range(dm_ref.shape[0] // SEQ)]
    units = [(i, h) for i in range(len(seqs)) for h in range(hs)]
    dgain = jnp.zeros_like(gain)
    dos, us = [], []
    for i, h in units:
        rows, sl = seqs[i].rows, slice(h * dv, (h + 1) * dv)
        o = o_ref[rows, sl]
        pg = pg_ref[rows, sl]
        dm = dm_ref[rows, sl]
        r = lax.rsqrt(jnp.mean(o * o, axis=-1, keepdims=True) + 1e-5)
        nrm = o * r
        sg = sigmoid(pg)
        dp_ref[rows, 2 * wq + wv + h * dv : 2 * wq + wv + (h + 1) * dv] = (dm * nrm * gain * (sg * (1.0 + pg * (1.0 - sg)))).astype(bf16)
        dy = dm * (pg * sg)
        dgain = dgain + jnp.sum(dy * nrm, axis=0, keepdims=True)
        dn = dy * gain
        dos.append(r * (dn - nrm * jnp.mean(nrm * dn, axis=-1, keepdims=True)))
        us.append(u_ref[rows, sl])
    bm = [jnp.where(strict, seqs[i].ls[h] * three(seqs[i].ks[h], seqs[i].ks[h], NT), 0.0) for i, h in units]
    ps = [seqs[i].ls[h] * three(seqs[i].qs[h], seqs[i].ks[h], NT) for i, h in units]
    dps = [three(do, u, NT) for do, u in zip(dos, us)]
    dus = [three(p, do, TN) for p, do in zip(ps, dos)]
    dws = [three(x_ref[i * hs + h], du, TN) for (i, h), du in zip(units, dus)]
    das = [-three(dw, u, NT) for dw, u in zip(dws, us)]

    @pl.when(pl.program_id(0) == 0)
    def _():
        dtaps_ref[...] = jnp.zeros_like(dtaps_ref)
        dgain_ref[...] = jnp.zeros_like(dgain_ref)
        dprm_ref[...] = jnp.zeros_like(dprm_ref)

    dgain_ref[...] += dgain
    lane = lax.broadcasted_iota(jnp.int32, (SEQ, 128), 1)
    ones = jnp.ones((SEQ, 128), f32)
    sc = dk ** -0.5
    for i, q in enumerate(seqs):
        rows, pos = q.rows, q.pos
        dbeta = jnp.zeros((SEQ, 128), f32)
        dlog = jnp.zeros((SEQ, 128), f32)
        dz = ([], [], [])
        for h in range(hs):
            n = i * hs + h
            vh = q.v[:, h * dv : (h + 1) * dv]
            ab = das[n] * bm[n]
            dbeta = jnp.where(lane == at + h, jnp.sum(dws[n] * vh, axis=-1, keepdims=True) + jnp.sum(ab, axis=-1, keepdims=True), dbeta)
            e = q.bs[h] * ab + dps[n] * ps[n]
            dlog = jnp.where(lane == nh + at + h, jnp.sum(e, axis=-1, keepdims=True) - exact_right(e, ones, TN), dlog)
            ds = dps[n] * q.ls[h]
            dmm = jnp.where(strict, q.bs[h] * das[n] * q.ls[h], 0.0)
            dq = sc * three(ds, q.ks[h], NN)
            dkh = three(ds, q.qs[h], TN) + three(dmm, q.ks[h], NN) + three(dmm, q.ks[h], TN)
            qh, rq = q.uq[h]
            kh, rk = q.uk[h]
            dz[0].append(rq * (dq - qh * jnp.sum(qh * dq, axis=-1, keepdims=True)))
            dz[1].append(rk * (dkh - kh * jnp.sum(kh * dkh, axis=-1, keepdims=True)))
            dz[2].append(q.bs[h] * dws[n])
        ddecay = exact_left(tri, dlog, TN)
        drate = -prm[0:1] * ddecay * sigmoid(q.rate)
        dba = dbeta * q.beta * (1.0 - q.beta) + drate
        if has_before:
            dba = dba + refs[13][rows, :]
            dp_ref[rows, 2 * wq + 2 * wv :] = dba.astype(bf16)
        dba_ref[rows, :] = dba
        dprm_ref[0:1, :] += jnp.sum(ddecay * q.decay, axis=0, keepdims=True)
        dprm_ref[1:2, :] += jnp.sum(drate, axis=0, keepdims=True)
        to = 0
        for parts, z, sg, c, tap in zip(dz, q.z, q.sig, q.raw, q.taps):
            d = jnp.concatenate(parts, axis=1) * (sg * (1.0 + z * (1.0 - sg)))
            width = tap.shape[0]
            w = c.shape[1]
            dc = d * tap[width - 1 : width]
            dtaps_ref[width - 1 : width, to : to + w] += jnp.sum(d * c, axis=0, keepdims=True)
            for s in range(1, width):
                m = jnp.where(pos >= s, d, 0.0)
                dc = dc + pltpu.roll(m, SEQ - s, 0) * tap[width - 1 - s : width - s]
                dtaps_ref[width - 1 - s : width - s, to : to + w] += jnp.sum(m * pltpu.roll(c, s, 0), axis=0, keepdims=True)
            dp_ref[rows, to : to + w] = dc.astype(bf16)
            to += w


def shared_specs(dims):
    nh, dk, dv = dims
    wq, wv = nh // SPLIT * dk, nh // SPLIT * dv
    at = (2 * wq) // wv
    small = (2 * wq + 2 * wv) // 128
    return [
        pl.BlockSpec((ROWS, wq), lambda i: (i, 0)),
        pl.BlockSpec((ROWS, wq), lambda i: (i, 1)),
        pl.BlockSpec((ROWS, wv), lambda i: (i, at)),
        pl.BlockSpec((ROWS, wv), lambda i: (i, at + 1)),
        pl.BlockSpec((ROWS, 128), lambda i: (i, small)),
        pl.BlockSpec((ROWS, 1), lambda i: (i, 0)),
        pl.BlockSpec((4, 2 * wq + wv), lambda i: (0, 0)),
        pl.BlockSpec((1, dv), lambda i: (0, 0)),
        pl.BlockSpec((8, 128), lambda i: (0, 0)),
    ]


def cost(us):
    return pl.CostEstimate(flops=int(us * 1.1e9), bytes_accessed=int(us * 1e6), transcendentals=0)


def mixer_fwd(proj, first, pos, taps, gain, prm, dims, half, mixed=None):
    tok = pos.shape[0]
    nh, dk, dv = dims
    hs = nh // SPLIT
    ns = tok // SEQ
    wv = hs * dv
    row = pl.BlockSpec((ROWS, wv), lambda i: (i, 0))
    specs = shared_specs(dims)
    args = [proj, proj, proj, proj, first, pos, taps, gain, prm]
    alias = {}
    if mixed is not None:
        alias = {len(args): 0}
        args.append(mixed)
        specs.append(pl.BlockSpec(memory_space=pl.ANY))
    return pl.pallas_call(
        functools.partial(fwd_kernel, dims, half),
        grid=(ns // PAIR,),
        in_specs=specs,
        out_specs=[
            pl.BlockSpec((ROWS, wv), lambda i: (i, half)),
            pl.BlockSpec((PAIR * hs, SEQ, SEQ), lambda i: (i, 0, 0)),
            row,
            row,
        ],
        out_shape=[
            jax.ShapeDtypeStruct((tok, nh * dv), bf16),
            jax.ShapeDtypeStruct((ns * hs, SEQ, SEQ), f32),
            jax.ShapeDtypeStruct((tok, wv), f32),
            jax.ShapeDtypeStruct((tok, wv), f32),
        ],
        input_output_aliases=alias,
        cost_estimate=cost(45),
        compiler_params=pltpu.CompilerParams(vmem_limit_bytes=48 << 20),
    )(*args)


def mixer_bwd(proj, first, pos, taps, gain, prm, x, u, o, dm, dims, half, before=None):
    tok = pos.shape[0]
    nh, dk, dv = dims
    hs = nh // SPLIT
    ns = tok // SEQ
    wq, wv = hs * dk, hs * dv
    row = pl.BlockSpec((ROWS, wv), lambda i: (i, 0))
    lanes = pl.BlockSpec((ROWS, 128), lambda i: (i, 0))
    specs = shared_specs(dims) + [
        pl.BlockSpec((PAIR * hs, SEQ, SEQ), lambda i: (i, 0, 0)), row, row, pl.BlockSpec((ROWS, wv), lambda i: (i, half))]
    args = [proj, proj, proj, proj, first, pos, taps, gain, prm, x, u, o, dm]
    width = 2 * wq + 2 * wv
    if before is not None:
        args.append(before)
        specs.append(lanes)
        width += 128
    return pl.pallas_call(
        functools.partial(bwd_kernel, dims, half, before is not None),
        grid=(ns // PAIR,),
        in_specs=specs,
        out_specs=[
            pl.BlockSpec((ROWS, width), lambda i: (i, 0)),
            lanes,
            pl.BlockSpec((4, 2 * wq + wv), lambda i: (0, 0)),
            pl.BlockSpec((1, dv), lambda i: (0, 0)),
            pl.BlockSpec((8, 128), lambda i: (0, 0)),
        ],
        out_shape=[
            jax.ShapeDtypeStruct((tok, width), bf16),
            jax.ShapeDtypeStruct((tok, 128), f32),
            jax.ShapeDtypeStruct((4, 2 * wq + wv), f32),
            jax.ShapeDtypeStruct((1, dv), f32),
            jax.ShapeDtypeStruct((8, 128), f32),
        ],
        cost_estimate=cost(50),
        compiler_params=pltpu.CompilerParams(vmem_limit_bytes=56 << 20),
    )(*args)


def xor_send(value, axis, size, step):
    return lax.ppermute(value, axis, [(i, i ^ step) for i in range(size)])


def after(value, *needs):
    return lax.optimization_barrier((value, *needs))[0]


def lines(size):
    return [[low + 2 * i for i in range(size // 2)] for low in range(2)]


def gather_line(rows, size):
    return lax.all_gather(rows, "fsdp", axis=0, tiled=True, axis_index_groups=lines(size))


def gather_side(near, size):
    return jnp.concatenate([near, xor_send(near, "fsdp", size, 1)], axis=0)


def dot(left, right, dims=NN, out=f32):
    return lax.dot_general(left, right, dims, preferred_element_type=f32).astype(out)


class Summed:
    def __init__(self, left, right, size):
        self.size = size
        self.half = left.shape[1] // 2
        self.left, self.right = left, right
        self.sent = dot(left[:, self.half :], right, TN, bf16)
        self.got = xor_send(self.sent, "fsdp", size, 1)

    def side(self, *needs):
        keep = dot(self.left[:, : self.half], after(self.right, *needs) if needs else self.right, TN)
        self.low = (keep + self.got.astype(f32)).astype(bf16)
        self.sum = lax.psum_scatter(self.low, "fsdp", scatter_dimension=0, tiled=True, axis_index_groups=lines(self.size))

    def total(self, ranks):
        return lax.all_to_all(self.sum.reshape(ranks, -1, self.sum.shape[1]), "rep", 0, 0)


def join_tokens(rows, size):
    far = {0: rows}
    step = size // 2
    while step:
        for j in list(far):
            far[j ^ step] = xor_send(far[j], "rep", size, step)
        step //= 2
    return jnp.concatenate([far[j] for j in range(size)], axis=0)


def sum_tokens(product, size):
    half = size // 2
    held = {}
    for lo in range(size - half, -1, -half):
        part = product(lo, lo + half)
        for j, block in enumerate(jnp.split(part, half, axis=0)):
            held[lo + j] = block
        step = 1
        while step < half:
            for j in range(lo, lo + half, 2 * step):
                got = xor_send(held[j + step].astype(bf16), "rep", size, step)
                held[j] = held[j] + got.astype(f32)
            step *= 2
        if lo:
            held[lo] = xor_send(held[lo].astype(bf16), "rep", size, lo)
    return held[0] + held[half].astype(f32)


def rms(values):
    return lax.rsqrt(jnp.mean(values * values, axis=-1, keepdims=True) + 1e-06)


def norm_back(n, r, gain, dout):
    scaled = dout * gain
    return r * (scaled - n * jnp.mean(n * scaled, axis=-1, keepdims=True)), jnp.sum(dout * n, axis=0)


def make(F, R):
    both = ("fsdp", "rep")

    def on_device(tokens, segments, cotangent, gain_one, w_query, w_key, w_value, w_gate, w_beta, w_alpha, conv_q, conv_k,
                  conv_v, a_log, dt_bias, norm_gain, w_out, gain_two, w_ffgate, w_ffup, w_down):
        f = lax.axis_index("fsdp")
        r = lax.axis_index("rep")
        N = F * R
        rows_own, D = tokens.shape
        heads = a_log.shape[0]
        dk = w_query.shape[1] // heads
        dv = w_value.shape[1] // heads
        nh = heads // R
        dims = (nh, dk, dv)
        wq, wv = nh * dk, nh * dv
        hq, hv = wq // SPLIT, wv // SPLIT
        shard = D // N
        block = D // F
        ffq = w_ffgate.shape[1] // R
        tok = rows_own * R
        ns = tok // SEQ
        tiny = dv // N
        per = conv_v.shape[1] // shard

        low_bit = f & 1

        def swap(array, axis):
            half = array.shape[axis] // 2
            return jnp.concatenate(
                [lax.dynamic_slice_in_dim(array, (low_bit ^ j) * half, half, axis=axis) for j in range(2)], axis=axis)

        def mix(array, axis):
            at = [slice(None)] * array.ndim
            parts = []
            for bit in range(2):
                for i in range(F // 2):
                    at[axis] = slice((2 * i + bit) * block, (2 * i + bit + 1) * block)
                    parts.append(array[tuple(at)])
            return swap(jnp.concatenate(parts, axis=axis), axis)

        def unmix(array, axis):
            array = swap(array, axis)
            at = [slice(None)] * array.ndim
            parts = []
            for i in range(F // 2):
                for bit in range(2):
                    p = bit * (F // 2) + i
                    at[axis] = slice(p * block, (p + 1) * block)
                    parts.append(array[tuple(at)])
            return jnp.concatenate(parts, axis=axis)

        def quarter(arrays):
            return jnp.concatenate([a.reshape(shard, R, -1) for a in arrays], axis=2)

        def spread(packed):
            return lax.all_to_all(packed.transpose(1, 0, 2), "rep", 0, 0).reshape(R * shard, -1)

        extra = jnp.concatenate(
            [gain_one[:, None], gain_two[:, None], conv_q.T, conv_k.T,
             conv_v.reshape(4, shard, per).transpose(1, 0, 2).reshape(shard, 4 * per),
             jnp.pad(norm_gain, (0, shard - tiny))[:, None]], axis=1)
        n_extra = extra.shape[1]
        extra = jnp.broadcast_to(extra[:, None], (shard, R, n_extra))
        small = jnp.concatenate([w_beta.reshape(shard, R, nh), w_alpha.reshape(shard, R, nh), extra], axis=2)
        small = jnp.pad(small, ((0, 0), (0, 0), (0, 128 - small.shape[2])))

        def halves(array, width):
            parts = array.reshape(shard, R, SPLIT, width)
            return [parts[:, :, h] for h in range(SPLIT)]

        q_h, k_h, v_h, g_h = halves(w_query, hq), halves(w_key, hq), halves(w_value, hv), halves(w_gate, hv)
        own = mix(tokens, 1)
        part_a = spread(jnp.concatenate([q_h[0], k_h[0], v_h[0], g_h[0], small, q_h[1], k_h[1], v_h[1], g_h[1]], axis=2))
        w1 = 2 * hq + 2 * hv
        part_1, part_2 = part_a[:, : w1 + 128], part_a[:, w1 + 128 :]
        line_1 = gather_line(part_1, F)
        every = join_tokens(own, R)
        ids_all = join_tokens(segments[:, None], R).reshape(ns, SEQ)
        part_r = spread(quarter([after(w_out.T, part_a), w_ffgate, w_ffup, w_down.T]))
        part_b, part_g, part_u, part_d = (
            part_r[:, :wv], part_r[:, wv : wv + ffq], part_r[:, wv + ffq : wv + 2 * ffq], part_r[:, wv + 2 * ffq :])
        line_2 = gather_line(after(part_2, line_1), F)
        wa1 = gather_side(line_1, F)
        cot = mix(cotangent, 1)
        cot_all = join_tokens(after(cot, every), R)
        line_b = gather_line(after(part_b, line_2), F)
        line_g = gather_line(after(part_g, line_b), F)
        line_u = gather_line(after(part_u, line_g), F)
        line_d = gather_line(after(part_d, line_u), F)

        extra_all = wa1[:, w1 + 2 * nh : w1 + 2 * nh + n_extra]
        gain_first, gain_second = extra_all[:, 0].astype(f32)[None], extra_all[:, 1].astype(f32)[None]
        rest = unmix(extra_all[:, 2:], 0)
        cq = lax.dynamic_slice_in_dim(rest[:, 0:4], r * wq, wq, axis=0).astype(f32).T
        ck = lax.dynamic_slice_in_dim(rest[:, 4:8], r * wq, wq, axis=0).astype(f32).T
        cv = rest[:, 8 : 8 + 4 * per].reshape(D, 4, per).transpose(1, 0, 2).reshape(4, D * per)
        cv = lax.dynamic_slice_in_dim(cv, r * wv, wv, axis=1).astype(f32)
        gain_out = rest[:, 8 + 4 * per].reshape(N, shard)[:, :tiny].reshape(1, dv).astype(f32)
        taps = [jnp.concatenate([cq[:, h * hq : (h + 1) * hq], ck[:, h * hq : (h + 1) * hq], cv[:, h * hv : (h + 1) * hv]], axis=1)
                for h in range(SPLIT)]
        prm = jnp.stack([jnp.exp(lax.dynamic_slice_in_dim(a_log, r * nh, nh)), lax.dynamic_slice_in_dim(dt_bias, r * nh, nh)])
        prm = jnp.pad(prm, ((0, 6), (nh, 128 - 2 * nh)))
        place = jnp.arange(SEQ)
        same = (ids_all[:, :, None] == ids_all[:, None, :]) & (place[:, None] >= place[None, :])[None]
        pos = (jnp.sum(same.astype(f32), axis=2) - 1.0).reshape(tok, 1)

        every32 = every.astype(f32)
        normed_one = (every32 * rms(every32) * gain_first).astype(bf16)
        normed_one = after(normed_one, line_2)
        proj_1 = dot(normed_one, wa1)
        mixed, x_1, u_1, o_1 = mixer_fwd(proj_1, proj_1, pos, taps[0], gain_out, prm, dims, 0)
        wa2 = gather_side(line_2, F)
        proj_2 = dot(after(normed_one, mixed, line_b), wa2)
        mixed, x_2, u_2, o_2 = mixer_fwd(proj_2, proj_1, pos, taps[1], gain_out, prm, dims, 1, mixed)
        wb = gather_side(line_b, F)
        mixed = after(mixed, line_g)
        wg = gather_side(line_g, F)
        own32 = own.astype(f32)
        middle = own32 + sum_tokens(lambda lo, hi: dot(mixed[lo * rows_own : hi * rows_own], wb, NT), R)
        r2 = rms(middle)
        n2 = middle * r2
        normed_own = (n2 * gain_second).astype(bf16)
        normed_two = join_tokens(after(normed_own, line_u), R)
        wu = gather_side(line_u, F)
        gate_pre = dot(normed_two, wg)
        up_pre = dot(after(normed_two, gate_pre), wu)
        wd = gather_side(line_d, F)
        gate_sig = jax.nn.sigmoid(gate_pre)
        gate_act = gate_pre * gate_sig
        hidden = (gate_act * up_pre).astype(bf16)

        cot_wd = after(cot_all, hidden)
        g_down = Summed(cot_wd, hidden, F)
        dhidden = dot(after(cot_all, g_down.sent), wd)
        dgate = (dhidden * up_pre * (gate_sig * (1.0 + gate_pre * (1.0 - gate_sig)))).astype(bf16)
        dup = (dhidden * gate_act).astype(bf16)
        dnormed_two = sum_tokens(
            lambda lo, hi: dot(dgate[lo * rows_own : hi * rows_own], wg, NT) + dot(dup[lo * rows_own : hi * rows_own], wu, NT), R)
        g_gate = Summed(normed_two, dgate, F)
        g_down.side(g_gate.sent)
        g_up = Summed(normed_two, after(dup, g_gate.sent), F)
        dinner, dgain_second = norm_back(n2, r2, gain_second, dnormed_two)
        dmiddle = cot.astype(f32) + dinner
        dmiddle_low = join_tokens(dmiddle.astype(bf16), R)
        g_gate.side(g_up.sent)
        dmixed = dot(dmiddle_low, wb)
        before = None
        dprm, dgain_out, dtaps = 0.0, 0.0, {}
        dproj = {}
        dp_2, dba, dtaps[1], dg, dpar = mixer_bwd(proj_2, proj_1, pos, taps[1], gain_out, prm, x_2, u_2, o_2, dmixed, dims, 1)
        g_out = Summed(dmiddle_low, mixed, F)
        g_up.side(g_out.sent)
        g_2 = Summed(normed_one, dp_2, F)
        dp_1, dba, dtaps[0], dg1, dpar1 = mixer_bwd(
            proj_1, proj_1, pos, taps[0], gain_out, prm, x_1, u_1, o_1, after(dmixed, g_2.sent), dims, 0, dba)
        g_out.side()
        g_1 = Summed(normed_one, dp_1, F)
        g_2.side(g_1.sent)
        dnormed_one = sum_tokens(
            lambda lo, hi: dot(dp_1[lo * rows_own : hi * rows_own], wa1, NT) + dot(dp_2[lo * rows_own : hi * rows_own], wa2, NT), R)
        g_1.side()
        dprm = dpar + dpar1
        dgain_out = dg + dg1
        hidden_late = after(hidden, g_1.sent)
        layer_out = (middle + sum_tokens(lambda lo, hi: dot(hidden_late[lo * rows_own : hi * rows_own], wd, NT), R)).astype(bf16)

        n1 = own32 * rms(own32)
        dfirst, dgain_first = norm_back(n1, rms(own32), gain_first, dnormed_one)
        grad_tokens = unmix(dmiddle + dfirst, 1)

        def wide(parts):
            return parts.astype(f32).transpose(1, 0, 2).reshape(shard, -1)

        def tall(parts):
            return parts.astype(f32).transpose(0, 2, 1).reshape(-1, shard)

        t_1, t_2 = g_1.total(R), g_2.total(R)

        def joined(lo, width):
            return jnp.stack([t[:, :, lo : lo + width] for t in (t_1, t_2)], axis=2).astype(f32).transpose(1, 0, 2, 3).reshape(shard, -1)

        grad_query, grad_key = joined(0, hq), joined(hq, hq)
        grad_value, grad_gate_w = joined(2 * hq, hv), joined(2 * hq + hv, hv)
        grad_beta, grad_alpha = wide(t_1[:, :, w1 : w1 + nh]), wide(t_1[:, :, w1 + nh : w1 + 2 * nh])
        grad_down, grad_out = tall(g_down.total(R)), tall(g_out.total(R))
        grad_gate, grad_up = wide(g_gate.total(R)), wide(g_up.total(R))

        def placed(parts, total, width):
            part = jnp.concatenate(parts, axis=1)
            return lax.dynamic_update_slice(jnp.zeros((4, total), f32), part, (0, r * width))

        gq = placed([dtaps[h][:, :hq] for h in range(SPLIT)], R * wq, wq)
        gk = placed([dtaps[h][:, hq : 2 * hq] for h in range(SPLIT)], R * wq, wq)
        gv = placed([dtaps[h][:, 2 * hq :] for h in range(SPLIT)], R * wv, wv)
        heads_part = lax.dynamic_update_slice(jnp.zeros((2, heads), f32), dprm[:2, nh : 2 * nh], (0, r * nh)).reshape(1, -1)
        packed = jnp.concatenate([
            unmix(dgain_first[None], 1).reshape(N, -1),
            unmix(dgain_second[None], 1).reshape(N, -1),
            gq.reshape(4, N, -1).transpose(1, 0, 2).reshape(N, -1),
            gk.reshape(4, N, -1).transpose(1, 0, 2).reshape(N, -1),
            gv.reshape(4, N, -1).transpose(1, 0, 2).reshape(N, -1),
            dgain_out.reshape(N, tiny),
            jnp.broadcast_to(heads_part, (N, 2 * heads))], axis=1)
        summed = jnp.sum(lax.all_to_all(packed, both, 0, 0, tiled=True), axis=0)
        sizes = [shard, shard, 4 * shard, 4 * shard, 4 * shard * per, tiny, heads, heads]
        ends = [0]
        for size in sizes:
            ends.append(ends[-1] + size)
        pick = [summed[ends[i] : ends[i + 1]] for i in range(len(sizes))]
        return (
            unmix(layer_out, 1), grad_tokens, pick[0], grad_query, grad_key, grad_value, grad_gate_w, grad_beta, grad_alpha,
            pick[2].reshape(4, shard), pick[3].reshape(4, shard), pick[4].reshape(4, shard * per), pick[6], pick[7], pick[5],
            grad_out, pick[1], grad_gate, grad_up, grad_down)

    return on_device


def solution(mesh):
    rows, cols, flat = P(("fsdp", "rep"), None), P(None, ("fsdp", "rep")), P(("fsdp", "rep"))
    placed = (rows, flat, rows, flat, rows, rows, rows, rows, rows, rows, cols, cols, cols, P(), P(), flat, cols, flat, rows, rows, cols)
    made = (rows, rows, flat, rows, rows, rows, rows, rows, rows, cols, cols, cols, P(), P(), flat, cols, flat, rows, rows, cols)
    return jax.shard_map(
        make(mesh.shape["fsdp"], mesh.shape["rep"]), mesh=mesh, in_specs=placed, out_specs=made, check_vma=False)
```

```python
import functools

import jax
import jax.numpy as jnp
from jax import lax
from jax.experimental import pallas as pl
from jax.experimental.pallas import tpu as pltpu
from jax.sharding import PartitionSpec as P

SEQ = 256
SPLIT = 2
PAIR = 2
ROWS = PAIR * SEQ

f32 = jnp.float32
bf16 = jnp.bfloat16
NN = (((1,), (0,)), ((), ()))
NT = (((1,), (1,)), ((), ()))
TN = (((0,), (0,)), ((), ()))


def split(a):
    hi = a.astype(bf16)
    return hi, (a - hi.astype(f32)).astype(bf16)


def one(a, b, dims):
    return lax.dot_general(a.astype(bf16), b.astype(bf16), dims, preferred_element_type=f32)


def three(a, b, dims):
    ah, al = split(a)
    bh, bl = split(b)
    out = lax.dot_general(ah, bl, dims, preferred_element_type=f32)
    out = out + lax.dot_general(al, bh, dims, preferred_element_type=f32)
    return out + lax.dot_general(ah, bh, dims, preferred_element_type=f32)


def exact_left(a, b, dims):
    bh, bl = split(b)
    a = a.astype(bf16)
    return lax.dot_general(a, bh, dims, preferred_element_type=f32) + lax.dot_general(a, bl, dims, preferred_element_type=f32)


def exact_right(a, b, dims):
    ah, al = split(a)
    b = b.astype(bf16)
    return lax.dot_general(ah, b, dims, preferred_element_type=f32) + lax.dot_general(al, b, dims, preferred_element_type=f32)


def sigmoid(v):
    return 1.0 / (1.0 + jnp.exp(-v))


def conv(c, taps, pos):
    width = taps.shape[0]
    z = c * taps[width - 1 : width]
    for s in range(1, width):
        z = z + jnp.where(pos >= s, pltpu.roll(c, s, 0), 0.0) * taps[width - 1 - s : width - s]
    return z


def unit(c):
    r = lax.rsqrt(jnp.sum(c * c, axis=-1, keepdims=True) + 1e-6)
    return c * r, r


def inverses(n_list, iota_r, iota_c):
    size = n_list[0].shape[0]
    eye = (iota_r == iota_c).astype(f32)
    xs = None
    b = 1
    while b < size:
        mask = ((iota_r // (2 * b)) == (iota_c // (2 * b))) & ((iota_r // b) % 2 == 1) & ((iota_c // b) % 2 == 0)
        cs = [jnp.where(mask, n, 0.0) for n in n_list]
        if xs is None:
            xs = [eye - c for c in cs]
        else:
            low = [x.astype(bf16) for x in xs]
            t = [one(c, x, NN) for c, x in zip(cs, low)]
            xs = [x - one(y, z, NN) for x, y, z in zip(xs, low, t)]
        b *= 2
    left = [(eye - x) - three(n, x, NN) for n, x in zip(n_list, xs)]
    return [x + one(x, r, NN) for x, r in zip(xs, left)]


def rates(pba, prm, tri):
    beta = sigmoid(pba)
    rate = pba + prm[1:2]
    decay = -prm[0:1] * (jnp.maximum(rate, 0.0) + jnp.log1p(jnp.exp(-jnp.abs(rate))))
    return beta, rate, decay, exact_left(tri, decay, NN), exact_right(decay, tri, (((0,), (1,)), ((), ())))


class Sequence:
    def __init__(self, dims, half, refs, rows, iota_r, iota_c, tri):
        pq_ref, pk_ref, pv_ref, pg_ref, ba_ref, pos_ref, taps_ref, gain_ref, prm_ref = refs
        nh, dk, dv = dims
        hs = nh // SPLIT
        wq = hs * dk
        at = half * hs
        H = range(hs)
        self.rows = rows
        self.pos = pos_ref[rows, :]
        taps = taps_ref[...]
        self.taps = (taps[:, :wq], taps[:, wq : 2 * wq], taps[:, 2 * wq :])
        self.raw = (pq_ref[rows, :], pk_ref[rows, :], pv_ref[rows, :])
        self.beta, self.rate, self.decay, gcol, grow = rates(ba_ref[rows, :], prm_ref[...], tri)
        self.z = tuple(conv(c, t, self.pos) for c, t in zip(self.raw, self.taps))
        self.sig = tuple(sigmoid(z) for z in self.z)
        qc, kc, self.v = (z * g for z, g in zip(self.z, self.sig))
        live = (iota_c <= iota_r) & (iota_c >= iota_r - self.pos.astype(jnp.int32))
        self.bs = [self.beta[:, at + h : at + h + 1] for h in H]
        self.uq = [unit(qc[:, h * dk : (h + 1) * dk]) for h in H]
        self.uk = [unit(kc[:, h * dk : (h + 1) * dk]) for h in H]
        self.qs = [a * dk ** -0.5 for a, _ in self.uq]
        self.ks = [a for a, _ in self.uk]
        lane = nh + at
        self.ls = [
            jnp.where(live, jnp.exp(jnp.where(live, gcol[:, lane + h : lane + h + 1] - grow[lane + h : lane + h + 1, :], 0.0)), 0.0)
            for h in H]


def planes(n):
    iota_r = lax.broadcasted_iota(jnp.int32, (n, n), 0)
    iota_c = lax.broadcasted_iota(jnp.int32, (n, n), 1)
    return iota_r, iota_c, (iota_c <= iota_r).astype(f32), iota_c < iota_r


def fwd_kernel(dims, half, *refs):
    shared, (out_ref, x_ref, u_ref, o_ref) = refs[:9], refs[-4:]
    pg_ref, gain_ref = refs[3], refs[7]
    nh, dk, dv = dims
    hs = nh // SPLIT
    iota_r, iota_c, tri, strict = planes(SEQ)
    gain = gain_ref[...]
    seqs = [Sequence(dims, half, shared, slice(i * SEQ, (i + 1) * SEQ), iota_r, iota_c, tri) for i in range(out_ref.shape[0] // SEQ)]
    units = [(i, h) for i in range(len(seqs)) for h in range(hs)]
    ms = [three(seqs[i].ks[h], seqs[i].ks[h], NT) for i, h in units]
    ns = [jnp.where(strict, seqs[i].bs[h] * seqs[i].ls[h] * m, 0.0) for (i, h), m in zip(units, ms)]
    xs = inverses(ns, iota_r, iota_c)
    us = [three(x, seqs[i].bs[h] * seqs[i].v[:, h * dv : (h + 1) * dv], NN) for (i, h), x in zip(units, xs)]
    ps = [seqs[i].ls[h] * three(seqs[i].qs[h], seqs[i].ks[h], NT) for i, h in units]
    os = [three(p, u, NN) for p, u in zip(ps, us)]
    for (i, h), x, u, o in zip(units, xs, us, os):
        rows, sl = seqs[i].rows, slice(h * dv, (h + 1) * dv)
        x_ref[i * hs + h] = x
        u_ref[rows, sl] = u
        o_ref[rows, sl] = o
        r = lax.rsqrt(jnp.mean(o * o, axis=-1, keepdims=True) + 1e-5)
        pg = pg_ref[rows, sl]
        out_ref[rows, sl] = (o * r * gain * (pg * sigmoid(pg))).astype(bf16)


def bwd_kernel(dims, half, has_before, *refs):
    shared, (x_ref, u_ref, o_ref, dm_ref) = refs[:9], refs[9:13]
    dp_ref, dba_ref, dtaps_ref, dgain_ref, dprm_ref = refs[-5:]
    pg_ref, gain_ref, prm_ref = refs[3], refs[7], refs[8]
    nh, dk, dv = dims
    hs = nh // SPLIT
    wq, wv = hs * dk, hs * dv
    at = half * hs
    iota_r, iota_c, tri, strict = planes(SEQ)
    gain = gain_ref[...]
    prm = prm_ref[...]
    seqs = [Sequence(dims, half, shared, slice(i * SEQ, (i + 1) * SEQ), iota_r, iota_c, tri) for i in range(dm_ref.shape[0] // SEQ)]
    units = [(i, h) for i in range(len(seqs)) for h in range(hs)]
    dgain = jnp.zeros_like(gain)
    dos, us = [], []
    for i, h in units:
        rows, sl = seqs[i].rows, slice(h * dv, (h + 1) * dv)
        o = o_ref[rows, sl]
        pg = pg_ref[rows, sl]
        dm = dm_ref[rows, sl]
        r = lax.rsqrt(jnp.mean(o * o, axis=-1, keepdims=True) + 1e-5)
        nrm = o * r
        sg = sigmoid(pg)
        dp_ref[rows, 2 * wq + wv + h * dv : 2 * wq + wv + (h + 1) * dv] = (dm * nrm * gain * (sg * (1.0 + pg * (1.0 - sg)))).astype(bf16)
        dy = dm * (pg * sg)
        dgain = dgain + jnp.sum(dy * nrm, axis=0, keepdims=True)
        dn = dy * gain
        dos.append(r * (dn - nrm * jnp.mean(nrm * dn, axis=-1, keepdims=True)))
        us.append(u_ref[rows, sl])
    bm = [jnp.where(strict, seqs[i].ls[h] * three(seqs[i].ks[h], seqs[i].ks[h], NT), 0.0) for i, h in units]
    ps = [seqs[i].ls[h] * three(seqs[i].qs[h], seqs[i].ks[h], NT) for i, h in units]
    dps = [three(do, u, NT) for do, u in zip(dos, us)]
    dus = [three(p, do, TN) for p, do in zip(ps, dos)]
    dws = [three(x_ref[i * hs + h], du, TN) for (i, h), du in zip(units, dus)]
    das = [-three(dw, u, NT) for dw, u in zip(dws, us)]

    @pl.when(pl.program_id(0) == 0)
    def _():
        dtaps_ref[...] = jnp.zeros_like(dtaps_ref)
        dgain_ref[...] = jnp.zeros_like(dgain_ref)
        dprm_ref[...] = jnp.zeros_like(dprm_ref)

    dgain_ref[...] += dgain
    lane = lax.broadcasted_iota(jnp.int32, (SEQ, 128), 1)
    ones = jnp.ones((SEQ, 128), f32)
    sc = dk ** -0.5
    for i, q in enumerate(seqs):
        rows, pos = q.rows, q.pos
        dbeta = jnp.zeros((SEQ, 128), f32)
        dlog = jnp.zeros((SEQ, 128), f32)
        dz = ([], [], [])
        for h in range(hs):
            n = i * hs + h
            vh = q.v[:, h * dv : (h + 1) * dv]
            ab = das[n] * bm[n]
            dbeta = jnp.where(lane == at + h, jnp.sum(dws[n] * vh, axis=-1, keepdims=True) + jnp.sum(ab, axis=-1, keepdims=True), dbeta)
            e = q.bs[h] * ab + dps[n] * ps[n]
            dlog = jnp.where(lane == nh + at + h, jnp.sum(e, axis=-1, keepdims=True) - exact_right(e, ones, TN), dlog)
            ds = dps[n] * q.ls[h]
            dmm = jnp.where(strict, q.bs[h] * das[n] * q.ls[h], 0.0)
            dq = sc * three(ds, q.ks[h], NN)
            dkh = three(ds, q.qs[h], TN) + three(dmm, q.ks[h], NN) + three(dmm, q.ks[h], TN)
            qh, rq = q.uq[h]
            kh, rk = q.uk[h]
            dz[0].append(rq * (dq - qh * jnp.sum(qh * dq, axis=-1, keepdims=True)))
            dz[1].append(rk * (dkh - kh * jnp.sum(kh * dkh, axis=-1, keepdims=True)))
            dz[2].append(q.bs[h] * dws[n])
        ddecay = exact_left(tri, dlog, TN)
        drate = -prm[0:1] * ddecay * sigmoid(q.rate)
        dba = dbeta * q.beta * (1.0 - q.beta) + drate
        if has_before:
            dba = dba + refs[13][rows, :]
            dp_ref[rows, 2 * wq + 2 * wv :] = dba.astype(bf16)
        dba_ref[rows, :] = dba
        dprm_ref[0:1, :] += jnp.sum(ddecay * q.decay, axis=0, keepdims=True)
        dprm_ref[1:2, :] += jnp.sum(drate, axis=0, keepdims=True)
        to = 0
        for parts, z, sg, c, tap in zip(dz, q.z, q.sig, q.raw, q.taps):
            d = jnp.concatenate(parts, axis=1) * (sg * (1.0 + z * (1.0 - sg)))
            width = tap.shape[0]
            w = c.shape[1]
            dc = d * tap[width - 1 : width]
            dtaps_ref[width - 1 : width, to : to + w] += jnp.sum(d * c, axis=0, keepdims=True)
            for s in range(1, width):
                m = jnp.where(pos >= s, d, 0.0)
                dc = dc + pltpu.roll(m, SEQ - s, 0) * tap[width - 1 - s : width - s]
                dtaps_ref[width - 1 - s : width - s, to : to + w] += jnp.sum(m * pltpu.roll(c, s, 0), axis=0, keepdims=True)
            dp_ref[rows, to : to + w] = dc.astype(bf16)
            to += w


def shared_specs(dims, off=0):
    nh, dk, dv = dims
    wq, wv = nh // SPLIT * dk, nh // SPLIT * dv
    at = (2 * wq) // wv
    small = (2 * wq + 2 * wv) // 128
    return [
        pl.BlockSpec((ROWS, wq), lambda i: (i + off, 0)),
        pl.BlockSpec((ROWS, wq), lambda i: (i + off, 1)),
        pl.BlockSpec((ROWS, wv), lambda i: (i + off, at)),
        pl.BlockSpec((ROWS, wv), lambda i: (i + off, at + 1)),
        pl.BlockSpec((ROWS, 128), lambda i: (i + off, small)),
        pl.BlockSpec((ROWS, 1), lambda i: (i + off, 0)),
        pl.BlockSpec((4, 2 * wq + wv), lambda i: (0, 0)),
        pl.BlockSpec((1, dv), lambda i: (0, 0)),
        pl.BlockSpec((8, 128), lambda i: (0, 0)),
    ]


def cost(us):
    return pl.CostEstimate(flops=int(us * 1.1e9), bytes_accessed=int(us * 1e6), transcendentals=0)


def mixer_fwd(proj, first, pos, taps, gain, prm, dims, half, mixed=None):
    tok = pos.shape[0]
    nh, dk, dv = dims
    hs = nh // SPLIT
    ns = tok // SEQ
    wv = hs * dv
    row = pl.BlockSpec((ROWS, wv), lambda i: (i, 0))
    specs = shared_specs(dims)
    args = [proj, proj, proj, proj, first, pos, taps, gain, prm]
    alias = {}
    if mixed is not None:
        alias = {len(args): 0}
        args.append(mixed)
        specs.append(pl.BlockSpec(memory_space=pl.ANY))
    return pl.pallas_call(
        functools.partial(fwd_kernel, dims, half),
        grid=(ns // PAIR,),
        in_specs=specs,
        out_specs=[
            pl.BlockSpec((ROWS, wv), lambda i: (i, half)),
            pl.BlockSpec((PAIR * hs, SEQ, SEQ), lambda i: (i, 0, 0)),
            row,
            row,
        ],
        out_shape=[
            jax.ShapeDtypeStruct((tok, nh * dv), bf16),
            jax.ShapeDtypeStruct((ns * hs, SEQ, SEQ), f32),
            jax.ShapeDtypeStruct((tok, wv), f32),
            jax.ShapeDtypeStruct((tok, wv), f32),
        ],
        input_output_aliases=alias,
        cost_estimate=cost(4),
        compiler_params=pltpu.CompilerParams(vmem_limit_bytes=48 << 20),
    )(*args)


def mixer_bwd(proj, first, pos, taps, gain, prm, x, u, o, dm, dims, half, part, before=None, filled=None):
    tok = pos.shape[0]
    nh, dk, dv = dims
    hs = nh // SPLIT
    ns = tok // SEQ
    wq, wv = hs * dk, hs * dv
    steps = dm.shape[0] // ROWS
    off = part * steps
    row = pl.BlockSpec((ROWS, wv), lambda i: (i + off, 0))
    lanes = pl.BlockSpec((ROWS, 128), lambda i: (i + off, 0))
    specs = shared_specs(dims, off) + [
        pl.BlockSpec((PAIR * hs, SEQ, SEQ), lambda i: (i + off, 0, 0)), row, row, pl.BlockSpec((ROWS, wv), lambda i: (i, half))]
    args = [proj, proj, proj, proj, first, pos, taps, gain, prm, x, u, o, dm]
    width = 2 * wq + 2 * wv
    if before is not None:
        args.append(before)
        specs.append(lanes)
        width += 128
    alias = {}
    if filled is not None:
        alias = {len(args): 0, len(args) + 1: 1}
        args += filled
        specs += [pl.BlockSpec(memory_space=pl.ANY)] * 2
    return pl.pallas_call(
        functools.partial(bwd_kernel, dims, half, before is not None),
        grid=(steps,),
        in_specs=specs,
        out_specs=[
            pl.BlockSpec((ROWS, width), lambda i: (i + off, 0)),
            lanes,
            pl.BlockSpec((4, 2 * wq + wv), lambda i: (0, 0)),
            pl.BlockSpec((1, dv), lambda i: (0, 0)),
            pl.BlockSpec((8, 128), lambda i: (0, 0)),
        ],
        out_shape=[
            jax.ShapeDtypeStruct((tok, width), bf16),
            jax.ShapeDtypeStruct((tok, 128), f32),
            jax.ShapeDtypeStruct((4, 2 * wq + wv), f32),
            jax.ShapeDtypeStruct((1, dv), f32),
            jax.ShapeDtypeStruct((8, 128), f32),
        ],
        input_output_aliases=alias,
        cost_estimate=cost(26),
        compiler_params=pltpu.CompilerParams(vmem_limit_bytes=56 << 20),
    )(*args)


def xor_send(value, axis, size, step):
    return lax.ppermute(value, axis, [(i, i ^ step) for i in range(size)])


def after(value, *needs):
    return lax.optimization_barrier((value, *needs))[0]


def lines(size):
    return [[low + 2 * i for i in range(size // 2)] for low in range(2)]


def gather_line(rows, size):
    return lax.all_gather(rows, "fsdp", axis=0, tiled=True, axis_index_groups=lines(size))


def gather_side(near, size, *needs):
    got = xor_send(after(near, *needs) if needs else near, "fsdp", size, 1)
    return jnp.concatenate([near, got], axis=0), got


def dot(left, right, dims=NN, out=f32):
    return lax.dot_general(left, right, dims, preferred_element_type=f32).astype(out)


class Summed:
    def __init__(self, left, right, size, *needs):
        self.size = size
        self.half = left.shape[1] // 2
        self.left, self.right = left, right
        self.sent = dot(left[:, self.half :], right, TN, bf16)
        self.got = xor_send(after(self.sent, *needs) if needs else self.sent, "fsdp", size, 1)

    def side(self, *needs):
        keep = dot(self.left[:, : self.half], after(self.right, *needs) if needs else self.right, TN)
        self.low = (keep + self.got.astype(f32)).astype(bf16)
        self.sum = lax.psum_scatter(self.low, "fsdp", scatter_dimension=0, tiled=True, axis_index_groups=lines(self.size))

    def total(self, ranks):
        return lax.all_to_all(self.sum.reshape(ranks, -1, self.sum.shape[1]), "rep", 0, 0)


def join_tokens(rows, size):
    half = size // 2

    def around(block):
        held = {0: block}
        step = half // 2
        while step:
            for j in list(held):
                held[j ^ step] = xor_send(held[j], "rep", size, step)
            step //= 2
        return jnp.concatenate([held[j] for j in range(half)], axis=0)

    beyond = xor_send(rows, "rep", size, half)
    return around(rows), around(beyond)


def sum_tokens(far, near, size, *needs):
    half = size // 2

    def around(part):
        held = jnp.split(part, half, axis=0)
        step = 1
        while step < half:
            for j in range(0, half, 2 * step):
                held[j] = held[j] + xor_send(held[j + step].astype(bf16), "rep", size, step).astype(f32)
            step *= 2
        return held[0]

    beyond = around(far()).astype(bf16)
    part = near(beyond)
    if needs:
        beyond = after(beyond, *needs)
    got = xor_send(beyond, "rep", size, half)
    return around(part) + got.astype(f32), got


def rms(values):
    return lax.rsqrt(jnp.mean(values * values, axis=-1, keepdims=True) + 1e-06)


def norm_back(n, r, gain, dout):
    scaled = dout * gain
    return r * (scaled - n * jnp.mean(n * scaled, axis=-1, keepdims=True)), jnp.sum(dout * n, axis=0)


def make(F, R):
    both = ("fsdp", "rep")

    def on_device(tokens, segments, cotangent, gain_one, w_query, w_key, w_value, w_gate, w_beta, w_alpha, conv_q, conv_k,
                  conv_v, a_log, dt_bias, norm_gain, w_out, gain_two, w_ffgate, w_ffup, w_down):
        f = lax.axis_index("fsdp")
        r = lax.axis_index("rep")
        N = F * R
        rows_own, D = tokens.shape
        heads = a_log.shape[0]
        dk = w_query.shape[1] // heads
        dv = w_value.shape[1] // heads
        nh = heads // R
        dims = (nh, dk, dv)
        wq, wv = nh * dk, nh * dv
        hq, hv = wq // SPLIT, wv // SPLIT
        shard = D // N
        block = D // F
        ffq = w_ffgate.shape[1] // R
        tok = rows_own * R
        ns = tok // SEQ
        tiny = dv // N
        per = conv_v.shape[1] // shard

        low_bit = f & 1

        def swap(array, axis):
            half = array.shape[axis] // 2
            return jnp.concatenate(
                [lax.dynamic_slice_in_dim(array, (low_bit ^ j) * half, half, axis=axis) for j in range(2)], axis=axis)

        def mix(array, axis):
            at = [slice(None)] * array.ndim
            parts = []
            for bit in range(2):
                for i in range(F // 2):
                    at[axis] = slice((2 * i + bit) * block, (2 * i + bit + 1) * block)
                    parts.append(array[tuple(at)])
            return swap(jnp.concatenate(parts, axis=axis), axis)

        def unmix(array, axis):
            array = swap(array, axis)
            at = [slice(None)] * array.ndim
            parts = []
            for i in range(F // 2):
                for bit in range(2):
                    p = bit * (F // 2) + i
                    at[axis] = slice(p * block, (p + 1) * block)
                    parts.append(array[tuple(at)])
            return jnp.concatenate(parts, axis=axis)

        def quarter(arrays):
            return jnp.concatenate([a.reshape(shard, R, -1) for a in arrays], axis=2)

        def spread(packed):
            return lax.all_to_all(packed.transpose(1, 0, 2), "rep", 0, 0).reshape(R * shard, -1)

        extra = jnp.concatenate(
            [gain_one[:, None], gain_two[:, None], conv_q.T, conv_k.T,
             conv_v.reshape(4, shard, per).transpose(1, 0, 2).reshape(shard, 4 * per),
             jnp.pad(norm_gain, (0, shard - tiny))[:, None]], axis=1).T
        small = jnp.concatenate([w_beta.reshape(shard, R, nh), w_alpha.reshape(shard, R, nh)], axis=2)
        small = jnp.pad(small, ((0, 0), (0, 0), (0, 128 - 2 * nh)))

        def halves(array, width):
            parts = array.reshape(shard, R, SPLIT, width)
            return [parts[:, :, h] for h in range(SPLIT)]

        q_h, k_h, v_h, g_h = halves(w_query, hq), halves(w_key, hq), halves(w_value, hv), halves(w_gate, hv)
        own = mix(tokens, 1)
        part_a = spread(jnp.concatenate([q_h[0], k_h[0], v_h[0], g_h[0], small, q_h[1], k_h[1], v_h[1], g_h[1]], axis=2))
        w1 = 2 * hq + 2 * hv
        part_1, part_2 = part_a[:, : w1 + 128], part_a[:, w1 + 128 :]
        extra_all = lax.all_to_all(jnp.broadcast_to(after(extra, part_a)[None], (N, *extra.shape)), both, 0, 0)
        extra_all = extra_all.transpose(1, 0, 2).reshape(-1, D).astype(f32)
        line_1 = gather_line(part_1, F)
        every = jnp.concatenate(join_tokens(own, R), axis=0)
        ids_all = jnp.concatenate(join_tokens(segments[:, None], R), axis=0).reshape(ns, SEQ)
        part_r = spread(quarter([after(w_out.T, extra_all), w_ffgate, w_ffup, w_down.T]))
        part_b, part_g, part_u, part_d = (
            part_r[:, :wv], part_r[:, wv : wv + ffq], part_r[:, wv + ffq : wv + 2 * ffq], part_r[:, wv + 2 * ffq :])
        line_2 = gather_line(after(part_2, extra_all), F)
        wa1, side_1 = gather_side(line_1, F)
        cot = mix(cotangent, 1)
        cot_near, cot_far = join_tokens(after(cot, every), R)
        line_b = gather_line(part_b, F)
        line_g = gather_line(part_g, F)
        line_u = gather_line(part_u, F)
        line_d = gather_line(part_d, F)

        gains = mix(extra_all[:2], 1)
        gain_first, gain_second = gains[0:1], gains[1:2]
        cq = lax.dynamic_slice_in_dim(extra_all[2:6], r * wq, wq, axis=1)
        ck = lax.dynamic_slice_in_dim(extra_all[6:10], r * wq, wq, axis=1)
        cv = extra_all[10 : 10 + 4 * per].reshape(4, per, D).transpose(0, 2, 1).reshape(4, D * per)
        cv = lax.dynamic_slice_in_dim(cv, r * wv, wv, axis=1)
        gain_out = extra_all[10 + 4 * per].reshape(N, shard)[:, :tiny].reshape(1, dv)
        taps = [jnp.concatenate([cq[:, h * hq : (h + 1) * hq], ck[:, h * hq : (h + 1) * hq], cv[:, h * hv : (h + 1) * hv]], axis=1)
                for h in range(SPLIT)]
        prm = jnp.stack([jnp.exp(lax.dynamic_slice_in_dim(a_log, r * nh, nh)), lax.dynamic_slice_in_dim(dt_bias, r * nh, nh)])
        prm = jnp.pad(prm, ((0, 6), (nh, 128 - 2 * nh)))
        place = jnp.arange(SEQ)
        same = (ids_all[:, :, None] == ids_all[:, None, :]) & (place[:, None] >= place[None, :])[None]
        pos = (jnp.sum(same.astype(f32), axis=2) - 1.0).reshape(tok, 1)

        every32 = every.astype(f32)
        normed_one = (every32 * rms(every32) * gain_first).astype(bf16)
        proj_1 = dot(after(normed_one, line_2, cot_near, cot_far, part_r, pos), wa1)
        mixed, x_1, u_1, o_1 = mixer_fwd(proj_1, proj_1, pos, taps[0], gain_out, prm, dims, 0)
        wa2, side_2 = gather_side(line_2, F, side_1)
        proj_2 = dot(after(normed_one, mixed, line_b), wa2)
        mixed, x_2, u_2, o_2 = mixer_fwd(proj_2, proj_1, pos, taps[1], gain_out, prm, dims, 1, mixed)
        wb, side_b = gather_side(line_b, F, side_2)
        mixed = after(mixed, line_g)
        wg, side_g = gather_side(line_g, F, side_b)
        own32 = own.astype(f32)
        mid = tok // 2
        added, unused = sum_tokens(lambda: dot(mixed[mid:], wb, NT), lambda part: dot(after(mixed, part)[:mid], wb, NT), R)
        middle = own32 + added
        r2 = rms(middle)
        n2 = middle * r2
        normed_own = (n2 * gain_second).astype(bf16)
        wu, side_u = gather_side(line_u, F, side_g)
        two = join_tokens(after(normed_own, line_u), R)
        wd, side_d = gather_side(line_d, F, side_u)
        gates, ups, acts, sigs, hiddens = [], [], [], [], []
        for normed in two:
            gates.append(dot(normed, wg))
            ups.append(dot(normed, wu))
            sigs.append(jax.nn.sigmoid(gates[-1]))
            acts.append(gates[-1] * sigs[-1])
            hiddens.append((acts[-1] * ups[-1]).astype(bf16))
        hidden = jnp.concatenate(hiddens, axis=0)
        normed_two = jnp.concatenate(two, axis=0)
        cot_all = jnp.concatenate([cot_near, cot_far], axis=0)

        kept = {}

        def keep(name, value):
            kept[name] = value
            return value

        g_down = Summed(cot_all, hidden, F)
        dgates, dups = [None, None], [None, None]

        def back_two(t, *needs):
            dhidden = dot(after((cot_near, cot_far)[t], *needs), wd)
            dgates[t] = (dhidden * ups[t] * (sigs[t] * (1.0 + gates[t] * (1.0 - sigs[t])))).astype(bf16)
            dups[t] = (dhidden * acts[t]).astype(bf16)
            return dot(dgates[t], wg, NT) + dot(dups[t], wu, NT)

        dnormed_two, far_two = sum_tokens(lambda: back_two(1, g_down.sent), lambda part: keep("two", back_two(0, part)), R)
        g_gate = Summed(normed_two, after(jnp.concatenate(dgates, axis=0), kept["two"]), F, g_down.got)
        dinner, dgain_second = norm_back(n2, r2, gain_second, after(dnormed_two, g_gate.sent))
        dmiddle = cot.astype(f32) + dinner
        dmiddle_own = dmiddle.astype(bf16)
        dlow = join_tokens(dmiddle_own, R)
        g_down.side(dmiddle_own)
        dm_near = dot(after(dlow[0], g_down.low), wb)
        args_2 = (proj_2, proj_1, pos, taps[1], gain_out, prm, x_2, u_2, o_2)
        args_1 = (proj_1, proj_1, pos, taps[0], gain_out, prm, x_1, u_1, o_1)
        dp_2, dba, dt_2, dg_2, dr_2 = mixer_bwd(*args_2, dm_near, dims, 1, 0)
        g_up = Summed(normed_two, after(jnp.concatenate(dups, axis=0), dba), F, g_gate.got)
        g_gate.side(g_up.sent)
        dp_1, dba_1, dt_1, dg_1, dr_1 = mixer_bwd(*args_1, after(dm_near, g_gate.low), dims, 0, 0, dba)
        t_down = g_down.total(R)
        dm_far = dot(after(dlow[1], dba_1), wb)
        dp_2, dba, et_2, eg_2, er_2 = mixer_bwd(*args_2, dm_far, dims, 1, 1, None, [dp_2, dba])
        g_2 = Summed(normed_one, dp_2, F, g_up.got)
        g_up.side(g_2.sent)
        t_gate = g_gate.total(R)
        dp_1, dba_1, et_1, eg_1, er_1 = mixer_bwd(
            *args_1, after(dm_far, g_up.low, t_down), dims, 0, 1, dba, [dp_1, dba_1])
        g_1 = Summed(normed_one, dp_1, F, g_2.got)
        g_out = Summed(jnp.concatenate(dlow, axis=0), after(mixed, g_1.sent), F, g_1.got)
        t_up = g_up.total(R)
        g_2.side(g_out.sent)

        def back_one(lo, hi, *needs):
            return dot(after(dp_1, *needs)[lo:hi], wa1, NT) + dot(dp_2[lo:hi], wa2, NT)

        dnormed_one, far_one = sum_tokens(
            lambda: back_one(mid, tok, g_out.sent, t_gate), lambda part: keep("one", back_one(0, mid, part, g_2.low)), R)
        added, unused = sum_tokens(
            lambda: dot(after(hiddens[1], kept["one"], t_up), wd, NT), lambda part: dot(after(hiddens[0], part), wd, NT), R)
        layer_out = (middle + added).astype(bf16)
        g_1.side(kept["one"])
        g_out.side(g_1.low)
        t_out = g_out.total(R)
        dprm = dr_1 + dr_2 + er_1 + er_2
        dgain_out = dg_1 + dg_2 + eg_1 + eg_2
        dtaps = [dt_1 + et_1, dt_2 + et_2]

        n1 = own32 * rms(own32)
        dfirst, dgain_first = norm_back(n1, rms(own32), gain_first, dnormed_one)
        grad_tokens = unmix(dmiddle + dfirst, 1)

        def wide(parts):
            return parts.astype(f32).transpose(1, 0, 2).reshape(shard, -1)

        def tall(parts):
            return parts.astype(f32).transpose(0, 2, 1).reshape(-1, shard)

        t_2 = g_2.total(R)
        t_1 = g_1.total(R)

        def joined(lo, width):
            return jnp.stack([t[:, :, lo : lo + width] for t in (t_1, t_2)], axis=2).astype(f32).transpose(1, 0, 2, 3).reshape(shard, -1)

        grad_query, grad_key = joined(0, hq), joined(hq, hq)
        grad_value, grad_gate_w = joined(2 * hq, hv), joined(2 * hq + hv, hv)
        grad_beta, grad_alpha = wide(t_1[:, :, w1 : w1 + nh]), wide(t_1[:, :, w1 + nh : w1 + 2 * nh])
        grad_down, grad_out = tall(t_down), tall(t_out)
        grad_gate, grad_up = wide(t_gate), wide(t_up)

        def placed(parts, total, width):
            part = jnp.concatenate(parts, axis=1)
            return lax.dynamic_update_slice(jnp.zeros((4, total), f32), part, (0, r * width))

        gq = placed([dtaps[h][:, :hq] for h in range(SPLIT)], R * wq, wq)
        gk = placed([dtaps[h][:, hq : 2 * hq] for h in range(SPLIT)], R * wq, wq)
        gv = placed([dtaps[h][:, 2 * hq :] for h in range(SPLIT)], R * wv, wv)
        heads_part = lax.dynamic_update_slice(jnp.zeros((2, heads), f32), dprm[:2, nh : 2 * nh], (0, r * nh)).reshape(1, -1)
        packed = jnp.concatenate([
            unmix(dgain_first[None], 1).reshape(N, -1),
            unmix(dgain_second[None], 1).reshape(N, -1),
            gq.reshape(4, N, -1).transpose(1, 0, 2).reshape(N, -1),
            gk.reshape(4, N, -1).transpose(1, 0, 2).reshape(N, -1),
            gv.reshape(4, N, -1).transpose(1, 0, 2).reshape(N, -1),
            dgain_out.reshape(N, tiny),
            jnp.broadcast_to(heads_part, (N, 2 * heads))], axis=1)
        summed = jnp.sum(lax.all_to_all(packed, both, 0, 0, tiled=True), axis=0)
        sizes = [shard, shard, 4 * shard, 4 * shard, 4 * shard * per, tiny, heads, heads]
        ends = [0]
        for size in sizes:
            ends.append(ends[-1] + size)
        pick = [summed[ends[i] : ends[i + 1]] for i in range(len(sizes))]
        return (
            unmix(layer_out, 1), grad_tokens, pick[0], grad_query, grad_key, grad_value, grad_gate_w, grad_beta, grad_alpha,
            pick[2].reshape(4, shard), pick[3].reshape(4, shard), pick[4].reshape(4, shard * per), pick[6], pick[7], pick[5],
            grad_out, pick[1], grad_gate, grad_up, grad_down)

    return on_device


def solution(mesh):
    rows, cols, flat = P(("fsdp", "rep"), None), P(None, ("fsdp", "rep")), P(("fsdp", "rep"))
    placed = (rows, flat, rows, flat, rows, rows, rows, rows, rows, rows, cols, cols, cols, P(), P(), flat, cols, flat, rows, rows, cols)
    made = (rows, rows, flat, rows, rows, rows, rows, rows, rows, cols, cols, cols, P(), P(), flat, cols, flat, rows, rows, cols)
    return jax.shard_map(
        make(mesh.shape["fsdp"], mesh.shape["rep"]), mesh=mesh, in_specs=placed, out_specs=made, check_vma=False)
```

```python
import functools

import jax
import jax.numpy as jnp
from jax import lax
from jax.experimental import pallas as pl
from jax.experimental.pallas import tpu as pltpu
from jax.sharding import PartitionSpec as P

SEQ = 256
SPLIT = 2
PAIR = 2
ROWS = PAIR * SEQ

f32 = jnp.float32
bf16 = jnp.bfloat16
NN = (((1,), (0,)), ((), ()))
NT = (((1,), (1,)), ((), ()))
TN = (((0,), (0,)), ((), ()))


def split(a):
    hi = a.astype(bf16)
    return hi, (a - hi.astype(f32)).astype(bf16)


def one(a, b, dims):
    return lax.dot_general(a.astype(bf16), b.astype(bf16), dims, preferred_element_type=f32)


def three(a, b, dims):
    ah, al = split(a)
    bh, bl = split(b)
    out = lax.dot_general(ah, bl, dims, preferred_element_type=f32)
    out = out + lax.dot_general(al, bh, dims, preferred_element_type=f32)
    return out + lax.dot_general(ah, bh, dims, preferred_element_type=f32)


def exact_left(a, b, dims):
    bh, bl = split(b)
    a = a.astype(bf16)
    return lax.dot_general(a, bh, dims, preferred_element_type=f32) + lax.dot_general(a, bl, dims, preferred_element_type=f32)


def exact_right(a, b, dims):
    ah, al = split(a)
    b = b.astype(bf16)
    return lax.dot_general(ah, b, dims, preferred_element_type=f32) + lax.dot_general(al, b, dims, preferred_element_type=f32)


def sigmoid(v):
    return 1.0 / (1.0 + jnp.exp(-v))


def conv(c, taps, pos):
    width = taps.shape[0]
    z = c * taps[width - 1 : width]
    for s in range(1, width):
        z = z + jnp.where(pos >= s, pltpu.roll(c, s, 0), 0.0) * taps[width - 1 - s : width - s]
    return z


def unit(c):
    r = lax.rsqrt(jnp.sum(c * c, axis=-1, keepdims=True) + 1e-6)
    return c * r, r


def inverses(n_list, iota_r, iota_c):
    size = n_list[0].shape[0]
    eye = (iota_r == iota_c).astype(f32)
    xs = None
    b = 1
    while b < size:
        mask = ((iota_r // (2 * b)) == (iota_c // (2 * b))) & ((iota_r // b) % 2 == 1) & ((iota_c // b) % 2 == 0)
        cs = [jnp.where(mask, n, 0.0) for n in n_list]
        if xs is None:
            xs = [eye - c for c in cs]
        else:
            low = [x.astype(bf16) for x in xs]
            t = [one(c, x, NN) for c, x in zip(cs, low)]
            xs = [x - one(y, z, NN) for x, y, z in zip(xs, low, t)]
        b *= 2
    left = [(eye - x) - three(n, x, NN) for n, x in zip(n_list, xs)]
    return [x + one(x, r, NN) for x, r in zip(xs, left)]


def rates(pba, prm, tri):
    beta = sigmoid(pba)
    rate = pba + prm[1:2]
    decay = -prm[0:1] * (jnp.maximum(rate, 0.0) + jnp.log1p(jnp.exp(-jnp.abs(rate))))
    return beta, rate, decay, exact_left(tri, decay, NN), exact_right(decay, tri, (((0,), (1,)), ((), ())))


class Sequence:
    def __init__(self, dims, half, refs, rows, iota_r, iota_c, tri):
        pq_ref, pk_ref, pv_ref, pg_ref, ba_ref, pos_ref, taps_ref, gain_ref, prm_ref = refs
        nh, dk, dv = dims
        hs = nh // SPLIT
        wq = hs * dk
        at = half * hs
        H = range(hs)
        self.rows = rows
        self.pos = pos_ref[rows, :]
        taps = taps_ref[...]
        self.taps = (taps[:, :wq], taps[:, wq : 2 * wq], taps[:, 2 * wq :])
        self.raw = (pq_ref[rows, :], pk_ref[rows, :], pv_ref[rows, :])
        self.beta, self.rate, self.decay, gcol, grow = rates(ba_ref[rows, :], prm_ref[...], tri)
        self.z = tuple(conv(c, t, self.pos) for c, t in zip(self.raw, self.taps))
        self.sig = tuple(sigmoid(z) for z in self.z)
        qc, kc, self.v = (z * g for z, g in zip(self.z, self.sig))
        live = (iota_c <= iota_r) & (iota_c >= iota_r - self.pos.astype(jnp.int32))
        self.bs = [self.beta[:, at + h : at + h + 1] for h in H]
        self.uq = [unit(qc[:, h * dk : (h + 1) * dk]) for h in H]
        self.uk = [unit(kc[:, h * dk : (h + 1) * dk]) for h in H]
        self.qs = [a * dk ** -0.5 for a, _ in self.uq]
        self.ks = [a for a, _ in self.uk]
        lane = nh + at
        self.ls = [
            jnp.where(live, jnp.exp(jnp.where(live, gcol[:, lane + h : lane + h + 1] - grow[lane + h : lane + h + 1, :], 0.0)), 0.0)
            for h in H]


def planes(n):
    iota_r = lax.broadcasted_iota(jnp.int32, (n, n), 0)
    iota_c = lax.broadcasted_iota(jnp.int32, (n, n), 1)
    return iota_r, iota_c, (iota_c <= iota_r).astype(f32), iota_c < iota_r


def fwd_kernel(dims, half, *refs):
    shared, (out_ref, x_ref, u_ref, o_ref) = refs[:9], refs[-4:]
    pg_ref, gain_ref = refs[3], refs[7]
    nh, dk, dv = dims
    hs = nh // SPLIT
    iota_r, iota_c, tri, strict = planes(SEQ)
    gain = gain_ref[...]
    seqs = [Sequence(dims, half, shared, slice(i * SEQ, (i + 1) * SEQ), iota_r, iota_c, tri) for i in range(out_ref.shape[0] // SEQ)]
    units = [(i, h) for i in range(len(seqs)) for h in range(hs)]
    ms = [three(seqs[i].ks[h], seqs[i].ks[h], NT) for i, h in units]
    ns = [jnp.where(strict, seqs[i].bs[h] * seqs[i].ls[h] * m, 0.0) for (i, h), m in zip(units, ms)]
    xs = inverses(ns, iota_r, iota_c)
    us = [three(x, seqs[i].bs[h] * seqs[i].v[:, h * dv : (h + 1) * dv], NN) for (i, h), x in zip(units, xs)]
    ps = [seqs[i].ls[h] * three(seqs[i].qs[h], seqs[i].ks[h], NT) for i, h in units]
    os = [three(p, u, NN) for p, u in zip(ps, us)]
    for (i, h), x, u, o in zip(units, xs, us, os):
        rows, sl = seqs[i].rows, slice(h * dv, (h + 1) * dv)
        x_ref[i * hs + h] = x
        u_ref[rows, sl] = u
        o_ref[rows, sl] = o
        r = lax.rsqrt(jnp.mean(o * o, axis=-1, keepdims=True) + 1e-5)
        pg = pg_ref[rows, sl]
        out_ref[rows, sl] = (o * r * gain * (pg * sigmoid(pg))).astype(bf16)


def bwd_kernel(dims, half, has_before, *refs):
    shared, (x_ref, u_ref, o_ref, dm_ref) = refs[:9], refs[9:13]
    dp_ref, dba_ref, dtaps_ref, dgain_ref, dprm_ref = refs[-5:]
    pg_ref, gain_ref, prm_ref = refs[3], refs[7], refs[8]
    nh, dk, dv = dims
    hs = nh // SPLIT
    wq, wv = hs * dk, hs * dv
    at = half * hs
    iota_r, iota_c, tri, strict = planes(SEQ)
    gain = gain_ref[...]
    prm = prm_ref[...]
    seqs = [Sequence(dims, half, shared, slice(i * SEQ, (i + 1) * SEQ), iota_r, iota_c, tri) for i in range(dm_ref.shape[0] // SEQ)]
    units = [(i, h) for i in range(len(seqs)) for h in range(hs)]
    dgain = jnp.zeros_like(gain)
    dos, us = [], []
    for i, h in units:
        rows, sl = seqs[i].rows, slice(h * dv, (h + 1) * dv)
        o = o_ref[rows, sl]
        pg = pg_ref[rows, sl]
        dm = dm_ref[rows, sl]
        r = lax.rsqrt(jnp.mean(o * o, axis=-1, keepdims=True) + 1e-5)
        nrm = o * r
        sg = sigmoid(pg)
        dp_ref[rows, 2 * wq + wv + h * dv : 2 * wq + wv + (h + 1) * dv] = (dm * nrm * gain * (sg * (1.0 + pg * (1.0 - sg)))).astype(bf16)
        dy = dm * (pg * sg)
        dgain = dgain + jnp.sum(dy * nrm, axis=0, keepdims=True)
        dn = dy * gain
        dos.append(r * (dn - nrm * jnp.mean(nrm * dn, axis=-1, keepdims=True)))
        us.append(u_ref[rows, sl])
    bm = [jnp.where(strict, seqs[i].ls[h] * three(seqs[i].ks[h], seqs[i].ks[h], NT), 0.0) for i, h in units]
    ps = [seqs[i].ls[h] * three(seqs[i].qs[h], seqs[i].ks[h], NT) for i, h in units]
    dps = [three(do, u, NT) for do, u in zip(dos, us)]
    dus = [three(p, do, TN) for p, do in zip(ps, dos)]
    dws = [three(x_ref[i * hs + h], du, TN) for (i, h), du in zip(units, dus)]
    das = [-three(dw, u, NT) for dw, u in zip(dws, us)]

    @pl.when(pl.program_id(0) == 0)
    def _():
        dtaps_ref[...] = jnp.zeros_like(dtaps_ref)
        dgain_ref[...] = jnp.zeros_like(dgain_ref)
        dprm_ref[...] = jnp.zeros_like(dprm_ref)

    dgain_ref[...] += dgain
    lane = lax.broadcasted_iota(jnp.int32, (SEQ, 128), 1)
    ones = jnp.ones((SEQ, 128), f32)
    sc = dk ** -0.5
    for i, q in enumerate(seqs):
        rows, pos = q.rows, q.pos
        dbeta = jnp.zeros((SEQ, 128), f32)
        dlog = jnp.zeros((SEQ, 128), f32)
        dz = ([], [], [])
        for h in range(hs):
            n = i * hs + h
            vh = q.v[:, h * dv : (h + 1) * dv]
            ab = das[n] * bm[n]
            dbeta = jnp.where(lane == at + h, jnp.sum(dws[n] * vh, axis=-1, keepdims=True) + jnp.sum(ab, axis=-1, keepdims=True), dbeta)
            e = q.bs[h] * ab + dps[n] * ps[n]
            dlog = jnp.where(lane == nh + at + h, jnp.sum(e, axis=-1, keepdims=True) - exact_right(e, ones, TN), dlog)
            ds = dps[n] * q.ls[h]
            dmm = jnp.where(strict, q.bs[h] * das[n] * q.ls[h], 0.0)
            dq = sc * three(ds, q.ks[h], NN)
            dkh = three(ds, q.qs[h], TN) + three(dmm, q.ks[h], NN) + three(dmm, q.ks[h], TN)
            qh, rq = q.uq[h]
            kh, rk = q.uk[h]
            dz[0].append(rq * (dq - qh * jnp.sum(qh * dq, axis=-1, keepdims=True)))
            dz[1].append(rk * (dkh - kh * jnp.sum(kh * dkh, axis=-1, keepdims=True)))
            dz[2].append(q.bs[h] * dws[n])
        ddecay = exact_left(tri, dlog, TN)
        drate = -prm[0:1] * ddecay * sigmoid(q.rate)
        dba = dbeta * q.beta * (1.0 - q.beta) + drate
        if has_before:
            dba = dba + refs[13][rows, :]
            dp_ref[rows, 2 * wq + 2 * wv :] = dba.astype(bf16)
        dba_ref[rows, :] = dba
        dprm_ref[0:1, :] += jnp.sum(ddecay * q.decay, axis=0, keepdims=True)
        dprm_ref[1:2, :] += jnp.sum(drate, axis=0, keepdims=True)
        to = 0
        for parts, z, sg, c, tap in zip(dz, q.z, q.sig, q.raw, q.taps):
            d = jnp.concatenate(parts, axis=1) * (sg * (1.0 + z * (1.0 - sg)))
            width = tap.shape[0]
            w = c.shape[1]
            dc = d * tap[width - 1 : width]
            dtaps_ref[width - 1 : width, to : to + w] += jnp.sum(d * c, axis=0, keepdims=True)
            for s in range(1, width):
                m = jnp.where(pos >= s, d, 0.0)
                dc = dc + pltpu.roll(m, SEQ - s, 0) * tap[width - 1 - s : width - s]
                dtaps_ref[width - 1 - s : width - s, to : to + w] += jnp.sum(m * pltpu.roll(c, s, 0), axis=0, keepdims=True)
            dp_ref[rows, to : to + w] = dc.astype(bf16)
            to += w


def shared_specs(dims, off=0):
    nh, dk, dv = dims
    wq, wv = nh // SPLIT * dk, nh // SPLIT * dv
    at = (2 * wq) // wv
    small = (2 * wq + 2 * wv) // 128
    return [
        pl.BlockSpec((ROWS, wq), lambda i: (i + off, 0)),
        pl.BlockSpec((ROWS, wq), lambda i: (i + off, 1)),
        pl.BlockSpec((ROWS, wv), lambda i: (i + off, at)),
        pl.BlockSpec((ROWS, wv), lambda i: (i + off, at + 1)),
        pl.BlockSpec((ROWS, 128), lambda i: (i + off, small)),
        pl.BlockSpec((ROWS, 1), lambda i: (i + off, 0)),
        pl.BlockSpec((4, 2 * wq + wv), lambda i: (0, 0)),
        pl.BlockSpec((1, dv), lambda i: (0, 0)),
        pl.BlockSpec((8, 128), lambda i: (0, 0)),
    ]


def cost(us):
    return pl.CostEstimate(flops=int(us * 1.1e9), bytes_accessed=int(us * 1e6), transcendentals=0)


def mixer_fwd(proj, first, pos, taps, gain, prm, dims, half, mixed=None):
    tok = pos.shape[0]
    nh, dk, dv = dims
    hs = nh // SPLIT
    ns = tok // SEQ
    wv = hs * dv
    row = pl.BlockSpec((ROWS, wv), lambda i: (i, 0))
    specs = shared_specs(dims)
    args = [proj, proj, proj, proj, first, pos, taps, gain, prm]
    alias = {}
    if mixed is not None:
        alias = {len(args): 0}
        args.append(mixed)
        specs.append(pl.BlockSpec(memory_space=pl.ANY))
    return pl.pallas_call(
        functools.partial(fwd_kernel, dims, half),
        grid=(ns // PAIR,),
        in_specs=specs,
        out_specs=[
            pl.BlockSpec((ROWS, wv), lambda i: (i, half)),
            pl.BlockSpec((PAIR * hs, SEQ, SEQ), lambda i: (i, 0, 0)),
            row,
            row,
        ],
        out_shape=[
            jax.ShapeDtypeStruct((tok, nh * dv), bf16),
            jax.ShapeDtypeStruct((ns * hs, SEQ, SEQ), f32),
            jax.ShapeDtypeStruct((tok, wv), f32),
            jax.ShapeDtypeStruct((tok, wv), f32),
        ],
        input_output_aliases=alias,
        cost_estimate=cost(4),
        compiler_params=pltpu.CompilerParams(vmem_limit_bytes=48 << 20),
    )(*args)


def mixer_bwd(proj, first, pos, taps, gain, prm, x, u, o, dm, dims, half, part, before=None, filled=None):
    tok = pos.shape[0]
    nh, dk, dv = dims
    hs = nh // SPLIT
    ns = tok // SEQ
    wq, wv = hs * dk, hs * dv
    steps = dm.shape[0] // ROWS
    off = part * steps
    row = pl.BlockSpec((ROWS, wv), lambda i: (i + off, 0))
    lanes = pl.BlockSpec((ROWS, 128), lambda i: (i + off, 0))
    specs = shared_specs(dims, off) + [
        pl.BlockSpec((PAIR * hs, SEQ, SEQ), lambda i: (i + off, 0, 0)), row, row, pl.BlockSpec((ROWS, wv), lambda i: (i, half))]
    args = [proj, proj, proj, proj, first, pos, taps, gain, prm, x, u, o, dm]
    width = 2 * wq + 2 * wv
    if before is not None:
        args.append(before)
        specs.append(lanes)
        width += 128
    alias = {}
    if filled is not None:
        alias = {len(args): 0, len(args) + 1: 1}
        args += filled
        specs += [pl.BlockSpec(memory_space=pl.ANY)] * 2
    return pl.pallas_call(
        functools.partial(bwd_kernel, dims, half, before is not None),
        grid=(steps,),
        in_specs=specs,
        out_specs=[
            pl.BlockSpec((ROWS, width), lambda i: (i + off, 0)),
            lanes,
            pl.BlockSpec((4, 2 * wq + wv), lambda i: (0, 0)),
            pl.BlockSpec((1, dv), lambda i: (0, 0)),
            pl.BlockSpec((8, 128), lambda i: (0, 0)),
        ],
        out_shape=[
            jax.ShapeDtypeStruct((tok, width), bf16),
            jax.ShapeDtypeStruct((tok, 128), f32),
            jax.ShapeDtypeStruct((4, 2 * wq + wv), f32),
            jax.ShapeDtypeStruct((1, dv), f32),
            jax.ShapeDtypeStruct((8, 128), f32),
        ],
        input_output_aliases=alias,
        cost_estimate=cost(26),
        compiler_params=pltpu.CompilerParams(vmem_limit_bytes=56 << 20),
    )(*args)


def xor_send(value, axis, size, step):
    return lax.ppermute(value, axis, [(i, i ^ step) for i in range(size)])


def after(value, *needs):
    return lax.optimization_barrier((value, *needs))[0]


def lines(size):
    return [[low + 2 * i for i in range(size // 2)] for low in range(2)]


def gather_line(rows, size):
    return lax.all_gather(rows, "fsdp", axis=0, tiled=True, axis_index_groups=lines(size))


def gather_side(near, size, *needs):
    got = xor_send(after(near, *needs) if needs else near, "fsdp", size, 1)
    return jnp.concatenate([near, got], axis=0), got


def dot(left, right, dims=NN, out=f32):
    return lax.dot_general(left, right, dims, preferred_element_type=f32).astype(out)


class Summed:
    def __init__(self, left, right, size, *needs):
        self.size = size
        self.half = left.shape[1] // 2
        self.left, self.right = left, right
        self.sent = dot(left[:, self.half :], right, TN, bf16)
        self.got = xor_send(after(self.sent, *needs) if needs else self.sent, "fsdp", size, 1)

    def side(self, *needs):
        keep = dot(self.left[:, : self.half], after(self.right, *needs) if needs else self.right, TN)
        self.low = (keep + self.got.astype(f32)).astype(bf16)
        self.sum = lax.psum_scatter(self.low, "fsdp", scatter_dimension=0, tiled=True, axis_index_groups=lines(self.size))

    def total(self, ranks):
        return lax.all_to_all(self.sum.reshape(ranks, -1, self.sum.shape[1]), "rep", 0, 0)


def join_tokens(rows, size):
    half = size // 2

    def around(block):
        held = {0: block}
        step = half // 2
        while step:
            for j in list(held):
                held[j ^ step] = xor_send(held[j], "rep", size, step)
            step //= 2
        return jnp.concatenate([held[j] for j in range(half)], axis=0)

    beyond = xor_send(rows, "rep", size, half)
    return around(rows), around(beyond), beyond


def sum_tokens(far, near, size, *needs):
    half = size // 2

    def around(part):
        held = jnp.split(part, half, axis=0)
        step = 1
        while step < half:
            for j in range(0, half, 2 * step):
                held[j] = held[j] + xor_send(held[j + step].astype(bf16), "rep", size, step).astype(f32)
            step *= 2
        return held[0]

    beyond = around(far()).astype(bf16)
    part = near(beyond)
    if needs:
        beyond = after(beyond, *needs)
    got = xor_send(beyond, "rep", size, half)
    return around(part) + got.astype(f32), got


def rms(values):
    return lax.rsqrt(jnp.mean(values * values, axis=-1, keepdims=True) + 1e-06)


def norm_back(n, r, gain, dout):
    scaled = dout * gain
    return r * (scaled - n * jnp.mean(n * scaled, axis=-1, keepdims=True)), jnp.sum(dout * n, axis=0)


def make(F, R):
    both = ("fsdp", "rep")

    def on_device(tokens, segments, cotangent, gain_one, w_query, w_key, w_value, w_gate, w_beta, w_alpha, conv_q, conv_k,
                  conv_v, a_log, dt_bias, norm_gain, w_out, gain_two, w_ffgate, w_ffup, w_down):
        f = lax.axis_index("fsdp")
        r = lax.axis_index("rep")
        N = F * R
        rows_own, D = tokens.shape
        heads = a_log.shape[0]
        dk = w_query.shape[1] // heads
        dv = w_value.shape[1] // heads
        nh = heads // R
        dims = (nh, dk, dv)
        wq, wv = nh * dk, nh * dv
        hq, hv = wq // SPLIT, wv // SPLIT
        shard = D // N
        block = D // F
        ffq = w_ffgate.shape[1] // R
        tok = rows_own * R
        ns = tok // SEQ
        tiny = dv // N
        per = conv_v.shape[1] // shard

        low_bit = f & 1

        def swap(array, axis):
            half = array.shape[axis] // 2
            return jnp.concatenate(
                [lax.dynamic_slice_in_dim(array, (low_bit ^ j) * half, half, axis=axis) for j in range(2)], axis=axis)

        def mix(array, axis):
            at = [slice(None)] * array.ndim
            parts = []
            for bit in range(2):
                for i in range(F // 2):
                    at[axis] = slice((2 * i + bit) * block, (2 * i + bit + 1) * block)
                    parts.append(array[tuple(at)])
            return swap(jnp.concatenate(parts, axis=axis), axis)

        def unmix(array, axis):
            array = swap(array, axis)
            at = [slice(None)] * array.ndim
            parts = []
            for i in range(F // 2):
                for bit in range(2):
                    p = bit * (F // 2) + i
                    at[axis] = slice(p * block, (p + 1) * block)
                    parts.append(array[tuple(at)])
            return jnp.concatenate(parts, axis=axis)

        def quarter(arrays):
            return jnp.concatenate([a.reshape(shard, R, -1) for a in arrays], axis=2)

        def spread(packed):
            return lax.all_to_all(packed.transpose(1, 0, 2), "rep", 0, 0).reshape(R * shard, -1)

        extra = jnp.concatenate(
            [gain_one[:, None], gain_two[:, None], conv_q.T, conv_k.T,
             conv_v.reshape(4, shard, per).transpose(1, 0, 2).reshape(shard, 4 * per),
             jnp.pad(norm_gain, (0, shard - tiny))[:, None]], axis=1).T
        small = jnp.concatenate([w_beta.reshape(shard, R, nh), w_alpha.reshape(shard, R, nh)], axis=2)
        small = jnp.pad(small, ((0, 0), (0, 0), (0, 128 - 2 * nh)))

        def halves(array, width):
            parts = array.reshape(shard, R, SPLIT, width)
            return [parts[:, :, h] for h in range(SPLIT)]

        q_h, k_h, v_h, g_h = halves(w_query, hq), halves(w_key, hq), halves(w_value, hv), halves(w_gate, hv)
        own = mix(tokens, 1)
        part_a = spread(jnp.concatenate([q_h[0], k_h[0], v_h[0], g_h[0], small, q_h[1], k_h[1], v_h[1], g_h[1]], axis=2))
        w1 = 2 * hq + 2 * hv
        part_a = after(part_a, own)
        part_1, part_2 = part_a[:, : w1 + 128], part_a[:, w1 + 128 :]
        extra_all = lax.all_to_all(jnp.broadcast_to(after(extra, part_a)[None], (N, *extra.shape)), both, 0, 0)
        extra_all = extra_all.transpose(1, 0, 2).reshape(-1, D).astype(f32)
        line_1 = gather_line(part_1, F)
        every_near, every_far, every_got = join_tokens(own, R)
        every = jnp.concatenate([every_near, every_far], axis=0)
        ids_all = jnp.concatenate(join_tokens(segments[:, None], R)[:2], axis=0).reshape(ns, SEQ)
        part_r = spread(quarter([after(w_out.T, extra_all, every_got), w_ffgate, w_ffup, w_down.T]))
        part_b, part_g, part_u, part_d = (
            part_r[:, :wv], part_r[:, wv : wv + ffq], part_r[:, wv + ffq : wv + 2 * ffq], part_r[:, wv + 2 * ffq :])
        line_2 = gather_line(after(part_2, extra_all), F)
        wa1, side_1 = gather_side(line_1, F)
        cot = mix(cotangent, 1)
        cot_near, cot_far, unused = join_tokens(after(cot, line_1), R)
        line_b = gather_line(part_b, F)
        line_g = gather_line(part_g, F)
        line_u = gather_line(part_u, F)
        line_d = gather_line(part_d, F)

        gains = mix(extra_all[:2], 1)
        gain_first, gain_second = gains[0:1], gains[1:2]
        cq = lax.dynamic_slice_in_dim(extra_all[2:6], r * wq, wq, axis=1)
        ck = lax.dynamic_slice_in_dim(extra_all[6:10], r * wq, wq, axis=1)
        cv = extra_all[10 : 10 + 4 * per].reshape(4, per, D).transpose(0, 2, 1).reshape(4, D * per)
        cv = lax.dynamic_slice_in_dim(cv, r * wv, wv, axis=1)
        gain_out = extra_all[10 + 4 * per].reshape(N, shard)[:, :tiny].reshape(1, dv)
        taps = [jnp.concatenate([cq[:, h * hq : (h + 1) * hq], ck[:, h * hq : (h + 1) * hq], cv[:, h * hv : (h + 1) * hv]], axis=1)
                for h in range(SPLIT)]
        prm = jnp.stack([jnp.exp(lax.dynamic_slice_in_dim(a_log, r * nh, nh)), lax.dynamic_slice_in_dim(dt_bias, r * nh, nh)])
        prm = jnp.pad(prm, ((0, 6), (nh, 128 - 2 * nh)))
        place = jnp.arange(SEQ)
        same = (ids_all[:, :, None] == ids_all[:, None, :]) & (place[:, None] >= place[None, :])[None]
        pos = (jnp.sum(same.astype(f32), axis=2) - 1.0).reshape(tok, 1)

        every32 = every.astype(f32)
        normed_one = (every32 * rms(every32) * gain_first).astype(bf16)
        proj_1 = dot(after(normed_one, line_2, part_r), wa1)
        mixed, x_1, u_1, o_1 = mixer_fwd(proj_1, proj_1, pos, taps[0], gain_out, prm, dims, 0)
        wa2, side_2 = gather_side(line_2, F, side_1)
        proj_2 = dot(after(normed_one, mixed, line_b, cot_near, cot_far), wa2)
        mixed, x_2, u_2, o_2 = mixer_fwd(proj_2, proj_1, pos, taps[1], gain_out, prm, dims, 1, mixed)
        wb, side_b = gather_side(line_b, F, side_2)
        mixed = after(mixed, line_g)
        wg, side_g = gather_side(line_g, F, side_b)
        own32 = own.astype(f32)
        mid = tok // 2
        added, unused = sum_tokens(lambda: dot(mixed[mid:], wb, NT), lambda part: dot(after(mixed, part)[:mid], wb, NT), R)
        middle = own32 + added
        r2 = rms(middle)
        n2 = middle * r2
        normed_own = (n2 * gain_second).astype(bf16)
        wu, side_u = gather_side(line_u, F, side_g)
        two = join_tokens(after(normed_own, line_u), R)[:2]
        wd, side_d = gather_side(line_d, F, side_u)
        gates, ups, acts, sigs, hiddens = [], [], [], [], []
        for normed in two:
            gates.append(dot(normed, wg))
            ups.append(dot(normed, wu))
            sigs.append(jax.nn.sigmoid(gates[-1]))
            acts.append(gates[-1] * sigs[-1])
            hiddens.append((acts[-1] * ups[-1]).astype(bf16))
        hidden = jnp.concatenate(hiddens, axis=0)
        normed_two = jnp.concatenate(two, axis=0)
        cot_all = jnp.concatenate([cot_near, cot_far], axis=0)

        kept = {}

        def keep(name, value):
            kept[name] = value
            return value

        g_down = Summed(cot_all, hidden, F)
        dgates, dups = [None, None], [None, None]

        def back_two(t, *needs):
            dhidden = dot(after((cot_near, cot_far)[t], *needs), wd)
            dgates[t] = (dhidden * ups[t] * (sigs[t] * (1.0 + gates[t] * (1.0 - sigs[t])))).astype(bf16)
            dups[t] = (dhidden * acts[t]).astype(bf16)
            return dot(dgates[t], wg, NT) + dot(dups[t], wu, NT)

        dnormed_two, far_two = sum_tokens(lambda: back_two(1, g_down.sent), lambda part: keep("two", back_two(0, part)), R)
        g_down.side(kept["two"])
        g_gate = Summed(normed_two, after(jnp.concatenate(dgates, axis=0), g_down.low), F, g_down.got)
        dinner, dgain_second = norm_back(n2, r2, gain_second, after(dnormed_two, g_gate.sent))
        dmiddle = cot.astype(f32) + dinner
        dmiddle_own = dmiddle.astype(bf16)
        dlow = join_tokens(dmiddle_own, R)[:2]
        dm_near = dot(dlow[0], wb)
        args_2 = (proj_2, proj_1, pos, taps[1], gain_out, prm, x_2, u_2, o_2)
        args_1 = (proj_1, proj_1, pos, taps[0], gain_out, prm, x_1, u_1, o_1)
        dp_2, dba, dt_2, dg_2, dr_2 = mixer_bwd(*args_2, dm_near, dims, 1, 0)
        g_up = Summed(normed_two, after(jnp.concatenate(dups, axis=0), dba), F, g_gate.got)
        g_gate.side(g_up.sent)
        dp_1, dba_1, dt_1, dg_1, dr_1 = mixer_bwd(*args_1, after(dm_near, g_gate.low), dims, 0, 0, dba)
        t_down = g_down.total(R)
        g_out = Summed(jnp.concatenate(dlow, axis=0), after(mixed, dba_1), F, g_up.got)
        dm_far = dot(after(dlow[1], dba_1), wb)
        dp_2, dba, et_2, eg_2, er_2 = mixer_bwd(*args_2, after(dm_far, g_out.sent), dims, 1, 1, None, [dp_2, dba])
        g_up.side(dba)
        g_2 = Summed(normed_one, after(dp_2, g_up.low), F)
        t_gate = g_gate.total(R)
        dp_1, dba_1, et_1, eg_1, er_1 = mixer_bwd(
            *args_1, after(dm_far, g_2.sent, t_down), dims, 0, 1, dba, [dp_1, dba_1])
        g_1 = Summed(normed_one, dp_1, F, g_2.got)
        t_up = g_up.total(R)
        g_out.side(g_1.sent)
        g_2.side(g_out.low)

        def back_one(lo, hi, *needs):
            return dot(after(dp_1, *needs)[lo:hi], wa1, NT) + dot(after(dp_2, *needs)[lo:hi], wa2, NT)

        dnormed_one, far_one = sum_tokens(
            lambda: back_one(mid, tok, g_out.low, t_gate), lambda part: keep("one", back_one(0, mid, part, g_2.low)), R)
        added, unused = sum_tokens(
            lambda: dot(after(hiddens[1], kept["one"], t_up), wd, NT), lambda part: dot(after(hiddens[0], part), wd, NT), R)
        layer_out = (middle + added).astype(bf16)
        g_1.side(kept["one"])
        t_out = g_out.total(R)
        dprm = dr_1 + dr_2 + er_1 + er_2
        dgain_out = dg_1 + dg_2 + eg_1 + eg_2
        dtaps = [dt_1 + et_1, dt_2 + et_2]

        n1 = own32 * rms(own32)
        dfirst, dgain_first = norm_back(n1, rms(own32), gain_first, dnormed_one)
        grad_tokens = unmix(dmiddle + dfirst, 1)

        def wide(parts):
            return parts.astype(f32).transpose(1, 0, 2).reshape(shard, -1)

        def tall(parts):
            return parts.astype(f32).transpose(0, 2, 1).reshape(-1, shard)

        t_2 = g_2.total(R)
        t_1 = g_1.total(R)

        def joined(lo, width):
            return jnp.stack([t[:, :, lo : lo + width] for t in (t_1, t_2)], axis=2).astype(f32).transpose(1, 0, 2, 3).reshape(shard, -1)

        grad_query, grad_key = joined(0, hq), joined(hq, hq)
        grad_value, grad_gate_w = joined(2 * hq, hv), joined(2 * hq + hv, hv)
        grad_beta, grad_alpha = wide(t_1[:, :, w1 : w1 + nh]), wide(t_1[:, :, w1 + nh : w1 + 2 * nh])
        grad_down, grad_out = tall(t_down), tall(t_out)
        grad_gate, grad_up = wide(t_gate), wide(t_up)

        def placed(parts, total, width):
            part = jnp.concatenate(parts, axis=1)
            return lax.dynamic_update_slice(jnp.zeros((4, total), f32), part, (0, r * width))

        gq = placed([dtaps[h][:, :hq] for h in range(SPLIT)], R * wq, wq)
        gk = placed([dtaps[h][:, hq : 2 * hq] for h in range(SPLIT)], R * wq, wq)
        gv = placed([dtaps[h][:, 2 * hq :] for h in range(SPLIT)], R * wv, wv)
        heads_part = lax.dynamic_update_slice(jnp.zeros((2, heads), f32), dprm[:2, nh : 2 * nh], (0, r * nh)).reshape(1, -1)
        packed = jnp.concatenate([
            unmix(dgain_first[None], 1).reshape(N, -1),
            unmix(dgain_second[None], 1).reshape(N, -1),
            gq.reshape(4, N, -1).transpose(1, 0, 2).reshape(N, -1),
            gk.reshape(4, N, -1).transpose(1, 0, 2).reshape(N, -1),
            gv.reshape(4, N, -1).transpose(1, 0, 2).reshape(N, -1),
            dgain_out.reshape(N, tiny),
            jnp.broadcast_to(heads_part, (N, 2 * heads))], axis=1)
        summed = jnp.sum(lax.all_to_all(packed, both, 0, 0, tiled=True), axis=0)
        sizes = [shard, shard, 4 * shard, 4 * shard, 4 * shard * per, tiny, heads, heads]
        ends = [0]
        for size in sizes:
            ends.append(ends[-1] + size)
        pick = [summed[ends[i] : ends[i + 1]] for i in range(len(sizes))]
        return (
            unmix(layer_out, 1), grad_tokens, pick[0], grad_query, grad_key, grad_value, grad_gate_w, grad_beta, grad_alpha,
            pick[2].reshape(4, shard), pick[3].reshape(4, shard), pick[4].reshape(4, shard * per), pick[6], pick[7], pick[5],
            grad_out, pick[1], grad_gate, grad_up, grad_down)

    return on_device


def solution(mesh):
    rows, cols, flat = P(("fsdp", "rep"), None), P(None, ("fsdp", "rep")), P(("fsdp", "rep"))
    placed = (rows, flat, rows, flat, rows, rows, rows, rows, rows, rows, cols, cols, cols, P(), P(), flat, cols, flat, rows, rows, cols)
    made = (rows, rows, flat, rows, rows, rows, rows, rows, rows, cols, cols, cols, P(), P(), flat, cols, flat, rows, rows, cols)
    return jax.shard_map(
        make(mesh.shape["fsdp"], mesh.shape["rep"]), mesh=mesh, in_specs=placed, out_specs=made, check_vma=False)
```

```python
import functools

import jax
import jax.numpy as jnp
from jax import lax
from jax.experimental import pallas as pl
from jax.experimental.pallas import tpu as pltpu
from jax.sharding import PartitionSpec as P

SEQ = 256
SPLIT = 2
PAIR = 2
ROWS = PAIR * SEQ

f32 = jnp.float32
bf16 = jnp.bfloat16
NN = (((1,), (0,)), ((), ()))
NT = (((1,), (1,)), ((), ()))
TN = (((0,), (0,)), ((), ()))


def split(a):
    hi = a.astype(bf16)
    return hi, (a - hi.astype(f32)).astype(bf16)


def one(a, b, dims):
    return lax.dot_general(a.astype(bf16), b.astype(bf16), dims, preferred_element_type=f32)


def three(a, b, dims):
    ah, al = split(a)
    bh, bl = split(b)
    out = lax.dot_general(ah, bl, dims, preferred_element_type=f32)
    out = out + lax.dot_general(al, bh, dims, preferred_element_type=f32)
    return out + lax.dot_general(ah, bh, dims, preferred_element_type=f32)


def exact_left(a, b, dims):
    bh, bl = split(b)
    a = a.astype(bf16)
    return lax.dot_general(a, bh, dims, preferred_element_type=f32) + lax.dot_general(a, bl, dims, preferred_element_type=f32)


def exact_right(a, b, dims):
    ah, al = split(a)
    b = b.astype(bf16)
    return lax.dot_general(ah, b, dims, preferred_element_type=f32) + lax.dot_general(al, b, dims, preferred_element_type=f32)


def sigmoid(v):
    return 1.0 / (1.0 + jnp.exp(-v))


def conv(c, taps, pos):
    width = taps.shape[0]
    z = c * taps[width - 1 : width]
    for s in range(1, width):
        z = z + jnp.where(pos >= s, pltpu.roll(c, s, 0), 0.0) * taps[width - 1 - s : width - s]
    return z


def unit(c):
    r = lax.rsqrt(jnp.sum(c * c, axis=-1, keepdims=True) + 1e-6)
    return c * r, r


def inverses(n_list, iota_r, iota_c):
    size = n_list[0].shape[0]
    eye = (iota_r == iota_c).astype(f32)
    xs = None
    b = 1
    while b < size:
        mask = ((iota_r // (2 * b)) == (iota_c // (2 * b))) & ((iota_r // b) % 2 == 1) & ((iota_c // b) % 2 == 0)
        cs = [jnp.where(mask, n, 0.0) for n in n_list]
        if xs is None:
            xs = [eye - c for c in cs]
        else:
            low = [x.astype(bf16) for x in xs]
            t = [one(c, x, NN) for c, x in zip(cs, low)]
            xs = [x - one(y, z, NN) for x, y, z in zip(xs, low, t)]
        b *= 2
    left = [(eye - x) - three(n, x, NN) for n, x in zip(n_list, xs)]
    return [x + one(x, r, NN) for x, r in zip(xs, left)]


def rates(pba, prm, tri):
    beta = sigmoid(pba)
    rate = pba + prm[1:2]
    decay = -prm[0:1] * (jnp.maximum(rate, 0.0) + jnp.log1p(jnp.exp(-jnp.abs(rate))))
    return beta, rate, decay, exact_left(tri, decay, NN), exact_right(decay, tri, (((0,), (1,)), ((), ())))


class Sequence:
    def __init__(self, dims, half, refs, rows, iota_r, iota_c, tri):
        pq_ref, pk_ref, pv_ref, pg_ref, ba_ref, pos_ref, taps_ref, gain_ref, prm_ref = refs
        nh, dk, dv = dims
        hs = nh // SPLIT
        wq = hs * dk
        at = half * hs
        H = range(hs)
        self.rows = rows
        self.pos = pos_ref[rows, :]
        taps = taps_ref[...]
        self.taps = (taps[:, :wq], taps[:, wq : 2 * wq], taps[:, 2 * wq :])
        self.raw = (pq_ref[rows, :], pk_ref[rows, :], pv_ref[rows, :])
        self.beta, self.rate, self.decay, gcol, grow = rates(ba_ref[rows, :], prm_ref[...], tri)
        self.z = tuple(conv(c, t, self.pos) for c, t in zip(self.raw, self.taps))
        self.sig = tuple(sigmoid(z) for z in self.z)
        qc, kc, self.v = (z * g for z, g in zip(self.z, self.sig))
        live = (iota_c <= iota_r) & (iota_c >= iota_r - self.pos.astype(jnp.int32))
        self.bs = [self.beta[:, at + h : at + h + 1] for h in H]
        self.uq = [unit(qc[:, h * dk : (h + 1) * dk]) for h in H]
        self.uk = [unit(kc[:, h * dk : (h + 1) * dk]) for h in H]
        self.qs = [a * dk ** -0.5 for a, _ in self.uq]
        self.ks = [a for a, _ in self.uk]
        lane = nh + at
        self.ls = [
            jnp.where(live, jnp.exp(jnp.where(live, gcol[:, lane + h : lane + h + 1] - grow[lane + h : lane + h + 1, :], 0.0)), 0.0)
            for h in H]


def planes(n):
    iota_r = lax.broadcasted_iota(jnp.int32, (n, n), 0)
    iota_c = lax.broadcasted_iota(jnp.int32, (n, n), 1)
    return iota_r, iota_c, (iota_c <= iota_r).astype(f32), iota_c < iota_r


def fwd_kernel(dims, half, *refs):
    shared, (out_ref, x_ref, u_ref, o_ref) = refs[:9], refs[-4:]
    pg_ref, gain_ref = refs[3], refs[7]
    nh, dk, dv = dims
    hs = nh // SPLIT
    iota_r, iota_c, tri, strict = planes(SEQ)
    gain = gain_ref[...]
    seqs = [Sequence(dims, half, shared, slice(i * SEQ, (i + 1) * SEQ), iota_r, iota_c, tri) for i in range(out_ref.shape[0] // SEQ)]
    units = [(i, h) for i in range(len(seqs)) for h in range(hs)]
    ms = [three(seqs[i].ks[h], seqs[i].ks[h], NT) for i, h in units]
    ns = [jnp.where(strict, seqs[i].bs[h] * seqs[i].ls[h] * m, 0.0) for (i, h), m in zip(units, ms)]
    xs = inverses(ns, iota_r, iota_c)
    us = [three(x, seqs[i].bs[h] * seqs[i].v[:, h * dv : (h + 1) * dv], NN) for (i, h), x in zip(units, xs)]
    ps = [seqs[i].ls[h] * three(seqs[i].qs[h], seqs[i].ks[h], NT) for i, h in units]
    os = [three(p, u, NN) for p, u in zip(ps, us)]
    for (i, h), x, u, o in zip(units, xs, us, os):
        rows, sl = seqs[i].rows, slice(h * dv, (h + 1) * dv)
        x_ref[i * hs + h] = x
        u_ref[rows, sl] = u
        o_ref[rows, sl] = o
        r = lax.rsqrt(jnp.mean(o * o, axis=-1, keepdims=True) + 1e-5)
        pg = pg_ref[rows, sl]
        out_ref[rows, sl] = (o * r * gain * (pg * sigmoid(pg))).astype(bf16)


def bwd_kernel(dims, half, has_before, *refs):
    shared, (x_ref, u_ref, o_ref, dm_ref) = refs[:9], refs[9:13]
    dp_ref, dba_ref, dtaps_ref, dgain_ref, dprm_ref = refs[-5:]
    pg_ref, gain_ref, prm_ref = refs[3], refs[7], refs[8]
    nh, dk, dv = dims
    hs = nh // SPLIT
    wq, wv = hs * dk, hs * dv
    at = half * hs
    iota_r, iota_c, tri, strict = planes(SEQ)
    gain = gain_ref[...]
    prm = prm_ref[...]
    seqs = [Sequence(dims, half, shared, slice(i * SEQ, (i + 1) * SEQ), iota_r, iota_c, tri) for i in range(dm_ref.shape[0] // SEQ)]
    units = [(i, h) for i in range(len(seqs)) for h in range(hs)]
    dgain = jnp.zeros_like(gain)
    dos, us = [], []
    for i, h in units:
        rows, sl = seqs[i].rows, slice(h * dv, (h + 1) * dv)
        o = o_ref[rows, sl]
        pg = pg_ref[rows, sl]
        dm = dm_ref[rows, sl]
        r = lax.rsqrt(jnp.mean(o * o, axis=-1, keepdims=True) + 1e-5)
        nrm = o * r
        sg = sigmoid(pg)
        dp_ref[rows, 2 * wq + wv + h * dv : 2 * wq + wv + (h + 1) * dv] = (dm * nrm * gain * (sg * (1.0 + pg * (1.0 - sg)))).astype(bf16)
        dy = dm * (pg * sg)
        dgain = dgain + jnp.sum(dy * nrm, axis=0, keepdims=True)
        dn = dy * gain
        dos.append(r * (dn - nrm * jnp.mean(nrm * dn, axis=-1, keepdims=True)))
        us.append(u_ref[rows, sl])
    bm = [jnp.where(strict, seqs[i].ls[h] * three(seqs[i].ks[h], seqs[i].ks[h], NT), 0.0) for i, h in units]
    ps = [seqs[i].ls[h] * three(seqs[i].qs[h], seqs[i].ks[h], NT) for i, h in units]
    dps = [three(do, u, NT) for do, u in zip(dos, us)]
    dus = [three(p, do, TN) for p, do in zip(ps, dos)]
    dws = [three(x_ref[i * hs + h], du, TN) for (i, h), du in zip(units, dus)]
    das = [-three(dw, u, NT) for dw, u in zip(dws, us)]

    @pl.when(pl.program_id(0) == 0)
    def _():
        dtaps_ref[...] = jnp.zeros_like(dtaps_ref)
        dgain_ref[...] = jnp.zeros_like(dgain_ref)
        dprm_ref[...] = jnp.zeros_like(dprm_ref)

    dgain_ref[...] += dgain
    lane = lax.broadcasted_iota(jnp.int32, (SEQ, 128), 1)
    ones = jnp.ones((SEQ, 128), f32)
    sc = dk ** -0.5
    for i, q in enumerate(seqs):
        rows, pos = q.rows, q.pos
        dbeta = jnp.zeros((SEQ, 128), f32)
        dlog = jnp.zeros((SEQ, 128), f32)
        dz = ([], [], [])
        for h in range(hs):
            n = i * hs + h
            vh = q.v[:, h * dv : (h + 1) * dv]
            ab = das[n] * bm[n]
            dbeta = jnp.where(lane == at + h, jnp.sum(dws[n] * vh, axis=-1, keepdims=True) + jnp.sum(ab, axis=-1, keepdims=True), dbeta)
            e = q.bs[h] * ab + dps[n] * ps[n]
            dlog = jnp.where(lane == nh + at + h, jnp.sum(e, axis=-1, keepdims=True) - exact_right(e, ones, TN), dlog)
            ds = dps[n] * q.ls[h]
            dmm = jnp.where(strict, q.bs[h] * das[n] * q.ls[h], 0.0)
            dq = sc * three(ds, q.ks[h], NN)
            dkh = three(ds, q.qs[h], TN) + three(dmm, q.ks[h], NN) + three(dmm, q.ks[h], TN)
            qh, rq = q.uq[h]
            kh, rk = q.uk[h]
            dz[0].append(rq * (dq - qh * jnp.sum(qh * dq, axis=-1, keepdims=True)))
            dz[1].append(rk * (dkh - kh * jnp.sum(kh * dkh, axis=-1, keepdims=True)))
            dz[2].append(q.bs[h] * dws[n])
        ddecay = exact_left(tri, dlog, TN)
        drate = -prm[0:1] * ddecay * sigmoid(q.rate)
        dba = dbeta * q.beta * (1.0 - q.beta) + drate
        if has_before:
            dba = dba + refs[13][rows, :]
            dp_ref[rows, 2 * wq + 2 * wv :] = dba.astype(bf16)
        dba_ref[rows, :] = dba
        dprm_ref[0:1, :] += jnp.sum(ddecay * q.decay, axis=0, keepdims=True)
        dprm_ref[1:2, :] += jnp.sum(drate, axis=0, keepdims=True)
        to = 0
        for parts, z, sg, c, tap in zip(dz, q.z, q.sig, q.raw, q.taps):
            d = jnp.concatenate(parts, axis=1) * (sg * (1.0 + z * (1.0 - sg)))
            width = tap.shape[0]
            w = c.shape[1]
            dc = d * tap[width - 1 : width]
            dtaps_ref[width - 1 : width, to : to + w] += jnp.sum(d * c, axis=0, keepdims=True)
            for s in range(1, width):
                m = jnp.where(pos >= s, d, 0.0)
                dc = dc + pltpu.roll(m, SEQ - s, 0) * tap[width - 1 - s : width - s]
                dtaps_ref[width - 1 - s : width - s, to : to + w] += jnp.sum(m * pltpu.roll(c, s, 0), axis=0, keepdims=True)
            dp_ref[rows, to : to + w] = dc.astype(bf16)
            to += w


def shared_specs(dims, off=0):
    nh, dk, dv = dims
    wq, wv = nh // SPLIT * dk, nh // SPLIT * dv
    at = (2 * wq) // wv
    small = (2 * wq + 2 * wv) // 128
    return [
        pl.BlockSpec((ROWS, wq), lambda i: (i + off, 0)),
        pl.BlockSpec((ROWS, wq), lambda i: (i + off, 1)),
        pl.BlockSpec((ROWS, wv), lambda i: (i + off, at)),
        pl.BlockSpec((ROWS, wv), lambda i: (i + off, at + 1)),
        pl.BlockSpec((ROWS, 128), lambda i: (i + off, small)),
        pl.BlockSpec((ROWS, 1), lambda i: (i + off, 0)),
        pl.BlockSpec((4, 2 * wq + wv), lambda i: (0, 0)),
        pl.BlockSpec((1, dv), lambda i: (0, 0)),
        pl.BlockSpec((8, 128), lambda i: (0, 0)),
    ]


def cost(us):
    return pl.CostEstimate(flops=int(us * 1.1e9), bytes_accessed=int(us * 1e6), transcendentals=0)


def mixer_fwd(proj, first, pos, taps, gain, prm, dims, half, mixed=None):
    tok = pos.shape[0]
    nh, dk, dv = dims
    hs = nh // SPLIT
    ns = tok // SEQ
    wv = hs * dv
    row = pl.BlockSpec((ROWS, wv), lambda i: (i, 0))
    specs = shared_specs(dims)
    args = [proj, proj, proj, proj, first, pos, taps, gain, prm]
    alias = {}
    if mixed is not None:
        alias = {len(args): 0}
        args.append(mixed)
        specs.append(pl.BlockSpec(memory_space=pl.ANY))
    return pl.pallas_call(
        functools.partial(fwd_kernel, dims, half),
        grid=(ns // PAIR,),
        in_specs=specs,
        out_specs=[
            pl.BlockSpec((ROWS, wv), lambda i: (i, half)),
            pl.BlockSpec((PAIR * hs, SEQ, SEQ), lambda i: (i, 0, 0)),
            row,
            row,
        ],
        out_shape=[
            jax.ShapeDtypeStruct((tok, nh * dv), bf16),
            jax.ShapeDtypeStruct((ns * hs, SEQ, SEQ), f32),
            jax.ShapeDtypeStruct((tok, wv), f32),
            jax.ShapeDtypeStruct((tok, wv), f32),
        ],
        input_output_aliases=alias,
        cost_estimate=cost(4),
        compiler_params=pltpu.CompilerParams(vmem_limit_bytes=48 << 20),
    )(*args)


def mixer_bwd(proj, first, pos, taps, gain, prm, x, u, o, dm, dims, half, part, before=None, filled=None):
    tok = pos.shape[0]
    nh, dk, dv = dims
    hs = nh // SPLIT
    ns = tok // SEQ
    wq, wv = hs * dk, hs * dv
    steps = dm.shape[0] // ROWS
    off = part * steps
    row = pl.BlockSpec((ROWS, wv), lambda i: (i + off, 0))
    lanes = pl.BlockSpec((ROWS, 128), lambda i: (i + off, 0))
    specs = shared_specs(dims, off) + [
        pl.BlockSpec((PAIR * hs, SEQ, SEQ), lambda i: (i + off, 0, 0)), row, row, pl.BlockSpec((ROWS, wv), lambda i: (i, half))]
    args = [proj, proj, proj, proj, first, pos, taps, gain, prm, x, u, o, dm]
    width = 2 * wq + 2 * wv
    if before is not None:
        args.append(before)
        specs.append(lanes)
        width += 128
    alias = {}
    if filled is not None:
        alias = {len(args): 0, len(args) + 1: 1}
        args += filled
        specs += [pl.BlockSpec(memory_space=pl.ANY)] * 2
    return pl.pallas_call(
        functools.partial(bwd_kernel, dims, half, before is not None),
        grid=(steps,),
        in_specs=specs,
        out_specs=[
            pl.BlockSpec((ROWS, width), lambda i: (i + off, 0)),
            lanes,
            pl.BlockSpec((4, 2 * wq + wv), lambda i: (0, 0)),
            pl.BlockSpec((1, dv), lambda i: (0, 0)),
            pl.BlockSpec((8, 128), lambda i: (0, 0)),
        ],
        out_shape=[
            jax.ShapeDtypeStruct((tok, width), bf16),
            jax.ShapeDtypeStruct((tok, 128), f32),
            jax.ShapeDtypeStruct((4, 2 * wq + wv), f32),
            jax.ShapeDtypeStruct((1, dv), f32),
            jax.ShapeDtypeStruct((8, 128), f32),
        ],
        input_output_aliases=alias,
        cost_estimate=cost(26),
        compiler_params=pltpu.CompilerParams(vmem_limit_bytes=56 << 20),
    )(*args)


def xor_send(value, axis, size, step):
    return lax.ppermute(value, axis, [(i, i ^ step) for i in range(size)])


def after(value, *needs):
    return lax.optimization_barrier((value, *needs))[0]


def lines(size):
    return [[low + 2 * i for i in range(size // 2)] for low in range(2)]


def gather_line(rows, size):
    return lax.all_gather(rows, "fsdp", axis=0, tiled=True, axis_index_groups=lines(size))


def gather_side(near, size, *needs):
    got = xor_send(after(near, *needs) if needs else near, "fsdp", size, 1)
    return jnp.concatenate([near, got], axis=0), got


def gather_side_first(rows, size, *needs):
    got = xor_send(after(rows, *needs), "fsdp", size, 1)
    full = gather_line(jnp.concatenate([rows, got], axis=0), size)
    width = rows.shape[1]
    return full.reshape(size // 2, 2, -1, width).swapaxes(0, 1).reshape(-1, width), full, got


def dot(left, right, dims=NN, out=f32):
    return lax.dot_general(left, right, dims, preferred_element_type=f32).astype(out)


class Summed:
    def __init__(self, left, right, size, *needs):
        self.size = size
        self.half = left.shape[1] // 2
        self.left, self.right = left, right
        self.sent = dot(left[:, self.half :], right, TN, bf16)
        self.got = xor_send(after(self.sent, *needs) if needs else self.sent, "fsdp", size, 1)

    def side(self, *needs):
        keep = dot(self.left[:, : self.half], after(self.right, *needs) if needs else self.right, TN)
        self.low = (keep + self.got.astype(f32)).astype(bf16)
        self.sum = lax.psum_scatter(self.low, "fsdp", scatter_dimension=0, tiled=True, axis_index_groups=lines(self.size))

    def total(self, ranks):
        return lax.all_to_all(self.sum.reshape(ranks, -1, self.sum.shape[1]), "rep", 0, 0)


def join_tokens(rows, size):
    half = size // 2

    def around(block):
        held = {0: block}
        step = half // 2
        while step:
            for j in list(held):
                held[j ^ step] = xor_send(held[j], "rep", size, step)
            step //= 2
        return jnp.concatenate([held[j] for j in range(half)], axis=0)

    beyond = xor_send(rows, "rep", size, half)
    return around(rows), around(beyond), beyond


def sum_tokens(far, near, size, *needs):
    half = size // 2

    def around(part):
        held = jnp.split(part, half, axis=0)
        step = 1
        while step < half:
            for j in range(0, half, 2 * step):
                held[j] = held[j] + xor_send(held[j + step].astype(bf16), "rep", size, step).astype(f32)
            step *= 2
        return held[0]

    beyond = around(far()).astype(bf16)
    part = near(beyond)
    if needs:
        beyond = after(beyond, *needs)
    got = xor_send(beyond, "rep", size, half)
    return around(part) + got.astype(f32), got


def rms(values):
    return lax.rsqrt(jnp.mean(values * values, axis=-1, keepdims=True) + 1e-06)


def norm_back(n, r, gain, dout):
    scaled = dout * gain
    return r * (scaled - n * jnp.mean(n * scaled, axis=-1, keepdims=True)), jnp.sum(dout * n, axis=0)


def make(F, R):
    both = ("fsdp", "rep")

    def on_device(tokens, segments, cotangent, gain_one, w_query, w_key, w_value, w_gate, w_beta, w_alpha, conv_q, conv_k,
                  conv_v, a_log, dt_bias, norm_gain, w_out, gain_two, w_ffgate, w_ffup, w_down):
        f = lax.axis_index("fsdp")
        r = lax.axis_index("rep")
        N = F * R
        rows_own, D = tokens.shape
        heads = a_log.shape[0]
        dk = w_query.shape[1] // heads
        dv = w_value.shape[1] // heads
        nh = heads // R
        dims = (nh, dk, dv)
        wq, wv = nh * dk, nh * dv
        hq, hv = wq // SPLIT, wv // SPLIT
        shard = D // N
        block = D // F
        ffq = w_ffgate.shape[1] // R
        tok = rows_own * R
        ns = tok // SEQ
        tiny = dv // N
        per = conv_v.shape[1] // shard

        low_bit = f & 1

        def swap(array, axis):
            half = array.shape[axis] // 2
            return jnp.concatenate(
                [lax.dynamic_slice_in_dim(array, (low_bit ^ j) * half, half, axis=axis) for j in range(2)], axis=axis)

        def mix(array, axis):
            at = [slice(None)] * array.ndim
            parts = []
            for bit in range(2):
                for i in range(F // 2):
                    at[axis] = slice((2 * i + bit) * block, (2 * i + bit + 1) * block)
                    parts.append(array[tuple(at)])
            return swap(jnp.concatenate(parts, axis=axis), axis)

        def unmix(array, axis):
            array = swap(array, axis)
            at = [slice(None)] * array.ndim
            parts = []
            for i in range(F // 2):
                for bit in range(2):
                    p = bit * (F // 2) + i
                    at[axis] = slice(p * block, (p + 1) * block)
                    parts.append(array[tuple(at)])
            return jnp.concatenate(parts, axis=axis)

        def quarter(arrays):
            return jnp.concatenate([a.reshape(shard, R, -1) for a in arrays], axis=2)

        def spread(packed):
            return lax.all_to_all(packed.transpose(1, 0, 2), "rep", 0, 0).reshape(R * shard, -1)

        extra = jnp.concatenate(
            [gain_one[:, None], gain_two[:, None], conv_q.T, conv_k.T,
             conv_v.reshape(4, shard, per).transpose(1, 0, 2).reshape(shard, 4 * per),
             jnp.pad(norm_gain, (0, shard - tiny))[:, None]], axis=1).T
        small = jnp.concatenate([w_beta.reshape(shard, R, nh), w_alpha.reshape(shard, R, nh)], axis=2)
        small = jnp.pad(small, ((0, 0), (0, 0), (0, 128 - 2 * nh)))

        def halves(array, width):
            parts = array.reshape(shard, R, SPLIT, width)
            return [parts[:, :, h] for h in range(SPLIT)]

        q_h, k_h, v_h, g_h = halves(w_query, hq), halves(w_key, hq), halves(w_value, hv), halves(w_gate, hv)
        own = mix(tokens, 1)
        part_a = spread(jnp.concatenate([q_h[0], k_h[0], v_h[0], g_h[0], small, q_h[1], k_h[1], v_h[1], g_h[1]], axis=2))
        w1 = 2 * hq + 2 * hv
        part_a = after(part_a, own)
        part_1, part_2 = part_a[:, : w1 + 128], part_a[:, w1 + 128 :]
        extra_all = lax.all_to_all(jnp.broadcast_to(after(extra, part_a)[None], (N, *extra.shape)), both, 0, 0)
        extra_all = extra_all.transpose(1, 0, 2).reshape(-1, D).astype(f32)
        line_1 = gather_line(part_1, F)
        every_near, every_far, every_got = join_tokens(own, R)
        every = jnp.concatenate([every_near, every_far], axis=0)
        ids_all = jnp.concatenate(join_tokens(segments[:, None], R)[:2], axis=0).reshape(ns, SEQ)
        part_r = spread(quarter([after(w_out.T, extra_all, every_got, line_1), w_ffgate, w_ffup, w_down.T]))
        part_b, part_g, part_u, part_d = (
            part_r[:, :wv], part_r[:, wv : wv + ffq], part_r[:, wv + ffq : wv + 2 * ffq], part_r[:, wv + 2 * ffq :])
        line_2 = gather_line(after(part_2, extra_all), F)
        wa1, side_1 = gather_side(line_1, F)
        cot = mix(cotangent, 1)
        cot_near, cot_far, unused = join_tokens(after(cot, side_1), R)
        line_b = gather_line(part_b, F)
        line_g = gather_line(part_g, F)
        line_u = gather_line(part_u, F)

        gains = mix(extra_all[:2], 1)
        gain_first, gain_second = gains[0:1], gains[1:2]
        cq = lax.dynamic_slice_in_dim(extra_all[2:6], r * wq, wq, axis=1)
        ck = lax.dynamic_slice_in_dim(extra_all[6:10], r * wq, wq, axis=1)
        cv = extra_all[10 : 10 + 4 * per].reshape(4, per, D).transpose(0, 2, 1).reshape(4, D * per)
        cv = lax.dynamic_slice_in_dim(cv, r * wv, wv, axis=1)
        gain_out = extra_all[10 + 4 * per].reshape(N, shard)[:, :tiny].reshape(1, dv)
        taps = [jnp.concatenate([cq[:, h * hq : (h + 1) * hq], ck[:, h * hq : (h + 1) * hq], cv[:, h * hv : (h + 1) * hv]], axis=1)
                for h in range(SPLIT)]
        prm = jnp.stack([jnp.exp(lax.dynamic_slice_in_dim(a_log, r * nh, nh)), lax.dynamic_slice_in_dim(dt_bias, r * nh, nh)])
        prm = jnp.pad(prm, ((0, 6), (nh, 128 - 2 * nh)))
        place = jnp.arange(SEQ)
        same = (ids_all[:, :, None] == ids_all[:, None, :]) & (place[:, None] >= place[None, :])[None]
        pos = (jnp.sum(same.astype(f32), axis=2) - 1.0).reshape(tok, 1)

        every32 = every.astype(f32)
        normed_one = (every32 * rms(every32) * gain_first).astype(bf16)
        proj_1 = dot(after(normed_one, line_2, part_r), wa1)
        mixed, x_1, u_1, o_1 = mixer_fwd(proj_1, proj_1, pos, taps[0], gain_out, prm, dims, 0)
        wa2, side_2 = gather_side(line_2, F, side_1)
        proj_2 = dot(after(normed_one, mixed, line_b, cot_near, cot_far), wa2)
        mixed, x_2, u_2, o_2 = mixer_fwd(proj_2, proj_1, pos, taps[1], gain_out, prm, dims, 1, mixed)
        wd, line_d, got_d = gather_side_first(part_d, F, side_2)
        wb, side_b = gather_side(line_b, F, side_2)
        mixed = after(mixed, line_g, got_d)
        wg, side_g = gather_side(line_g, F, side_b)
        own32 = own.astype(f32)
        mid = tok // 2
        added, unused = sum_tokens(lambda: dot(mixed[mid:], wb, NT), lambda part: dot(after(mixed, part)[:mid], wb, NT), R)
        middle = own32 + added
        r2 = rms(middle)
        n2 = middle * r2
        normed_own = (n2 * gain_second).astype(bf16)
        side_u = xor_send(after(line_u, side_g), "fsdp", F, 1)
        two = join_tokens(after(normed_own, line_u, side_g), R)[:2]
        gates, ups, acts, sigs, hiddens = [], [], [], [], []
        for normed in (two[0], after(two[1], line_d)):
            gates.append(dot(normed, wg))
            if not ups:
                wu = jnp.concatenate([line_u, after(side_u, gates[0])], axis=0)
            ups.append(dot(normed, wu))
            sigs.append(jax.nn.sigmoid(gates[-1]))
            acts.append(gates[-1] * sigs[-1])
            hiddens.append((acts[-1] * ups[-1]).astype(bf16))
        hidden = jnp.concatenate(hiddens, axis=0)
        normed_two = jnp.concatenate(two, axis=0)
        cot_all = jnp.concatenate([cot_near, cot_far], axis=0)

        kept = {}

        def keep(name, value):
            kept[name] = value
            return value

        g_down = Summed(cot_all, hidden, F)
        dgates, dups = [None, None], [None, None]

        def back_two(t, *needs):
            dhidden = dot(after((cot_near, cot_far)[t], *needs), wd)
            dgates[t] = (dhidden * ups[t] * (sigs[t] * (1.0 + gates[t] * (1.0 - sigs[t])))).astype(bf16)
            dups[t] = (dhidden * acts[t]).astype(bf16)
            ready = dgates[t] if t else after(dgates[t], g_down.got)
            return dot(ready, wg, NT) + dot(dups[t], wu, NT)

        dnormed_two, far_two = sum_tokens(lambda: back_two(1, g_down.sent), lambda part: keep("two", back_two(0, part)), R)
        g_down.side(kept["two"])
        g_gate = Summed(normed_two, after(jnp.concatenate(dgates, axis=0), g_down.low), F, g_down.got)
        dinner, dgain_second = norm_back(n2, r2, gain_second, after(dnormed_two, g_gate.sent))
        dmiddle = cot.astype(f32) + dinner
        dmiddle_own = dmiddle.astype(bf16)
        dlow = join_tokens(dmiddle_own, R)[:2]
        dm_near = dot(dlow[0], wb)
        args_2 = (proj_2, proj_1, pos, taps[1], gain_out, prm, x_2, u_2, o_2)
        args_1 = (proj_1, proj_1, pos, taps[0], gain_out, prm, x_1, u_1, o_1)
        dp_2, dba, dt_2, dg_2, dr_2 = mixer_bwd(*args_2, dm_near, dims, 1, 0)
        g_up = Summed(normed_two, after(jnp.concatenate(dups, axis=0), dba), F, g_gate.got)
        g_gate.side(g_up.sent)
        dp_1, dba_1, dt_1, dg_1, dr_1 = mixer_bwd(*args_1, after(dm_near, g_gate.low), dims, 0, 0, dba)
        t_down = g_down.total(R)
        g_out = Summed(jnp.concatenate(dlow, axis=0), after(mixed, dba_1), F)
        dm_far = dot(after(dlow[1], dba_1), wb)
        dp_2, dba, et_2, eg_2, er_2 = mixer_bwd(*args_2, after(dm_far, g_out.sent), dims, 1, 1, None, [dp_2, dba])
        g_up.side(dba)
        g_2 = Summed(normed_one, after(dp_2, g_up.low), F)
        t_gate = g_gate.total(R)
        dp_1, dba_1, et_1, eg_1, er_1 = mixer_bwd(
            *args_1, after(dm_far, g_2.sent, t_down), dims, 0, 1, dba, [dp_1, dba_1])
        g_out.side(dp_1)
        g_1 = Summed(normed_one, after(dp_1, g_out.low), F)
        t_up = g_up.total(R)

        def back_one(lo, hi, *needs):
            return dot(after(dp_1, *needs)[lo:hi], wa1, NT) + dot(after(dp_2, *needs)[lo:hi], wa2, NT)

        g_2.side(g_1.sent)

        def near_one(part):
            g_1.side(part)
            kept["out"], unused = sum_tokens(
                lambda: dot(after(hiddens[1], g_1.low), wd, NT), lambda held: keep("last", dot(after(hiddens[0], held), wd, NT)), R)
            return back_one(0, mid, kept["last"], t_out)

        t_out = g_out.total(R)
        dnormed_one, far_one = sum_tokens(lambda: back_one(mid, tok, g_2.low, t_gate, t_up), near_one, R)
        added = kept["out"]
        layer_out = (middle + added).astype(bf16)
        dprm = dr_1 + dr_2 + er_1 + er_2
        dgain_out = dg_1 + dg_2 + eg_1 + eg_2
        dtaps = [dt_1 + et_1, dt_2 + et_2]

        n1 = own32 * rms(own32)
        dfirst, dgain_first = norm_back(n1, rms(own32), gain_first, dnormed_one)
        grad_tokens = unmix(dmiddle + dfirst, 1)

        def wide(parts):
            return parts.astype(f32).transpose(1, 0, 2).reshape(shard, -1)

        def tall(parts):
            return parts.astype(f32).transpose(0, 2, 1).reshape(-1, shard)

        t_2 = g_2.total(R)
        t_1 = g_1.total(R)

        def joined(lo, width):
            return jnp.stack([t[:, :, lo : lo + width] for t in (t_1, t_2)], axis=2).astype(f32).transpose(1, 0, 2, 3).reshape(shard, -1)

        grad_query, grad_key = joined(0, hq), joined(hq, hq)
        grad_value, grad_gate_w = joined(2 * hq, hv), joined(2 * hq + hv, hv)
        grad_beta, grad_alpha = wide(t_1[:, :, w1 : w1 + nh]), wide(t_1[:, :, w1 + nh : w1 + 2 * nh])
        grad_down, grad_out = tall(t_down), tall(t_out)
        grad_gate, grad_up = wide(t_gate), wide(t_up)

        def placed(parts, total, width):
            part = jnp.concatenate(parts, axis=1)
            return lax.dynamic_update_slice(jnp.zeros((4, total), f32), part, (0, r * width))

        gq = placed([dtaps[h][:, :hq] for h in range(SPLIT)], R * wq, wq)
        gk = placed([dtaps[h][:, hq : 2 * hq] for h in range(SPLIT)], R * wq, wq)
        gv = placed([dtaps[h][:, 2 * hq :] for h in range(SPLIT)], R * wv, wv)
        heads_part = lax.dynamic_update_slice(jnp.zeros((2, heads), f32), dprm[:2, nh : 2 * nh], (0, r * nh)).reshape(1, -1)
        packed = jnp.concatenate([
            unmix(dgain_first[None], 1).reshape(N, -1),
            unmix(dgain_second[None], 1).reshape(N, -1),
            gq.reshape(4, N, -1).transpose(1, 0, 2).reshape(N, -1),
            gk.reshape(4, N, -1).transpose(1, 0, 2).reshape(N, -1),
            gv.reshape(4, N, -1).transpose(1, 0, 2).reshape(N, -1),
            dgain_out.reshape(N, tiny),
            jnp.broadcast_to(heads_part, (N, 2 * heads))], axis=1)
        summed = jnp.sum(lax.all_to_all(packed, both, 0, 0, tiled=True), axis=0)
        sizes = [shard, shard, 4 * shard, 4 * shard, 4 * shard * per, tiny, heads, heads]
        ends = [0]
        for size in sizes:
            ends.append(ends[-1] + size)
        pick = [summed[ends[i] : ends[i + 1]] for i in range(len(sizes))]
        return (
            unmix(layer_out, 1), grad_tokens, pick[0], grad_query, grad_key, grad_value, grad_gate_w, grad_beta, grad_alpha,
            pick[2].reshape(4, shard), pick[3].reshape(4, shard), pick[4].reshape(4, shard * per), pick[6], pick[7], pick[5],
            grad_out, pick[1], grad_gate, grad_up, grad_down)

    return on_device


def solution(mesh):
    rows, cols, flat = P(("fsdp", "rep"), None), P(None, ("fsdp", "rep")), P(("fsdp", "rep"))
    placed = (rows, flat, rows, flat, rows, rows, rows, rows, rows, rows, cols, cols, cols, P(), P(), flat, cols, flat, rows, rows, cols)
    made = (rows, rows, flat, rows, rows, rows, rows, rows, rows, cols, cols, cols, P(), P(), flat, cols, flat, rows, rows, cols)
    return jax.shard_map(
        make(mesh.shape["fsdp"], mesh.shape["rep"]), mesh=mesh, in_specs=placed, out_specs=made, check_vma=False)
```

```python
import functools

import jax
import jax.numpy as jnp
from jax import lax
from jax.experimental import pallas as pl
from jax.experimental.pallas import tpu as pltpu
from jax.sharding import PartitionSpec as P

SEQ = 256
SPLIT = 2
PAIR = 2
ROWS = PAIR * SEQ

f32 = jnp.float32
bf16 = jnp.bfloat16
NN = (((1,), (0,)), ((), ()))
NT = (((1,), (1,)), ((), ()))
TN = (((0,), (0,)), ((), ()))


def split(a):
    hi = a.astype(bf16)
    return hi, (a - hi.astype(f32)).astype(bf16)


def one(a, b, dims):
    return lax.dot_general(a.astype(bf16), b.astype(bf16), dims, preferred_element_type=f32)


def three(a, b, dims):
    ah, al = split(a)
    bh, bl = split(b)
    out = lax.dot_general(ah, bl, dims, preferred_element_type=f32)
    out = out + lax.dot_general(al, bh, dims, preferred_element_type=f32)
    return out + lax.dot_general(ah, bh, dims, preferred_element_type=f32)


def exact_left(a, b, dims):
    bh, bl = split(b)
    a = a.astype(bf16)
    return lax.dot_general(a, bh, dims, preferred_element_type=f32) + lax.dot_general(a, bl, dims, preferred_element_type=f32)


def exact_right(a, b, dims):
    ah, al = split(a)
    b = b.astype(bf16)
    return lax.dot_general(ah, b, dims, preferred_element_type=f32) + lax.dot_general(al, b, dims, preferred_element_type=f32)


def sigmoid(v):
    return 1.0 / (1.0 + jnp.exp(-v))


def conv(c, taps, pos):
    width = taps.shape[0]
    z = c * taps[width - 1 : width]
    for s in range(1, width):
        z = z + jnp.where(pos >= s, pltpu.roll(c, s, 0), 0.0) * taps[width - 1 - s : width - s]
    return z


def unit(c):
    r = lax.rsqrt(jnp.sum(c * c, axis=-1, keepdims=True) + 1e-6)
    return c * r, r


def inverses(n_list, iota_r, iota_c):
    size = n_list[0].shape[0]
    eye = (iota_r == iota_c).astype(f32)
    xs = None
    b = 1
    while b < size:
        mask = ((iota_r // (2 * b)) == (iota_c // (2 * b))) & ((iota_r // b) % 2 == 1) & ((iota_c // b) % 2 == 0)
        cs = [jnp.where(mask, n, 0.0) for n in n_list]
        if xs is None:
            xs = [eye - c for c in cs]
        else:
            low = [x.astype(bf16) for x in xs]
            t = [one(c, x, NN) for c, x in zip(cs, low)]
            xs = [x - one(y, z, NN) for x, y, z in zip(xs, low, t)]
        b *= 2
    left = [(eye - x) - three(n, x, NN) for n, x in zip(n_list, xs)]
    return [x + one(x, r, NN) for x, r in zip(xs, left)]


def rates(pba, prm, tri):
    beta = sigmoid(pba)
    rate = pba + prm[1:2]
    decay = -prm[0:1] * (jnp.maximum(rate, 0.0) + jnp.log1p(jnp.exp(-jnp.abs(rate))))
    return beta, rate, decay, exact_left(tri, decay, NN), exact_right(decay, tri, (((0,), (1,)), ((), ())))


class Sequence:
    def __init__(self, dims, half, refs, rows, iota_r, iota_c, tri):
        pq_ref, pk_ref, pv_ref, pg_ref, ba_ref, pos_ref, taps_ref, gain_ref, prm_ref = refs
        nh, dk, dv = dims
        hs = nh // SPLIT
        wq = hs * dk
        at = half * hs
        H = range(hs)
        self.rows = rows
        self.pos = pos_ref[rows, :]
        taps = taps_ref[...]
        self.taps = (taps[:, :wq], taps[:, wq : 2 * wq], taps[:, 2 * wq :])
        self.raw = (pq_ref[rows, :], pk_ref[rows, :], pv_ref[rows, :])
        self.beta, self.rate, self.decay, gcol, grow = rates(ba_ref[rows, :], prm_ref[...], tri)
        self.z = tuple(conv(c, t, self.pos) for c, t in zip(self.raw, self.taps))
        self.sig = tuple(sigmoid(z) for z in self.z)
        qc, kc, self.v = (z * g for z, g in zip(self.z, self.sig))
        live = (iota_c <= iota_r) & (iota_c >= iota_r - self.pos.astype(jnp.int32))
        self.bs = [self.beta[:, at + h : at + h + 1] for h in H]
        self.uq = [unit(qc[:, h * dk : (h + 1) * dk]) for h in H]
        self.uk = [unit(kc[:, h * dk : (h + 1) * dk]) for h in H]
        self.qs = [a * dk ** -0.5 for a, _ in self.uq]
        self.ks = [a for a, _ in self.uk]
        lane = nh + at
        self.ls = [
            jnp.where(live, jnp.exp(jnp.where(live, gcol[:, lane + h : lane + h + 1] - grow[lane + h : lane + h + 1, :], 0.0)), 0.0)
            for h in H]


def planes(n):
    iota_r = lax.broadcasted_iota(jnp.int32, (n, n), 0)
    iota_c = lax.broadcasted_iota(jnp.int32, (n, n), 1)
    return iota_r, iota_c, (iota_c <= iota_r).astype(f32), iota_c < iota_r


def fwd_kernel(dims, half, *refs):
    shared, (out_ref, x_ref, u_ref, o_ref) = refs[:9], refs[-4:]
    pg_ref, gain_ref = refs[3], refs[7]
    nh, dk, dv = dims
    hs = nh // SPLIT
    iota_r, iota_c, tri, strict = planes(SEQ)
    gain = gain_ref[...]
    seqs = [Sequence(dims, half, shared, slice(i * SEQ, (i + 1) * SEQ), iota_r, iota_c, tri) for i in range(out_ref.shape[0] // SEQ)]
    units = [(i, h) for i in range(len(seqs)) for h in range(hs)]
    ms = [three(seqs[i].ks[h], seqs[i].ks[h], NT) for i, h in units]
    ns = [jnp.where(strict, seqs[i].bs[h] * seqs[i].ls[h] * m, 0.0) for (i, h), m in zip(units, ms)]
    xs = inverses(ns, iota_r, iota_c)
    us = [three(x, seqs[i].bs[h] * seqs[i].v[:, h * dv : (h + 1) * dv], NN) for (i, h), x in zip(units, xs)]
    ps = [seqs[i].ls[h] * three(seqs[i].qs[h], seqs[i].ks[h], NT) for i, h in units]
    os = [three(p, u, NN) for p, u in zip(ps, us)]
    for (i, h), x, u, o in zip(units, xs, us, os):
        rows, sl = seqs[i].rows, slice(h * dv, (h + 1) * dv)
        x_ref[i * hs + h] = x
        u_ref[rows, sl] = u
        o_ref[rows, sl] = o
        r = lax.rsqrt(jnp.mean(o * o, axis=-1, keepdims=True) + 1e-5)
        pg = pg_ref[rows, sl]
        out_ref[rows, sl] = (o * r * gain * (pg * sigmoid(pg))).astype(bf16)


def bwd_kernel(dims, half, has_before, *refs):
    shared, (x_ref, u_ref, o_ref, dm_ref) = refs[:9], refs[9:13]
    dp_ref, dba_ref, dtaps_ref, dgain_ref, dprm_ref = refs[-5:]
    pg_ref, gain_ref, prm_ref = refs[3], refs[7], refs[8]
    nh, dk, dv = dims
    hs = nh // SPLIT
    wq, wv = hs * dk, hs * dv
    at = half * hs
    iota_r, iota_c, tri, strict = planes(SEQ)
    gain = gain_ref[...]
    prm = prm_ref[...]
    seqs = [Sequence(dims, half, shared, slice(i * SEQ, (i + 1) * SEQ), iota_r, iota_c, tri) for i in range(dm_ref.shape[0] // SEQ)]
    units = [(i, h) for i in range(len(seqs)) for h in range(hs)]
    dgain = jnp.zeros_like(gain)
    dos, us = [], []
    for i, h in units:
        rows, sl = seqs[i].rows, slice(h * dv, (h + 1) * dv)
        o = o_ref[rows, sl]
        pg = pg_ref[rows, sl]
        dm = dm_ref[rows, sl]
        r = lax.rsqrt(jnp.mean(o * o, axis=-1, keepdims=True) + 1e-5)
        nrm = o * r
        sg = sigmoid(pg)
        dp_ref[rows, 2 * wq + wv + h * dv : 2 * wq + wv + (h + 1) * dv] = (dm * nrm * gain * (sg * (1.0 + pg * (1.0 - sg)))).astype(bf16)
        dy = dm * (pg * sg)
        dgain = dgain + jnp.sum(dy * nrm, axis=0, keepdims=True)
        dn = dy * gain
        dos.append(r * (dn - nrm * jnp.mean(nrm * dn, axis=-1, keepdims=True)))
        us.append(u_ref[rows, sl])
    bm = [jnp.where(strict, seqs[i].ls[h] * three(seqs[i].ks[h], seqs[i].ks[h], NT), 0.0) for i, h in units]
    ps = [seqs[i].ls[h] * three(seqs[i].qs[h], seqs[i].ks[h], NT) for i, h in units]
    dps = [three(do, u, NT) for do, u in zip(dos, us)]
    dus = [three(p, do, TN) for p, do in zip(ps, dos)]
    dws = [three(x_ref[i * hs + h], du, TN) for (i, h), du in zip(units, dus)]
    das = [-three(dw, u, NT) for dw, u in zip(dws, us)]

    @pl.when(pl.program_id(0) == 0)
    def _():
        dtaps_ref[...] = jnp.zeros_like(dtaps_ref)
        dgain_ref[...] = jnp.zeros_like(dgain_ref)
        dprm_ref[...] = jnp.zeros_like(dprm_ref)

    dgain_ref[...] += dgain
    lane = lax.broadcasted_iota(jnp.int32, (SEQ, 128), 1)
    ones = jnp.ones((SEQ, 128), f32)
    sc = dk ** -0.5
    for i, q in enumerate(seqs):
        rows, pos = q.rows, q.pos
        dbeta = jnp.zeros((SEQ, 128), f32)
        dlog = jnp.zeros((SEQ, 128), f32)
        dz = ([], [], [])
        for h in range(hs):
            n = i * hs + h
            vh = q.v[:, h * dv : (h + 1) * dv]
            ab = das[n] * bm[n]
            dbeta = jnp.where(lane == at + h, jnp.sum(dws[n] * vh, axis=-1, keepdims=True) + jnp.sum(ab, axis=-1, keepdims=True), dbeta)
            e = q.bs[h] * ab + dps[n] * ps[n]
            dlog = jnp.where(lane == nh + at + h, jnp.sum(e, axis=-1, keepdims=True) - exact_right(e, ones, TN), dlog)
            ds = dps[n] * q.ls[h]
            dmm = jnp.where(strict, q.bs[h] * das[n] * q.ls[h], 0.0)
            dq = sc * three(ds, q.ks[h], NN)
            dkh = three(ds, q.qs[h], TN) + three(dmm, q.ks[h], NN) + three(dmm, q.ks[h], TN)
            qh, rq = q.uq[h]
            kh, rk = q.uk[h]
            dz[0].append(rq * (dq - qh * jnp.sum(qh * dq, axis=-1, keepdims=True)))
            dz[1].append(rk * (dkh - kh * jnp.sum(kh * dkh, axis=-1, keepdims=True)))
            dz[2].append(q.bs[h] * dws[n])
        ddecay = exact_left(tri, dlog, TN)
        drate = -prm[0:1] * ddecay * sigmoid(q.rate)
        dba = dbeta * q.beta * (1.0 - q.beta) + drate
        if has_before:
            dba = dba + refs[13][rows, :]
            dp_ref[rows, 2 * wq + 2 * wv :] = dba.astype(bf16)
        dba_ref[rows, :] = dba
        dprm_ref[0:1, :] += jnp.sum(ddecay * q.decay, axis=0, keepdims=True)
        dprm_ref[1:2, :] += jnp.sum(drate, axis=0, keepdims=True)
        to = 0
        for parts, z, sg, c, tap in zip(dz, q.z, q.sig, q.raw, q.taps):
            d = jnp.concatenate(parts, axis=1) * (sg * (1.0 + z * (1.0 - sg)))
            width = tap.shape[0]
            w = c.shape[1]
            dc = d * tap[width - 1 : width]
            dtaps_ref[width - 1 : width, to : to + w] += jnp.sum(d * c, axis=0, keepdims=True)
            for s in range(1, width):
                m = jnp.where(pos >= s, d, 0.0)
                dc = dc + pltpu.roll(m, SEQ - s, 0) * tap[width - 1 - s : width - s]
                dtaps_ref[width - 1 - s : width - s, to : to + w] += jnp.sum(m * pltpu.roll(c, s, 0), axis=0, keepdims=True)
            dp_ref[rows, to : to + w] = dc.astype(bf16)
            to += w


def shared_specs(dims, off=0):
    nh, dk, dv = dims
    wq, wv = nh // SPLIT * dk, nh // SPLIT * dv
    at = (2 * wq) // wv
    small = (2 * wq + 2 * wv) // 128
    return [
        pl.BlockSpec((ROWS, wq), lambda i: (i + off, 0)),
        pl.BlockSpec((ROWS, wq), lambda i: (i + off, 1)),
        pl.BlockSpec((ROWS, wv), lambda i: (i + off, at)),
        pl.BlockSpec((ROWS, wv), lambda i: (i + off, at + 1)),
        pl.BlockSpec((ROWS, 128), lambda i: (i + off, small)),
        pl.BlockSpec((ROWS, 1), lambda i: (i + off, 0)),
        pl.BlockSpec((4, 2 * wq + wv), lambda i: (0, 0)),
        pl.BlockSpec((1, dv), lambda i: (0, 0)),
        pl.BlockSpec((8, 128), lambda i: (0, 0)),
    ]


def cost(us):
    return pl.CostEstimate(flops=int(us * 1.1e9), bytes_accessed=int(us * 1e6), transcendentals=0)


def mixer_fwd(proj, first, pos, taps, gain, prm, dims, half, mixed=None):
    tok = pos.shape[0]
    nh, dk, dv = dims
    hs = nh // SPLIT
    ns = tok // SEQ
    wv = hs * dv
    row = pl.BlockSpec((ROWS, wv), lambda i: (i, 0))
    specs = shared_specs(dims)
    args = [proj, proj, proj, proj, first, pos, taps, gain, prm]
    alias = {}
    if mixed is not None:
        alias = {len(args): 0}
        args.append(mixed)
        specs.append(pl.BlockSpec(memory_space=pl.ANY))
    return pl.pallas_call(
        functools.partial(fwd_kernel, dims, half),
        grid=(ns // PAIR,),
        in_specs=specs,
        out_specs=[
            pl.BlockSpec((ROWS, wv), lambda i: (i, half)),
            pl.BlockSpec((PAIR * hs, SEQ, SEQ), lambda i: (i, 0, 0)),
            row,
            row,
        ],
        out_shape=[
            jax.ShapeDtypeStruct((tok, nh * dv), bf16),
            jax.ShapeDtypeStruct((ns * hs, SEQ, SEQ), f32),
            jax.ShapeDtypeStruct((tok, wv), f32),
            jax.ShapeDtypeStruct((tok, wv), f32),
        ],
        input_output_aliases=alias,
        cost_estimate=cost(4),
        compiler_params=pltpu.CompilerParams(vmem_limit_bytes=48 << 20),
    )(*args)


def mixer_bwd(proj, first, pos, taps, gain, prm, x, u, o, dm, dims, half, part, before=None, filled=None):
    tok = pos.shape[0]
    nh, dk, dv = dims
    hs = nh // SPLIT
    ns = tok // SEQ
    wq, wv = hs * dk, hs * dv
    steps = dm.shape[0] // ROWS
    off = part * steps
    row = pl.BlockSpec((ROWS, wv), lambda i: (i + off, 0))
    lanes = pl.BlockSpec((ROWS, 128), lambda i: (i + off, 0))
    specs = shared_specs(dims, off) + [
        pl.BlockSpec((PAIR * hs, SEQ, SEQ), lambda i: (i + off, 0, 0)), row, row, pl.BlockSpec((ROWS, wv), lambda i: (i, half))]
    args = [proj, proj, proj, proj, first, pos, taps, gain, prm, x, u, o, dm]
    width = 2 * wq + 2 * wv
    if before is not None:
        args.append(before)
        specs.append(lanes)
        width += 128
    alias = {}
    if filled is not None:
        alias = {len(args): 0, len(args) + 1: 1}
        args += filled
        specs += [pl.BlockSpec(memory_space=pl.ANY)] * 2
    return pl.pallas_call(
        functools.partial(bwd_kernel, dims, half, before is not None),
        grid=(steps,),
        in_specs=specs,
        out_specs=[
            pl.BlockSpec((ROWS, width), lambda i: (i + off, 0)),
            lanes,
            pl.BlockSpec((4, 2 * wq + wv), lambda i: (0, 0)),
            pl.BlockSpec((1, dv), lambda i: (0, 0)),
            pl.BlockSpec((8, 128), lambda i: (0, 0)),
        ],
        out_shape=[
            jax.ShapeDtypeStruct((tok, width), bf16),
            jax.ShapeDtypeStruct((tok, 128), f32),
            jax.ShapeDtypeStruct((4, 2 * wq + wv), f32),
            jax.ShapeDtypeStruct((1, dv), f32),
            jax.ShapeDtypeStruct((8, 128), f32),
        ],
        input_output_aliases=alias,
        cost_estimate=cost(26),
        compiler_params=pltpu.CompilerParams(vmem_limit_bytes=56 << 20),
    )(*args)


def xor_send(value, axis, size, step):
    return lax.ppermute(value, axis, [(i, i ^ step) for i in range(size)])


def after(value, *needs):
    return lax.optimization_barrier((value, *needs))[0]


def lines(size):
    return [[low + 2 * i for i in range(size // 2)] for low in range(2)]


def gather_line(rows, size):
    return lax.all_gather(rows, "fsdp", axis=0, tiled=True, axis_index_groups=lines(size))


def gather_side(near, size, *needs):
    got = xor_send(after(near, *needs) if needs else near, "fsdp", size, 1)
    return jnp.concatenate([near, got], axis=0), got


def gather_side_first(rows, size, *needs):
    got = xor_send(after(rows, *needs), "fsdp", size, 1)
    full = gather_line(jnp.concatenate([rows, got], axis=0), size)
    width = rows.shape[1]
    return full.reshape(size // 2, 2, -1, width).swapaxes(0, 1).reshape(-1, width), full, got


def dot(left, right, dims=NN, out=f32):
    return lax.dot_general(left, right, dims, preferred_element_type=f32).astype(out)


class Summed:
    def __init__(self, left, right, size, *needs):
        self.size = size
        self.half = left.shape[1] // 2
        self.left, self.right = left, right
        self.sent = dot(left[:, self.half :], right, TN, bf16)
        self.got = xor_send(after(self.sent, *needs) if needs else self.sent, "fsdp", size, 1)

    def side(self, *needs, before=()):
        keep = dot(self.left[:, : self.half], after(self.right, *needs) if needs else self.right, TN)
        self.low = (keep + self.got.astype(f32)).astype(bf16)
        ready = after(self.low, *before) if before else self.low
        self.sum = lax.psum_scatter(ready, "fsdp", scatter_dimension=0, tiled=True, axis_index_groups=lines(self.size))

    def total(self, ranks):
        return lax.all_to_all(self.sum.reshape(ranks, -1, self.sum.shape[1]), "rep", 0, 0)


def join_tokens(rows, size):
    half = size // 2

    def around(block):
        held = {0: block}
        step = half // 2
        while step:
            for j in list(held):
                held[j ^ step] = xor_send(held[j], "rep", size, step)
            step //= 2
        return jnp.concatenate([held[j] for j in range(half)], axis=0)

    beyond = xor_send(rows, "rep", size, half)
    return around(rows), around(beyond), beyond


def sum_tokens(far, near, size, *needs):
    half = size // 2

    def around(part):
        held = jnp.split(part, half, axis=0)
        step = 1
        while step < half:
            for j in range(0, half, 2 * step):
                held[j] = held[j] + xor_send(held[j + step].astype(bf16), "rep", size, step).astype(f32)
            step *= 2
        return held[0]

    beyond = around(far()).astype(bf16)
    part = near(beyond)
    if needs:
        beyond = after(beyond, *needs)
    got = xor_send(beyond, "rep", size, half)
    return around(part) + got.astype(f32), got


def rms(values):
    return lax.rsqrt(jnp.mean(values * values, axis=-1, keepdims=True) + 1e-06)


def norm_back(n, r, gain, dout):
    scaled = dout * gain
    return r * (scaled - n * jnp.mean(n * scaled, axis=-1, keepdims=True)), jnp.sum(dout * n, axis=0)


def make(F, R):
    both = ("fsdp", "rep")

    def on_device(tokens, segments, cotangent, gain_one, w_query, w_key, w_value, w_gate, w_beta, w_alpha, conv_q, conv_k,
                  conv_v, a_log, dt_bias, norm_gain, w_out, gain_two, w_ffgate, w_ffup, w_down):
        f = lax.axis_index("fsdp")
        r = lax.axis_index("rep")
        N = F * R
        rows_own, D = tokens.shape
        heads = a_log.shape[0]
        dk = w_query.shape[1] // heads
        dv = w_value.shape[1] // heads
        nh = heads // R
        dims = (nh, dk, dv)
        wq, wv = nh * dk, nh * dv
        hq, hv = wq // SPLIT, wv // SPLIT
        shard = D // N
        block = D // F
        ffq = w_ffgate.shape[1] // R
        tok = rows_own * R
        ns = tok // SEQ
        tiny = dv // N
        per = conv_v.shape[1] // shard

        low_bit = f & 1

        def swap(array, axis):
            half = array.shape[axis] // 2
            return jnp.concatenate(
                [lax.dynamic_slice_in_dim(array, (low_bit ^ j) * half, half, axis=axis) for j in range(2)], axis=axis)

        def mix(array, axis):
            at = [slice(None)] * array.ndim
            parts = []
            for bit in range(2):
                for i in range(F // 2):
                    at[axis] = slice((2 * i + bit) * block, (2 * i + bit + 1) * block)
                    parts.append(array[tuple(at)])
            return swap(jnp.concatenate(parts, axis=axis), axis)

        def unmix(array, axis):
            array = swap(array, axis)
            at = [slice(None)] * array.ndim
            parts = []
            for i in range(F // 2):
                for bit in range(2):
                    p = bit * (F // 2) + i
                    at[axis] = slice(p * block, (p + 1) * block)
                    parts.append(array[tuple(at)])
            return jnp.concatenate(parts, axis=axis)

        def quarter(arrays):
            return jnp.concatenate([a.reshape(shard, R, -1) for a in arrays], axis=2)

        def spread(packed):
            return lax.all_to_all(packed.transpose(1, 0, 2), "rep", 0, 0).reshape(R * shard, -1)

        extra = jnp.concatenate(
            [gain_one[:, None], gain_two[:, None], conv_q.T, conv_k.T,
             conv_v.reshape(4, shard, per).transpose(1, 0, 2).reshape(shard, 4 * per),
             jnp.pad(norm_gain, (0, shard - tiny))[:, None]], axis=1).T
        small = jnp.concatenate([w_beta.reshape(shard, R, nh), w_alpha.reshape(shard, R, nh)], axis=2)
        small = jnp.pad(small, ((0, 0), (0, 0), (0, 128 - 2 * nh)))

        def halves(array, width):
            parts = array.reshape(shard, R, SPLIT, width)
            return [parts[:, :, h] for h in range(SPLIT)]

        q_h, k_h, v_h, g_h = halves(w_query, hq), halves(w_key, hq), halves(w_value, hv), halves(w_gate, hv)
        own = mix(tokens, 1)
        part_a = spread(jnp.concatenate([q_h[0], k_h[0], v_h[0], g_h[0], small, q_h[1], k_h[1], v_h[1], g_h[1]], axis=2))
        w1 = 2 * hq + 2 * hv
        part_a = after(part_a, own)
        part_1, part_2 = part_a[:, : w1 + 128], part_a[:, w1 + 128 :]
        extra_all = lax.all_to_all(jnp.broadcast_to(after(extra, part_a)[None], (N, *extra.shape)), both, 0, 0)
        extra_all = extra_all.transpose(1, 0, 2).reshape(-1, D).astype(f32)
        line_1 = gather_line(part_1, F)
        every_near, every_far, every_got = join_tokens(own, R)
        every = jnp.concatenate([every_near, every_far], axis=0)
        ids_all = jnp.concatenate(join_tokens(segments[:, None], R)[:2], axis=0).reshape(ns, SEQ)
        part_r = spread(quarter([after(w_out.T, extra_all, every_got, line_1), w_ffgate, w_ffup, w_down.T]))
        part_b, part_gu, part_d = part_r[:, :wv], part_r[:, wv : wv + 2 * ffq], part_r[:, wv + 2 * ffq :]
        line_2 = gather_line(after(part_2, extra_all), F)
        wa1, side_1 = gather_side(line_1, F)
        cot = mix(cotangent, 1)
        cot_near, cot_far, unused = join_tokens(after(cot, side_1), R)
        line_b = gather_line(part_b, F)
        line_gu = gather_line(part_gu, F)

        gains = mix(extra_all[:2], 1)
        gain_first, gain_second = gains[0:1], gains[1:2]
        cq = lax.dynamic_slice_in_dim(extra_all[2:6], r * wq, wq, axis=1)
        ck = lax.dynamic_slice_in_dim(extra_all[6:10], r * wq, wq, axis=1)
        cv = extra_all[10 : 10 + 4 * per].reshape(4, per, D).transpose(0, 2, 1).reshape(4, D * per)
        cv = lax.dynamic_slice_in_dim(cv, r * wv, wv, axis=1)
        gain_out = extra_all[10 + 4 * per].reshape(N, shard)[:, :tiny].reshape(1, dv)
        taps = [jnp.concatenate([cq[:, h * hq : (h + 1) * hq], ck[:, h * hq : (h + 1) * hq], cv[:, h * hv : (h + 1) * hv]], axis=1)
                for h in range(SPLIT)]
        prm = jnp.stack([jnp.exp(lax.dynamic_slice_in_dim(a_log, r * nh, nh)), lax.dynamic_slice_in_dim(dt_bias, r * nh, nh)])
        prm = jnp.pad(prm, ((0, 6), (nh, 128 - 2 * nh)))
        place = jnp.arange(SEQ)
        same = (ids_all[:, :, None] == ids_all[:, None, :]) & (place[:, None] >= place[None, :])[None]
        pos = (jnp.sum(same.astype(f32), axis=2) - 1.0).reshape(tok, 1)

        every32 = every.astype(f32)
        normed_one = (every32 * rms(every32) * gain_first).astype(bf16)
        proj_1 = dot(after(normed_one, line_2, part_r), wa1)
        mixed, x_1, u_1, o_1 = mixer_fwd(proj_1, proj_1, pos, taps[0], gain_out, prm, dims, 0)
        wa2, side_2 = gather_side(line_2, F, side_1)
        proj_2 = dot(after(normed_one, mixed, line_b), wa2)
        mixed, x_2, u_2, o_2 = mixer_fwd(proj_2, proj_1, pos, taps[1], gain_out, prm, dims, 1, mixed)
        wd, line_d, got_d = gather_side_first(part_d, F, side_2)
        wb, side_b = gather_side(line_b, F, side_2)
        mixed = after(mixed, line_gu, got_d, cot_near, cot_far)
        side_gu = xor_send(after(line_gu, side_b), "fsdp", F, 1)
        wg, wu = (jnp.concatenate([line_gu[:, at : at + ffq], side_gu[:, at : at + ffq]], axis=0) for at in (0, ffq))
        own32 = own.astype(f32)
        mid = tok // 2
        added, unused = sum_tokens(lambda: dot(mixed[mid:], wb, NT), lambda part: dot(after(mixed, part)[:mid], wb, NT), R)
        middle = own32 + added
        r2 = rms(middle)
        n2 = middle * r2
        normed_own = (n2 * gain_second).astype(bf16)
        two = join_tokens(normed_own, R)[:2]
        gates, ups, acts, sigs, hiddens = [], [], [], [], []
        for normed in (two[0], after(two[1], line_d)):
            gates.append(dot(normed, wg))
            ups.append(dot(normed, wu))
            sigs.append(jax.nn.sigmoid(gates[-1]))
            acts.append(gates[-1] * sigs[-1])
            hiddens.append((acts[-1] * ups[-1]).astype(bf16))
        hidden = jnp.concatenate(hiddens, axis=0)
        normed_two = jnp.concatenate(two, axis=0)
        cot_all = jnp.concatenate([cot_near, cot_far], axis=0)

        kept = {}

        def keep(name, value):
            kept[name] = value
            return value

        g_down = Summed(cot_all, hidden, F)
        dgates, dups = [None, None], [None, None]

        def back_two(t, *needs):
            dhidden = dot(after((cot_near, cot_far)[t], *needs), wd)
            dgates[t] = (dhidden * ups[t] * (sigs[t] * (1.0 + gates[t] * (1.0 - sigs[t])))).astype(bf16)
            dups[t] = (dhidden * acts[t]).astype(bf16)
            return dot(dgates[t], wg, NT) + dot(dups[t], wu, NT)

        dnormed_two, far_two = sum_tokens(lambda: back_two(1, g_down.sent), lambda part: keep("two", back_two(0, part)), R)
        g_down.side(kept["two"])
        g_gate = Summed(normed_two, after(jnp.concatenate(dgates, axis=0), g_down.low), F, g_down.got)
        dinner, dgain_second = norm_back(n2, r2, gain_second, after(dnormed_two, g_gate.sent))
        dmiddle = cot.astype(f32) + dinner
        dmiddle_own = dmiddle.astype(bf16)
        dlow = join_tokens(dmiddle_own, R)[:2]
        dm_near = dot(dlow[0], wb)
        args_2 = (proj_2, proj_1, pos, taps[1], gain_out, prm, x_2, u_2, o_2)
        args_1 = (proj_1, proj_1, pos, taps[0], gain_out, prm, x_1, u_1, o_1)
        dp_2, dba, dt_2, dg_2, dr_2 = mixer_bwd(*args_2, dm_near, dims, 1, 0)
        g_up = Summed(normed_two, after(jnp.concatenate(dups, axis=0), dba), F, g_gate.got)
        g_gate.side(g_up.sent)
        dp_1, dba_1, dt_1, dg_1, dr_1 = mixer_bwd(*args_1, after(dm_near, g_gate.low, g_down.sum), dims, 0, 0, dba)
        t_down = g_down.total(R)
        g_out = Summed(jnp.concatenate(dlow, axis=0), after(mixed, dba_1), F)
        dm_far = dot(after(dlow[1], dba_1), wb)
        dp_2, dba, et_2, eg_2, er_2 = mixer_bwd(*args_2, after(dm_far, g_out.sent), dims, 1, 1, None, [dp_2, dba])
        g_up.side(dba)
        g_2 = Summed(normed_one, after(dp_2, g_up.low, g_gate.sum), F)
        t_gate = g_gate.total(R)
        dp_1, dba_1, et_1, eg_1, er_1 = mixer_bwd(
            *args_1, after(dm_far, g_2.sent, t_down), dims, 0, 1, dba, [dp_1, dba_1])
        g_out.side(dp_1)
        g_1 = Summed(normed_one, after(dp_1, g_out.low), F)
        t_up = g_up.total(R)

        def back_one(lo, hi, *needs):
            return dot(after(dp_1, *needs)[lo:hi], wa1, NT) + dot(after(dp_2, *needs)[lo:hi], wa2, NT)

        t_out = g_out.total(R)

        def near_one(part):
            g_2.side(part, before=(g_out.sum,))

            def far_out():
                return keep("far", dot(after(hiddens[1], g_2.low, t_up), wd, NT))

            def near_out(held):
                g_1.side(kept["far"], held, before=(g_2.sum,))
                return keep("last", dot(after(hiddens[0], g_1.low), wd, NT))

            kept["out"], unused = sum_tokens(far_out, near_out, R)
            return back_one(0, mid, kept["last"], t_out, g_2.sum)

        dnormed_one, far_one = sum_tokens(lambda: back_one(mid, tok, g_1.sent, g_up.sum, t_gate), near_one, R)
        added = kept["out"]
        layer_out = (middle + added).astype(bf16)
        dprm = dr_1 + dr_2 + er_1 + er_2
        dgain_out = dg_1 + dg_2 + eg_1 + eg_2
        dtaps = [dt_1 + et_1, dt_2 + et_2]

        n1 = own32 * rms(own32)
        dfirst, dgain_first = norm_back(n1, rms(own32), gain_first, dnormed_one)
        grad_tokens = unmix(dmiddle + dfirst, 1)

        def wide(parts):
            return parts.astype(f32).transpose(1, 0, 2).reshape(shard, -1)

        def tall(parts):
            return parts.astype(f32).transpose(0, 2, 1).reshape(-1, shard)

        t_2 = g_2.total(R)
        t_1 = g_1.total(R)

        def joined(lo, width):
            return jnp.stack([t[:, :, lo : lo + width] for t in (t_1, t_2)], axis=2).astype(f32).transpose(1, 0, 2, 3).reshape(shard, -1)

        grad_query, grad_key = joined(0, hq), joined(hq, hq)
        grad_value, grad_gate_w = joined(2 * hq, hv), joined(2 * hq + hv, hv)
        grad_beta, grad_alpha = wide(t_1[:, :, w1 : w1 + nh]), wide(t_1[:, :, w1 + nh : w1 + 2 * nh])
        grad_down, grad_out = tall(t_down), tall(t_out)
        grad_gate, grad_up = wide(t_gate), wide(t_up)

        def placed(parts, total, width):
            part = jnp.concatenate(parts, axis=1)
            return lax.dynamic_update_slice(jnp.zeros((4, total), f32), part, (0, r * width))

        gq = placed([dtaps[h][:, :hq] for h in range(SPLIT)], R * wq, wq)
        gk = placed([dtaps[h][:, hq : 2 * hq] for h in range(SPLIT)], R * wq, wq)
        gv = placed([dtaps[h][:, 2 * hq :] for h in range(SPLIT)], R * wv, wv)
        heads_part = lax.dynamic_update_slice(jnp.zeros((2, heads), f32), dprm[:2, nh : 2 * nh], (0, r * nh)).reshape(1, -1)
        packed = jnp.concatenate([
            unmix(dgain_first[None], 1).reshape(N, -1),
            unmix(dgain_second[None], 1).reshape(N, -1),
            gq.reshape(4, N, -1).transpose(1, 0, 2).reshape(N, -1),
            gk.reshape(4, N, -1).transpose(1, 0, 2).reshape(N, -1),
            gv.reshape(4, N, -1).transpose(1, 0, 2).reshape(N, -1),
            dgain_out.reshape(N, tiny),
            jnp.broadcast_to(heads_part, (N, 2 * heads))], axis=1)
        summed = jnp.sum(lax.all_to_all(packed, both, 0, 0, tiled=True), axis=0)
        sizes = [shard, shard, 4 * shard, 4 * shard, 4 * shard * per, tiny, heads, heads]
        ends = [0]
        for size in sizes:
            ends.append(ends[-1] + size)
        pick = [summed[ends[i] : ends[i + 1]] for i in range(len(sizes))]
        return (
            unmix(layer_out, 1), grad_tokens, pick[0], grad_query, grad_key, grad_value, grad_gate_w, grad_beta, grad_alpha,
            pick[2].reshape(4, shard), pick[3].reshape(4, shard), pick[4].reshape(4, shard * per), pick[6], pick[7], pick[5],
            grad_out, pick[1], grad_gate, grad_up, grad_down)

    return on_device


def solution(mesh):
    rows, cols, flat = P(("fsdp", "rep"), None), P(None, ("fsdp", "rep")), P(("fsdp", "rep"))
    placed = (rows, flat, rows, flat, rows, rows, rows, rows, rows, rows, cols, cols, cols, P(), P(), flat, cols, flat, rows, rows, cols)
    made = (rows, rows, flat, rows, rows, rows, rows, rows, rows, cols, cols, cols, P(), P(), flat, cols, flat, rows, rows, cols)
    return jax.shard_map(
        make(mesh.shape["fsdp"], mesh.shape["rep"]), mesh=mesh, in_specs=placed, out_specs=made, check_vma=False)
```

```python
import functools

import jax
import jax.numpy as jnp
from jax import lax
from jax.experimental import pallas as pl
from jax.experimental.pallas import tpu as pltpu
from jax.sharding import PartitionSpec as P

SEQ = 256
SPLIT = 2
PAIR = 2
ROWS = PAIR * SEQ

f32 = jnp.float32
bf16 = jnp.bfloat16
NN = (((1,), (0,)), ((), ()))
NT = (((1,), (1,)), ((), ()))
TN = (((0,), (0,)), ((), ()))


def split(a):
    hi = a.astype(bf16)
    return hi, (a - hi.astype(f32)).astype(bf16)


def one(a, b, dims):
    return lax.dot_general(a.astype(bf16), b.astype(bf16), dims, preferred_element_type=f32)


def three(a, b, dims):
    ah, al = split(a)
    bh, bl = split(b)
    out = lax.dot_general(ah, bl, dims, preferred_element_type=f32)
    out = out + lax.dot_general(al, bh, dims, preferred_element_type=f32)
    return out + lax.dot_general(ah, bh, dims, preferred_element_type=f32)


def exact_left(a, b, dims):
    bh, bl = split(b)
    a = a.astype(bf16)
    return lax.dot_general(a, bh, dims, preferred_element_type=f32) + lax.dot_general(a, bl, dims, preferred_element_type=f32)


def exact_right(a, b, dims):
    ah, al = split(a)
    b = b.astype(bf16)
    return lax.dot_general(ah, b, dims, preferred_element_type=f32) + lax.dot_general(al, b, dims, preferred_element_type=f32)


def sigmoid(v):
    return 1.0 / (1.0 + jnp.exp(-v))


def conv(c, taps, pos):
    width = taps.shape[0]
    z = c * taps[width - 1 : width]
    for s in range(1, width):
        z = z + jnp.where(pos >= s, pltpu.roll(c, s, 0), 0.0) * taps[width - 1 - s : width - s]
    return z


def unit(c):
    r = lax.rsqrt(jnp.sum(c * c, axis=-1, keepdims=True) + 1e-6)
    return c * r, r


def inverses(n_list, iota_r, iota_c):
    size = n_list[0].shape[0]
    eye = (iota_r == iota_c).astype(f32)
    xs = None
    b = 1
    while b < size:
        mask = ((iota_r // (2 * b)) == (iota_c // (2 * b))) & ((iota_r // b) % 2 == 1) & ((iota_c // b) % 2 == 0)
        cs = [jnp.where(mask, n, 0.0) for n in n_list]
        if xs is None:
            xs = [eye - c for c in cs]
        else:
            low = [x.astype(bf16) for x in xs]
            t = [one(c, x, NN) for c, x in zip(cs, low)]
            xs = [x - one(y, z, NN) for x, y, z in zip(xs, low, t)]
        b *= 2
    left = [(eye - x) - three(n, x, NN) for n, x in zip(n_list, xs)]
    return [x + one(x, r, NN) for x, r in zip(xs, left)]


def rates(pba, prm, tri):
    beta = sigmoid(pba)
    rate = pba + prm[1:2]
    decay = -prm[0:1] * (jnp.maximum(rate, 0.0) + jnp.log1p(jnp.exp(-jnp.abs(rate))))
    return beta, rate, decay, exact_left(tri, decay, NN), exact_right(decay, tri, (((0,), (1,)), ((), ())))


class Sequence:
    def __init__(self, dims, half, refs, rows, iota_r, iota_c, tri):
        pq_ref, pk_ref, pv_ref, pg_ref, ba_ref, pos_ref, taps_ref, gain_ref, prm_ref = refs
        nh, dk, dv = dims
        hs = nh // SPLIT
        wq = hs * dk
        at = half * hs
        H = range(hs)
        self.rows = rows
        self.pos = pos_ref[rows, :]
        taps = taps_ref[...]
        self.taps = (taps[:, :wq], taps[:, wq : 2 * wq], taps[:, 2 * wq :])
        self.raw = (pq_ref[rows, :], pk_ref[rows, :], pv_ref[rows, :])
        self.beta, self.rate, self.decay, gcol, grow = rates(ba_ref[rows, :], prm_ref[...], tri)
        self.z = tuple(conv(c, t, self.pos) for c, t in zip(self.raw, self.taps))
        self.sig = tuple(sigmoid(z) for z in self.z)
        qc, kc, self.v = (z * g for z, g in zip(self.z, self.sig))
        live = (iota_c <= iota_r) & (iota_c >= iota_r - self.pos.astype(jnp.int32))
        self.bs = [self.beta[:, at + h : at + h + 1] for h in H]
        self.uq = [unit(qc[:, h * dk : (h + 1) * dk]) for h in H]
        self.uk = [unit(kc[:, h * dk : (h + 1) * dk]) for h in H]
        self.qs = [a * dk ** -0.5 for a, _ in self.uq]
        self.ks = [a for a, _ in self.uk]
        lane = nh + at
        self.ls = [
            jnp.where(live, jnp.exp(jnp.where(live, gcol[:, lane + h : lane + h + 1] - grow[lane + h : lane + h + 1, :], 0.0)), 0.0)
            for h in H]


def planes(n):
    iota_r = lax.broadcasted_iota(jnp.int32, (n, n), 0)
    iota_c = lax.broadcasted_iota(jnp.int32, (n, n), 1)
    return iota_r, iota_c, (iota_c <= iota_r).astype(f32), iota_c < iota_r


def fwd_kernel(dims, half, *refs):
    shared, (out_ref, x_ref, u_ref, o_ref) = refs[:9], refs[-4:]
    pg_ref, gain_ref = refs[3], refs[7]
    nh, dk, dv = dims
    hs = nh // SPLIT
    iota_r, iota_c, tri, strict = planes(SEQ)
    gain = gain_ref[...]
    seqs = [Sequence(dims, half, shared, slice(i * SEQ, (i + 1) * SEQ), iota_r, iota_c, tri) for i in range(out_ref.shape[0] // SEQ)]
    units = [(i, h) for i in range(len(seqs)) for h in range(hs)]
    ms = [three(seqs[i].ks[h], seqs[i].ks[h], NT) for i, h in units]
    ns = [jnp.where(strict, seqs[i].bs[h] * seqs[i].ls[h] * m, 0.0) for (i, h), m in zip(units, ms)]
    xs = inverses(ns, iota_r, iota_c)
    us = [three(x, seqs[i].bs[h] * seqs[i].v[:, h * dv : (h + 1) * dv], NN) for (i, h), x in zip(units, xs)]
    ps = [seqs[i].ls[h] * three(seqs[i].qs[h], seqs[i].ks[h], NT) for i, h in units]
    os = [three(p, u, NN) for p, u in zip(ps, us)]
    for (i, h), x, u, o in zip(units, xs, us, os):
        rows, sl = seqs[i].rows, slice(h * dv, (h + 1) * dv)
        x_ref[i * hs + h] = x
        u_ref[rows, sl] = u
        o_ref[rows, sl] = o
        r = lax.rsqrt(jnp.mean(o * o, axis=-1, keepdims=True) + 1e-5)
        pg = pg_ref[rows, sl]
        out_ref[rows, sl] = (o * r * gain * (pg * sigmoid(pg))).astype(bf16)


def bwd_kernel(dims, half, has_before, *refs):
    shared, (x_ref, u_ref, o_ref, dm_ref) = refs[:9], refs[9:13]
    dp_ref, dba_ref, dtaps_ref, dgain_ref, dprm_ref = refs[-5:]
    pg_ref, gain_ref, prm_ref = refs[3], refs[7], refs[8]
    nh, dk, dv = dims
    hs = nh // SPLIT
    wq, wv = hs * dk, hs * dv
    at = half * hs
    iota_r, iota_c, tri, strict = planes(SEQ)
    gain = gain_ref[...]
    prm = prm_ref[...]
    seqs = [Sequence(dims, half, shared, slice(i * SEQ, (i + 1) * SEQ), iota_r, iota_c, tri) for i in range(dm_ref.shape[0] // SEQ)]
    units = [(i, h) for i in range(len(seqs)) for h in range(hs)]
    dgain = jnp.zeros_like(gain)
    dos, us = [], []
    for i, h in units:
        rows, sl = seqs[i].rows, slice(h * dv, (h + 1) * dv)
        o = o_ref[rows, sl]
        pg = pg_ref[rows, sl]
        dm = dm_ref[rows, sl]
        r = lax.rsqrt(jnp.mean(o * o, axis=-1, keepdims=True) + 1e-5)
        nrm = o * r
        sg = sigmoid(pg)
        dp_ref[rows, 2 * wq + wv + h * dv : 2 * wq + wv + (h + 1) * dv] = (dm * nrm * gain * (sg * (1.0 + pg * (1.0 - sg)))).astype(bf16)
        dy = dm * (pg * sg)
        dgain = dgain + jnp.sum(dy * nrm, axis=0, keepdims=True)
        dn = dy * gain
        dos.append(r * (dn - nrm * jnp.mean(nrm * dn, axis=-1, keepdims=True)))
        us.append(u_ref[rows, sl])
    bm = [jnp.where(strict, seqs[i].ls[h] * three(seqs[i].ks[h], seqs[i].ks[h], NT), 0.0) for i, h in units]
    ps = [seqs[i].ls[h] * three(seqs[i].qs[h], seqs[i].ks[h], NT) for i, h in units]
    dps = [three(do, u, NT) for do, u in zip(dos, us)]
    dus = [three(p, do, TN) for p, do in zip(ps, dos)]
    dws = [three(x_ref[i * hs + h], du, TN) for (i, h), du in zip(units, dus)]
    das = [-three(dw, u, NT) for dw, u in zip(dws, us)]

    @pl.when(pl.program_id(0) == 0)
    def _():
        dtaps_ref[...] = jnp.zeros_like(dtaps_ref)
        dgain_ref[...] = jnp.zeros_like(dgain_ref)
        dprm_ref[...] = jnp.zeros_like(dprm_ref)

    dgain_ref[...] += dgain
    lane = lax.broadcasted_iota(jnp.int32, (SEQ, 128), 1)
    ones = jnp.ones((SEQ, 128), f32)
    sc = dk ** -0.5
    for i, q in enumerate(seqs):
        rows, pos = q.rows, q.pos
        dbeta = jnp.zeros((SEQ, 128), f32)
        dlog = jnp.zeros((SEQ, 128), f32)
        dz = ([], [], [])
        for h in range(hs):
            n = i * hs + h
            vh = q.v[:, h * dv : (h + 1) * dv]
            ab = das[n] * bm[n]
            dbeta = jnp.where(lane == at + h, jnp.sum(dws[n] * vh, axis=-1, keepdims=True) + jnp.sum(ab, axis=-1, keepdims=True), dbeta)
            e = q.bs[h] * ab + dps[n] * ps[n]
            dlog = jnp.where(lane == nh + at + h, jnp.sum(e, axis=-1, keepdims=True) - exact_right(e, ones, TN), dlog)
            ds = dps[n] * q.ls[h]
            dmm = jnp.where(strict, q.bs[h] * das[n] * q.ls[h], 0.0)
            dq = sc * three(ds, q.ks[h], NN)
            dkh = three(ds, q.qs[h], TN) + three(dmm, q.ks[h], NN) + three(dmm, q.ks[h], TN)
            qh, rq = q.uq[h]
            kh, rk = q.uk[h]
            dz[0].append(rq * (dq - qh * jnp.sum(qh * dq, axis=-1, keepdims=True)))
            dz[1].append(rk * (dkh - kh * jnp.sum(kh * dkh, axis=-1, keepdims=True)))
            dz[2].append(q.bs[h] * dws[n])
        ddecay = exact_left(tri, dlog, TN)
        drate = -prm[0:1] * ddecay * sigmoid(q.rate)
        dba = dbeta * q.beta * (1.0 - q.beta) + drate
        if has_before:
            dba = dba + refs[13][rows, :]
            dp_ref[rows, 2 * wq + 2 * wv :] = dba.astype(bf16)
        dba_ref[rows, :] = dba
        dprm_ref[0:1, :] += jnp.sum(ddecay * q.decay, axis=0, keepdims=True)
        dprm_ref[1:2, :] += jnp.sum(drate, axis=0, keepdims=True)
        to = 0
        for parts, z, sg, c, tap in zip(dz, q.z, q.sig, q.raw, q.taps):
            d = jnp.concatenate(parts, axis=1) * (sg * (1.0 + z * (1.0 - sg)))
            width = tap.shape[0]
            w = c.shape[1]
            dc = d * tap[width - 1 : width]
            dtaps_ref[width - 1 : width, to : to + w] += jnp.sum(d * c, axis=0, keepdims=True)
            for s in range(1, width):
                m = jnp.where(pos >= s, d, 0.0)
                dc = dc + pltpu.roll(m, SEQ - s, 0) * tap[width - 1 - s : width - s]
                dtaps_ref[width - 1 - s : width - s, to : to + w] += jnp.sum(m * pltpu.roll(c, s, 0), axis=0, keepdims=True)
            dp_ref[rows, to : to + w] = dc.astype(bf16)
            to += w


def shared_specs(dims, off=0):
    nh, dk, dv = dims
    wq, wv = nh // SPLIT * dk, nh // SPLIT * dv
    at = (2 * wq) // wv
    small = (2 * wq + 2 * wv) // 128
    return [
        pl.BlockSpec((ROWS, wq), lambda i: (i + off, 0)),
        pl.BlockSpec((ROWS, wq), lambda i: (i + off, 1)),
        pl.BlockSpec((ROWS, wv), lambda i: (i + off, at)),
        pl.BlockSpec((ROWS, wv), lambda i: (i + off, at + 1)),
        pl.BlockSpec((ROWS, 128), lambda i: (i + off, small)),
        pl.BlockSpec((ROWS, 1), lambda i: (i + off, 0)),
        pl.BlockSpec((4, 2 * wq + wv), lambda i: (0, 0)),
        pl.BlockSpec((1, dv), lambda i: (0, 0)),
        pl.BlockSpec((8, 128), lambda i: (0, 0)),
    ]


def cost(us):
    return pl.CostEstimate(flops=int(us * 1.1e9), bytes_accessed=int(us * 1e6), transcendentals=0)


def mixer_fwd(proj, first, pos, taps, gain, prm, dims, half, part=None, filled=()):
    tok = pos.shape[0]
    nh, dk, dv = dims
    hs = nh // SPLIT
    ns = tok // SEQ
    wv = hs * dv
    steps = ns // PAIR if part is None else ns // PAIR // 2
    off = part * steps if part else 0
    row = pl.BlockSpec((ROWS, wv), lambda i: (i + off, 0))
    args = [proj, proj, proj, proj, first, pos, taps, gain, prm, *filled]
    return pl.pallas_call(
        functools.partial(fwd_kernel, dims, half),
        grid=(steps,),
        in_specs=shared_specs(dims, off) + [pl.BlockSpec(memory_space=pl.ANY)] * len(filled),
        out_specs=[
            pl.BlockSpec((ROWS, wv), lambda i: (i + off, half)),
            pl.BlockSpec((PAIR * hs, SEQ, SEQ), lambda i: (i + off, 0, 0)),
            row,
            row,
        ],
        out_shape=[
            jax.ShapeDtypeStruct((tok, nh * dv), bf16),
            jax.ShapeDtypeStruct((ns * hs, SEQ, SEQ), f32),
            jax.ShapeDtypeStruct((tok, wv), f32),
            jax.ShapeDtypeStruct((tok, wv), f32),
        ],
        input_output_aliases={9 + i: i for i in range(len(filled))},
        cost_estimate=cost(4 if part is None else 12),
        compiler_params=pltpu.CompilerParams(vmem_limit_bytes=48 << 20),
    )(*args)


def mixer_bwd(proj, first, pos, taps, gain, prm, x, u, o, dm, dims, half, part, before=None, filled=None):
    tok = pos.shape[0]
    nh, dk, dv = dims
    hs = nh // SPLIT
    ns = tok // SEQ
    wq, wv = hs * dk, hs * dv
    steps = dm.shape[0] // ROWS
    off = part * steps
    row = pl.BlockSpec((ROWS, wv), lambda i: (i + off, 0))
    lanes = pl.BlockSpec((ROWS, 128), lambda i: (i + off, 0))
    specs = shared_specs(dims, off) + [
        pl.BlockSpec((PAIR * hs, SEQ, SEQ), lambda i: (i + off, 0, 0)), row, row, pl.BlockSpec((ROWS, wv), lambda i: (i, half))]
    args = [proj, proj, proj, proj, first, pos, taps, gain, prm, x, u, o, dm]
    width = 2 * wq + 2 * wv
    if before is not None:
        args.append(before)
        specs.append(lanes)
        width += 128
    alias = {}
    if filled is not None:
        alias = {len(args): 0, len(args) + 1: 1}
        args += filled
        specs += [pl.BlockSpec(memory_space=pl.ANY)] * 2
    return pl.pallas_call(
        functools.partial(bwd_kernel, dims, half, before is not None),
        grid=(steps,),
        in_specs=specs,
        out_specs=[
            pl.BlockSpec((ROWS, width), lambda i: (i + off, 0)),
            lanes,
            pl.BlockSpec((4, 2 * wq + wv), lambda i: (0, 0)),
            pl.BlockSpec((1, dv), lambda i: (0, 0)),
            pl.BlockSpec((8, 128), lambda i: (0, 0)),
        ],
        out_shape=[
            jax.ShapeDtypeStruct((tok, width), bf16),
            jax.ShapeDtypeStruct((tok, 128), f32),
            jax.ShapeDtypeStruct((4, 2 * wq + wv), f32),
            jax.ShapeDtypeStruct((1, dv), f32),
            jax.ShapeDtypeStruct((8, 128), f32),
        ],
        input_output_aliases=alias,
        cost_estimate=cost(26),
        compiler_params=pltpu.CompilerParams(vmem_limit_bytes=56 << 20),
    )(*args)


def xor_send(value, axis, size, step):
    return lax.ppermute(value, axis, [(i, i ^ step) for i in range(size)])


def after(value, *needs):
    return lax.optimization_barrier((value, *needs))[0]


def lines(size):
    return [[low + 2 * i for i in range(size // 2)] for low in range(2)]


def gather_line(rows, size):
    return lax.all_gather(rows, "fsdp", axis=0, tiled=True, axis_index_groups=lines(size))


def gather_side(near, size, *needs):
    got = xor_send(after(near, *needs) if needs else near, "fsdp", size, 1)
    return jnp.concatenate([near, got], axis=0), got


def gather_side_first(rows, size, *needs):
    got = xor_send(after(rows, *needs), "fsdp", size, 1)
    full = gather_line(jnp.concatenate([rows, got], axis=0), size)
    width = rows.shape[1]
    return full.reshape(size // 2, 2, -1, width).swapaxes(0, 1).reshape(-1, width), full, got


def dot(left, right, dims=NN, out=f32):
    return lax.dot_general(left, right, dims, preferred_element_type=f32).astype(out)


class Summed:
    def __init__(self, left, right, size, *needs):
        self.size = size
        self.half = left.shape[1] // 2
        self.left, self.right = left, right
        self.sent = dot(left[:, self.half :], right, TN, bf16)
        self.got = xor_send(after(self.sent, *needs) if needs else self.sent, "fsdp", size, 1)

    def side(self, *needs, before=()):
        keep = dot(self.left[:, : self.half], after(self.right, *needs) if needs else self.right, TN)
        self.low = (keep + self.got.astype(f32)).astype(bf16)
        ready = after(self.low, *before) if before else self.low
        self.sum = lax.psum_scatter(ready, "fsdp", scatter_dimension=0, tiled=True, axis_index_groups=lines(self.size))

    def total(self, ranks):
        return lax.all_to_all(self.sum.reshape(ranks, -1, self.sum.shape[1]), "rep", 0, 0)


def join_tokens(rows, size):
    half = size // 2

    def around(block):
        held = {0: block}
        step = half // 2
        while step:
            for j in list(held):
                held[j ^ step] = xor_send(held[j], "rep", size, step)
            step //= 2
        return jnp.concatenate([held[j] for j in range(half)], axis=0)

    beyond = xor_send(rows, "rep", size, half)
    return around(rows), around(beyond), beyond


def sum_tokens(far, near, size, *needs, last=False):
    half = size // 2

    def around(part, *first):
        held = jnp.split(part, half, axis=0)
        step = 1
        while step < half:
            for j in range(0, half, 2 * step):
                low = held[j + step].astype(bf16)
                held[j] = held[j] + xor_send(after(low, *first) if first else low, "rep", size, step).astype(f32)
            step *= 2
        return held[0]

    beyond = around(far()).astype(bf16)
    part = near(beyond)
    if needs:
        beyond = after(beyond, *needs)
    got = xor_send(beyond, "rep", size, half)
    return around(part, *([got] if last else [])) + got.astype(f32), got


def rms(values):
    return lax.rsqrt(jnp.mean(values * values, axis=-1, keepdims=True) + 1e-06)


def norm_back(n, r, gain, dout):
    scaled = dout * gain
    return r * (scaled - n * jnp.mean(n * scaled, axis=-1, keepdims=True)), jnp.sum(dout * n, axis=0)


def make(F, R):
    both = ("fsdp", "rep")

    def on_device(tokens, segments, cotangent, gain_one, w_query, w_key, w_value, w_gate, w_beta, w_alpha, conv_q, conv_k,
                  conv_v, a_log, dt_bias, norm_gain, w_out, gain_two, w_ffgate, w_ffup, w_down):
        f = lax.axis_index("fsdp")
        r = lax.axis_index("rep")
        N = F * R
        rows_own, D = tokens.shape
        heads = a_log.shape[0]
        dk = w_query.shape[1] // heads
        dv = w_value.shape[1] // heads
        nh = heads // R
        dims = (nh, dk, dv)
        wq, wv = nh * dk, nh * dv
        hq, hv = wq // SPLIT, wv // SPLIT
        shard = D // N
        block = D // F
        ffq = w_ffgate.shape[1] // R
        tok = rows_own * R
        ns = tok // SEQ
        tiny = dv // N
        per = conv_v.shape[1] // shard

        low_bit = f & 1

        def swap(array, axis):
            half = array.shape[axis] // 2
            return jnp.concatenate(
                [lax.dynamic_slice_in_dim(array, (low_bit ^ j) * half, half, axis=axis) for j in range(2)], axis=axis)

        def mix(array, axis):
            at = [slice(None)] * array.ndim
            parts = []
            for bit in range(2):
                for i in range(F // 2):
                    at[axis] = slice((2 * i + bit) * block, (2 * i + bit + 1) * block)
                    parts.append(array[tuple(at)])
            return swap(jnp.concatenate(parts, axis=axis), axis)

        def unmix(array, axis):
            array = swap(array, axis)
            at = [slice(None)] * array.ndim
            parts = []
            for i in range(F // 2):
                for bit in range(2):
                    p = bit * (F // 2) + i
                    at[axis] = slice(p * block, (p + 1) * block)
                    parts.append(array[tuple(at)])
            return jnp.concatenate(parts, axis=axis)

        def quarter(arrays):
            return jnp.concatenate([a.reshape(shard, R, -1) for a in arrays], axis=2)

        def spread(packed, *needs):
            packed = packed.transpose(1, 0, 2)
            if needs:
                packed = after(packed, *needs)
            return lax.all_to_all(packed, "rep", 0, 0).reshape(R * shard, -1)

        extra = jnp.concatenate(
            [gain_one[:, None], gain_two[:, None], conv_q.T, conv_k.T,
             conv_v.reshape(4, shard, per).transpose(1, 0, 2).reshape(shard, 4 * per),
             jnp.pad(norm_gain, (0, shard - tiny))[:, None]], axis=1).T
        small = jnp.concatenate([w_beta.reshape(shard, R, nh), w_alpha.reshape(shard, R, nh)], axis=2)
        small = jnp.pad(small, ((0, 0), (0, 0), (0, 128 - 2 * nh)))

        def halves(array, width):
            parts = array.reshape(shard, R, SPLIT, width)
            return [parts[:, :, h] for h in range(SPLIT)]

        q_h, k_h, v_h, g_h = halves(w_query, hq), halves(w_key, hq), halves(w_value, hv), halves(w_gate, hv)
        own = mix(tokens, 1)
        part_a = spread(jnp.concatenate([q_h[0], k_h[0], v_h[0], g_h[0], small, q_h[1], k_h[1], v_h[1], g_h[1]], axis=2))
        w1 = 2 * hq + 2 * hv
        part_a = after(part_a, own)
        part_1, part_2 = part_a[:, : w1 + 128], part_a[:, w1 + 128 :]
        extra_all = lax.all_to_all(jnp.broadcast_to(after(extra, part_a)[None], (N, *extra.shape)), both, 0, 0)
        extra_all = extra_all.transpose(1, 0, 2).reshape(-1, D).astype(f32)
        line_1 = gather_line(part_1, F)
        every_near, every_far, every_got = join_tokens(own, R)
        every = jnp.concatenate([every_near, every_far], axis=0)
        ids_all = jnp.concatenate(join_tokens(segments[:, None], R)[:2], axis=0).reshape(ns, SEQ)
        part_r = spread(quarter([w_out.T, w_ffgate, w_ffup, w_down.T]), extra_all, every_got, line_1)
        part_b, part_gu, part_d = part_r[:, :wv], part_r[:, wv : wv + 2 * ffq], part_r[:, wv + 2 * ffq :]
        line_2 = gather_line(after(part_2, extra_all), F)
        wa1, side_1 = gather_side(line_1, F)
        cot = mix(cotangent, 1)
        cot_near, cot_far, unused = join_tokens(after(cot, side_1), R)
        line_b = gather_line(part_b, F)
        line_gu = gather_line(part_gu, F)

        gains = mix(extra_all[:2], 1)
        gain_first, gain_second = gains[0:1], gains[1:2]
        cq = lax.dynamic_slice_in_dim(extra_all[2:6], r * wq, wq, axis=1)
        ck = lax.dynamic_slice_in_dim(extra_all[6:10], r * wq, wq, axis=1)
        cv = extra_all[10 : 10 + 4 * per].reshape(4, per, D).transpose(0, 2, 1).reshape(4, D * per)
        cv = lax.dynamic_slice_in_dim(cv, r * wv, wv, axis=1)
        gain_out = extra_all[10 + 4 * per].reshape(N, shard)[:, :tiny].reshape(1, dv)
        taps = [jnp.concatenate([cq[:, h * hq : (h + 1) * hq], ck[:, h * hq : (h + 1) * hq], cv[:, h * hv : (h + 1) * hv]], axis=1)
                for h in range(SPLIT)]
        prm = jnp.stack([jnp.exp(lax.dynamic_slice_in_dim(a_log, r * nh, nh)), lax.dynamic_slice_in_dim(dt_bias, r * nh, nh)])
        prm = jnp.pad(prm, ((0, 6), (nh, 128 - 2 * nh)))
        place = jnp.arange(SEQ)
        same = (ids_all[:, :, None] == ids_all[:, None, :]) & (place[:, None] >= place[None, :])[None]
        pos = (jnp.sum(same.astype(f32), axis=2) - 1.0).reshape(tok, 1)

        every32 = every.astype(f32)
        normed_one = (every32 * rms(every32) * gain_first).astype(bf16)
        proj_1 = dot(after(normed_one, line_2, part_r), wa1)
        mixed, x_1, u_1, o_1 = mixer_fwd(proj_1, proj_1, pos, taps[0], gain_out, prm, dims, 0)
        wa2, side_2 = gather_side(line_2, F, side_1)
        proj_2 = dot(after(normed_one, mixed, line_b), wa2)
        mixed, *saved_2 = mixer_fwd(proj_2, proj_1, pos, taps[1], gain_out, prm, dims, 1, 1, [mixed])
        wd, line_d, got_d = gather_side_first(part_d, F, side_2)
        wb, side_b = gather_side(line_b, F, side_2)
        side_gu = xor_send(after(line_gu, side_b), "fsdp", F, 1)
        wg, wu = (jnp.concatenate([line_gu[:, at : at + ffq], side_gu[:, at : at + ffq]], axis=0) for at in (0, ffq))
        own32 = own.astype(f32)
        mid = tok // 2
        mixed = after(mixed, line_gu, got_d, cot_near, cot_far)
        out_far = dot(mixed[mid:], wb, NT)
        kept = {}

        def keep(name, value):
            kept[name] = value
            return value

        def near_mixed(part):
            kept["mixed"], *kept["saved"] = mixer_fwd(
                proj_2, proj_1, after(pos, part), taps[1], gain_out, prm, dims, 1, 0, [mixed, *saved_2])
            return dot(kept["mixed"][:mid], wb, NT)

        added, unused = sum_tokens(lambda: out_far, near_mixed, R, last=True)
        mixed, saved_2 = kept["mixed"], kept["saved"]
        middle = own32 + added
        r2 = rms(middle)
        n2 = middle * r2
        normed_own = (n2 * gain_second).astype(bf16)
        two = join_tokens(normed_own, R)[:2]
        gates, ups, acts, sigs, hiddens = [], [], [], [], []
        for normed in two:
            gates.append(dot(normed, wg))
            ups.append(dot(after(normed, gates[-1], line_d) if ups else normed, wu))
            sigs.append(jax.nn.sigmoid(gates[-1]))
            acts.append(gates[-1] * sigs[-1])
            hiddens.append((acts[-1] * ups[-1]).astype(bf16))
        hidden = jnp.concatenate(hiddens, axis=0)
        normed_two = jnp.concatenate(two, axis=0)
        cot_all = jnp.concatenate([cot_near, cot_far], axis=0)

        g_down = Summed(cot_all, hidden, F)
        dgates, dups = [None, None], [None, None]

        def back_two(t, *needs):
            dhidden = dot(after((cot_near, cot_far)[t], *needs), wd)
            dgates[t] = (dhidden * ups[t] * (sigs[t] * (1.0 + gates[t] * (1.0 - sigs[t])))).astype(bf16)
            dups[t] = (dhidden * acts[t]).astype(bf16)
            return dot(dgates[t], wg, NT) + dot(dups[t], wu, NT)

        dnormed_two, far_two = sum_tokens(lambda: back_two(1, g_down.sent), lambda part: keep("two", back_two(0, part)), R)
        g_down.side(kept["two"])
        g_gate = Summed(normed_two, after(jnp.concatenate(dgates, axis=0), g_down.low), F, g_down.got)
        dinner, dgain_second = norm_back(n2, r2, gain_second, after(dnormed_two, g_gate.sent))
        dmiddle = cot.astype(f32) + dinner
        dmiddle_own = dmiddle.astype(bf16)
        dlow = join_tokens(dmiddle_own, R)[:2]
        dm_near = dot(dlow[0], wb)
        args_2 = (proj_2, proj_1, pos, taps[1], gain_out, prm, *saved_2)
        args_1 = (proj_1, proj_1, pos, taps[0], gain_out, prm, x_1, u_1, o_1)
        dp_2, dba, dt_2, dg_2, dr_2 = mixer_bwd(*args_2, dm_near, dims, 1, 0)
        g_up = Summed(normed_two, after(jnp.concatenate(dups, axis=0), dba), F, g_gate.got)
        g_gate.side(g_up.sent)
        dp_1, dba_1, dt_1, dg_1, dr_1 = mixer_bwd(*args_1, after(dm_near, g_gate.low, g_down.sum), dims, 0, 0, dba)
        t_down = g_down.total(R)
        g_out = Summed(jnp.concatenate(dlow, axis=0), after(mixed, dba_1), F)
        dm_far = dot(after(dlow[1], dba_1), wb)
        dp_2, dba, et_2, eg_2, er_2 = mixer_bwd(*args_2, after(dm_far, g_out.sent), dims, 1, 1, None, [dp_2, dba])
        g_up.side(dba)
        g_2 = Summed(normed_one, after(dp_2, g_up.low, g_gate.sum), F)
        t_gate = g_gate.total(R)
        dp_1, dba_1, et_1, eg_1, er_1 = mixer_bwd(
            *args_1, after(dm_far, g_2.sent, t_down), dims, 0, 1, dba, [dp_1, dba_1])
        g_out.side(dp_1)
        g_1 = Summed(normed_one, after(dp_1, g_out.low), F)
        t_up = g_up.total(R)

        def back_one(lo, hi, *needs):
            return dot(after(dp_1, *needs)[lo:hi], wa1, NT) + dot(after(dp_2, *needs)[lo:hi], wa2, NT)

        t_out = g_out.total(R)

        def near_one(part):
            g_2.side(part, g_out.sum)

            keep("far", dot(after(hiddens[1], g_2.low, t_up), wd, NT))
            return keep("one", back_one(0, mid, kept["far"]))

        dnormed_one, far_one = sum_tokens(lambda: back_one(mid, tok, g_1.sent, g_up.sum, t_gate), near_one, R)
        g_1.side(kept["one"], before=(g_2.sum,))
        added, unused = sum_tokens(lambda: kept["far"], lambda part: dot(after(hiddens[0], g_1.low, t_out), wd, NT), R)
        layer_out = (middle + after(added, g_1.sum)).astype(bf16)
        dprm = dr_1 + dr_2 + er_1 + er_2
        dgain_out = dg_1 + dg_2 + eg_1 + eg_2
        dtaps = [dt_1 + et_1, dt_2 + et_2]

        n1 = own32 * rms(own32)
        dfirst, dgain_first = norm_back(n1, rms(own32), gain_first, dnormed_one)
        grad_tokens = unmix(dmiddle + dfirst, 1)

        def wide(parts):
            return parts.astype(f32).transpose(1, 0, 2).reshape(shard, -1)

        def tall(parts):
            return parts.astype(f32).transpose(0, 2, 1).reshape(-1, shard)

        t_2 = g_2.total(R)
        t_1 = g_1.total(R)

        def joined(lo, width):
            return jnp.stack([t[:, :, lo : lo + width] for t in (t_1, t_2)], axis=2).astype(f32).transpose(1, 0, 2, 3).reshape(shard, -1)

        grad_query, grad_key = joined(0, hq), joined(hq, hq)
        grad_value, grad_gate_w = joined(2 * hq, hv), joined(2 * hq + hv, hv)
        grad_beta, grad_alpha = wide(t_1[:, :, w1 : w1 + nh]), wide(t_1[:, :, w1 + nh : w1 + 2 * nh])
        grad_down, grad_out = tall(t_down), tall(t_out)
        grad_gate, grad_up = wide(t_gate), wide(t_up)

        def placed(parts, total, width):
            part = jnp.concatenate(parts, axis=1)
            return lax.dynamic_update_slice(jnp.zeros((4, total), f32), part, (0, r * width))

        gq = placed([dtaps[h][:, :hq] for h in range(SPLIT)], R * wq, wq)
        gk = placed([dtaps[h][:, hq : 2 * hq] for h in range(SPLIT)], R * wq, wq)
        gv = placed([dtaps[h][:, 2 * hq :] for h in range(SPLIT)], R * wv, wv)
        heads_part = lax.dynamic_update_slice(jnp.zeros((2, heads), f32), dprm[:2, nh : 2 * nh], (0, r * nh)).reshape(1, -1)
        packed = jnp.concatenate([
            unmix(dgain_first[None], 1).reshape(N, -1),
            unmix(dgain_second[None], 1).reshape(N, -1),
            gq.reshape(4, N, -1).transpose(1, 0, 2).reshape(N, -1),
            gk.reshape(4, N, -1).transpose(1, 0, 2).reshape(N, -1),
            gv.reshape(4, N, -1).transpose(1, 0, 2).reshape(N, -1),
            dgain_out.reshape(N, tiny),
            jnp.broadcast_to(heads_part, (N, 2 * heads))], axis=1)
        summed = jnp.sum(lax.all_to_all(packed, both, 0, 0, tiled=True), axis=0)
        sizes = [shard, shard, 4 * shard, 4 * shard, 4 * shard * per, tiny, heads, heads]
        ends = [0]
        for size in sizes:
            ends.append(ends[-1] + size)
        pick = [summed[ends[i] : ends[i + 1]] for i in range(len(sizes))]
        return (
            unmix(layer_out, 1), grad_tokens, pick[0], grad_query, grad_key, grad_value, grad_gate_w, grad_beta, grad_alpha,
            pick[2].reshape(4, shard), pick[3].reshape(4, shard), pick[4].reshape(4, shard * per), pick[6], pick[7], pick[5],
            grad_out, pick[1], grad_gate, grad_up, grad_down)

    return on_device


def solution(mesh):
    rows, cols, flat = P(("fsdp", "rep"), None), P(None, ("fsdp", "rep")), P(("fsdp", "rep"))
    placed = (rows, flat, rows, flat, rows, rows, rows, rows, rows, rows, cols, cols, cols, P(), P(), flat, cols, flat, rows, rows, cols)
    made = (rows, rows, flat, rows, rows, rows, rows, rows, rows, cols, cols, cols, P(), P(), flat, cols, flat, rows, rows, cols)
    return jax.shard_map(
        make(mesh.shape["fsdp"], mesh.shape["rep"]), mesh=mesh, in_specs=placed, out_specs=made, check_vma=False)
```

```python
import functools

import jax
import jax.numpy as jnp
from jax import lax
from jax.experimental import pallas as pl
from jax.experimental.pallas import tpu as pltpu
from jax.sharding import PartitionSpec as P

SEQ = 256
SPLIT = 2
PAIR = 2
ROWS = PAIR * SEQ

f32 = jnp.float32
bf16 = jnp.bfloat16
NN = (((1,), (0,)), ((), ()))
NT = (((1,), (1,)), ((), ()))
TN = (((0,), (0,)), ((), ()))


def split(a):
    hi = a.astype(bf16)
    return hi, (a - hi.astype(f32)).astype(bf16)


def one(a, b, dims):
    return lax.dot_general(a.astype(bf16), b.astype(bf16), dims, preferred_element_type=f32)


def three(a, b, dims):
    ah, al = split(a)
    bh, bl = split(b)
    out = lax.dot_general(ah, bl, dims, preferred_element_type=f32)
    out = out + lax.dot_general(al, bh, dims, preferred_element_type=f32)
    return out + lax.dot_general(ah, bh, dims, preferred_element_type=f32)


def exact_left(a, b, dims):
    bh, bl = split(b)
    a = a.astype(bf16)
    return lax.dot_general(a, bh, dims, preferred_element_type=f32) + lax.dot_general(a, bl, dims, preferred_element_type=f32)


def exact_right(a, b, dims):
    ah, al = split(a)
    b = b.astype(bf16)
    return lax.dot_general(ah, b, dims, preferred_element_type=f32) + lax.dot_general(al, b, dims, preferred_element_type=f32)


def sigmoid(v):
    return 1.0 / (1.0 + jnp.exp(-v))


def conv(c, taps, pos):
    width = taps.shape[0]
    z = c * taps[width - 1 : width]
    for s in range(1, width):
        z = z + jnp.where(pos >= s, pltpu.roll(c, s, 0), 0.0) * taps[width - 1 - s : width - s]
    return z


def unit(c):
    r = lax.rsqrt(jnp.sum(c * c, axis=-1, keepdims=True) + 1e-6)
    return c * r, r


def inverses(n_list, iota_r, iota_c):
    size = n_list[0].shape[0]
    eye = (iota_r == iota_c).astype(f32)
    xs = None
    b = 1
    while b < size:
        mask = ((iota_r // (2 * b)) == (iota_c // (2 * b))) & ((iota_r // b) % 2 == 1) & ((iota_c // b) % 2 == 0)
        cs = [jnp.where(mask, n, 0.0) for n in n_list]
        if xs is None:
            xs = [eye - c for c in cs]
        else:
            low = [x.astype(bf16) for x in xs]
            t = [one(c, x, NN) for c, x in zip(cs, low)]
            xs = [x - one(y, z, NN) for x, y, z in zip(xs, low, t)]
        b *= 2
    left = [(eye - x) - three(n, x, NN) for n, x in zip(n_list, xs)]
    return [x + one(x, r, NN) for x, r in zip(xs, left)]


def rates(pba, prm, tri):
    beta = sigmoid(pba)
    rate = pba + prm[1:2]
    decay = -prm[0:1] * (jnp.maximum(rate, 0.0) + jnp.log1p(jnp.exp(-jnp.abs(rate))))
    return beta, rate, decay, exact_left(tri, decay, NN), exact_right(decay, tri, (((0,), (1,)), ((), ())))


class Sequence:
    def __init__(self, dims, half, refs, rows, iota_r, iota_c, tri):
        pq_ref, pk_ref, pv_ref, pg_ref, ba_ref, pos_ref, taps_ref, gain_ref, prm_ref = refs
        nh, dk, dv = dims
        hs = nh // SPLIT
        wq = hs * dk
        at = half * hs
        H = range(hs)
        self.rows = rows
        self.pos = pos_ref[rows, :]
        taps = taps_ref[...]
        self.taps = (taps[:, :wq], taps[:, wq : 2 * wq], taps[:, 2 * wq :])
        self.raw = (pq_ref[rows, :], pk_ref[rows, :], pv_ref[rows, :])
        self.beta, self.rate, self.decay, gcol, grow = rates(ba_ref[rows, :], prm_ref[...], tri)
        self.z = tuple(conv(c, t, self.pos) for c, t in zip(self.raw, self.taps))
        self.sig = tuple(sigmoid(z) for z in self.z)
        qc, kc, self.v = (z * g for z, g in zip(self.z, self.sig))
        live = (iota_c <= iota_r) & (iota_c >= iota_r - self.pos.astype(jnp.int32))
        self.bs = [self.beta[:, at + h : at + h + 1] for h in H]
        self.uq = [unit(qc[:, h * dk : (h + 1) * dk]) for h in H]
        self.uk = [unit(kc[:, h * dk : (h + 1) * dk]) for h in H]
        self.qs = [a * dk ** -0.5 for a, _ in self.uq]
        self.ks = [a for a, _ in self.uk]
        lane = nh + at
        self.ls = [
            jnp.where(live, jnp.exp(jnp.where(live, gcol[:, lane + h : lane + h + 1] - grow[lane + h : lane + h + 1, :], 0.0)), 0.0)
            for h in H]


def planes(n):
    iota_r = lax.broadcasted_iota(jnp.int32, (n, n), 0)
    iota_c = lax.broadcasted_iota(jnp.int32, (n, n), 1)
    return iota_r, iota_c, (iota_c <= iota_r).astype(f32), iota_c < iota_r


def fwd_kernel(dims, half, *refs):
    shared, (out_ref, x_ref, u_ref, o_ref) = refs[:9], refs[-4:]
    pg_ref, gain_ref = refs[3], refs[7]
    nh, dk, dv = dims
    hs = nh // SPLIT
    iota_r, iota_c, tri, strict = planes(SEQ)
    gain = gain_ref[...]
    seqs = [Sequence(dims, half, shared, slice(i * SEQ, (i + 1) * SEQ), iota_r, iota_c, tri) for i in range(out_ref.shape[0] // SEQ)]
    units = [(i, h) for i in range(len(seqs)) for h in range(hs)]
    ms = [three(seqs[i].ks[h], seqs[i].ks[h], NT) for i, h in units]
    ns = [jnp.where(strict, seqs[i].bs[h] * seqs[i].ls[h] * m, 0.0) for (i, h), m in zip(units, ms)]
    xs = inverses(ns, iota_r, iota_c)
    us = [three(x, seqs[i].bs[h] * seqs[i].v[:, h * dv : (h + 1) * dv], NN) for (i, h), x in zip(units, xs)]
    ps = [seqs[i].ls[h] * three(seqs[i].qs[h], seqs[i].ks[h], NT) for i, h in units]
    os = [three(p, u, NN) for p, u in zip(ps, us)]
    for (i, h), x, u, o in zip(units, xs, us, os):
        rows, sl = seqs[i].rows, slice(h * dv, (h + 1) * dv)
        x_ref[i * hs + h] = x
        u_ref[rows, sl] = u
        o_ref[rows, sl] = o
        r = lax.rsqrt(jnp.mean(o * o, axis=-1, keepdims=True) + 1e-5)
        pg = pg_ref[rows, sl]
        out_ref[rows, sl] = (o * r * gain * (pg * sigmoid(pg))).astype(bf16)


def bwd_kernel(dims, half, has_before, *refs):
    shared, (x_ref, u_ref, o_ref, dm_ref) = refs[:9], refs[9:13]
    dp_ref, dba_ref, dtaps_ref, dgain_ref, dprm_ref = refs[-5:]
    pg_ref, gain_ref, prm_ref = refs[3], refs[7], refs[8]
    nh, dk, dv = dims
    hs = nh // SPLIT
    wq, wv = hs * dk, hs * dv
    at = half * hs
    iota_r, iota_c, tri, strict = planes(SEQ)
    gain = gain_ref[...]
    prm = prm_ref[...]
    seqs = [Sequence(dims, half, shared, slice(i * SEQ, (i + 1) * SEQ), iota_r, iota_c, tri) for i in range(dm_ref.shape[0] // SEQ)]
    units = [(i, h) for i in range(len(seqs)) for h in range(hs)]
    dgain = jnp.zeros_like(gain)
    dos, us = [], []
    for i, h in units:
        rows, sl = seqs[i].rows, slice(h * dv, (h + 1) * dv)
        o = o_ref[rows, sl]
        pg = pg_ref[rows, sl]
        dm = dm_ref[rows, sl]
        r = lax.rsqrt(jnp.mean(o * o, axis=-1, keepdims=True) + 1e-5)
        nrm = o * r
        sg = sigmoid(pg)
        dp_ref[rows, 2 * wq + wv + h * dv : 2 * wq + wv + (h + 1) * dv] = (dm * nrm * gain * (sg * (1.0 + pg * (1.0 - sg)))).astype(bf16)
        dy = dm * (pg * sg)
        dgain = dgain + jnp.sum(dy * nrm, axis=0, keepdims=True)
        dn = dy * gain
        dos.append(r * (dn - nrm * jnp.mean(nrm * dn, axis=-1, keepdims=True)))
        us.append(u_ref[rows, sl])
    bm = [jnp.where(strict, seqs[i].ls[h] * three(seqs[i].ks[h], seqs[i].ks[h], NT), 0.0) for i, h in units]
    ps = [seqs[i].ls[h] * three(seqs[i].qs[h], seqs[i].ks[h], NT) for i, h in units]
    dps = [three(do, u, NT) for do, u in zip(dos, us)]
    dus = [three(p, do, TN) for p, do in zip(ps, dos)]
    dws = [three(x_ref[i * hs + h], du, TN) for (i, h), du in zip(units, dus)]
    das = [-three(dw, u, NT) for dw, u in zip(dws, us)]

    @pl.when(pl.program_id(0) == 0)
    def _():
        dtaps_ref[...] = jnp.zeros_like(dtaps_ref)
        dgain_ref[...] = jnp.zeros_like(dgain_ref)
        dprm_ref[...] = jnp.zeros_like(dprm_ref)

    dgain_ref[...] += dgain
    lane = lax.broadcasted_iota(jnp.int32, (SEQ, 128), 1)
    ones = jnp.ones((SEQ, 128), f32)
    sc = dk ** -0.5
    for i, q in enumerate(seqs):
        rows, pos = q.rows, q.pos
        dbeta = jnp.zeros((SEQ, 128), f32)
        dlog = jnp.zeros((SEQ, 128), f32)
        dz = ([], [], [])
        for h in range(hs):
            n = i * hs + h
            vh = q.v[:, h * dv : (h + 1) * dv]
            ab = das[n] * bm[n]
            dbeta = jnp.where(lane == at + h, jnp.sum(dws[n] * vh, axis=-1, keepdims=True) + jnp.sum(ab, axis=-1, keepdims=True), dbeta)
            e = q.bs[h] * ab + dps[n] * ps[n]
            dlog = jnp.where(lane == nh + at + h, jnp.sum(e, axis=-1, keepdims=True) - exact_right(e, ones, TN), dlog)
            ds = dps[n] * q.ls[h]
            dmm = jnp.where(strict, q.bs[h] * das[n] * q.ls[h], 0.0)
            dq = sc * three(ds, q.ks[h], NN)
            dkh = three(ds, q.qs[h], TN) + three(dmm, q.ks[h], NN) + three(dmm, q.ks[h], TN)
            qh, rq = q.uq[h]
            kh, rk = q.uk[h]
            dz[0].append(rq * (dq - qh * jnp.sum(qh * dq, axis=-1, keepdims=True)))
            dz[1].append(rk * (dkh - kh * jnp.sum(kh * dkh, axis=-1, keepdims=True)))
            dz[2].append(q.bs[h] * dws[n])
        ddecay = exact_left(tri, dlog, TN)
        drate = -prm[0:1] * ddecay * sigmoid(q.rate)
        dba = dbeta * q.beta * (1.0 - q.beta) + drate
        if has_before:
            dba = dba + refs[13][rows, :]
            dp_ref[rows, 2 * wq + 2 * wv :] = dba.astype(bf16)
        dba_ref[rows, :] = dba
        dprm_ref[0:1, :] += jnp.sum(ddecay * q.decay, axis=0, keepdims=True)
        dprm_ref[1:2, :] += jnp.sum(drate, axis=0, keepdims=True)
        to = 0
        for parts, z, sg, c, tap in zip(dz, q.z, q.sig, q.raw, q.taps):
            d = jnp.concatenate(parts, axis=1) * (sg * (1.0 + z * (1.0 - sg)))
            width = tap.shape[0]
            w = c.shape[1]
            dc = d * tap[width - 1 : width]
            dtaps_ref[width - 1 : width, to : to + w] += jnp.sum(d * c, axis=0, keepdims=True)
            for s in range(1, width):
                m = jnp.where(pos >= s, d, 0.0)
                dc = dc + pltpu.roll(m, SEQ - s, 0) * tap[width - 1 - s : width - s]
                dtaps_ref[width - 1 - s : width - s, to : to + w] += jnp.sum(m * pltpu.roll(c, s, 0), axis=0, keepdims=True)
            dp_ref[rows, to : to + w] = dc.astype(bf16)
            to += w


def shared_specs(dims, off=0):
    nh, dk, dv = dims
    wq, wv = nh // SPLIT * dk, nh // SPLIT * dv
    at = (2 * wq) // wv
    small = (2 * wq + 2 * wv) // 128
    return [
        pl.BlockSpec((ROWS, wq), lambda i: (i + off, 0)),
        pl.BlockSpec((ROWS, wq), lambda i: (i + off, 1)),
        pl.BlockSpec((ROWS, wv), lambda i: (i + off, at)),
        pl.BlockSpec((ROWS, wv), lambda i: (i + off, at + 1)),
        pl.BlockSpec((ROWS, 128), lambda i: (i + off, small)),
        pl.BlockSpec((ROWS, 1), lambda i: (i + off, 0)),
        pl.BlockSpec((4, 2 * wq + wv), lambda i: (0, 0)),
        pl.BlockSpec((1, dv), lambda i: (0, 0)),
        pl.BlockSpec((8, 128), lambda i: (0, 0)),
    ]


def cost(us):
    return pl.CostEstimate(flops=int(us * 1.1e9), bytes_accessed=int(us * 1e6), transcendentals=0)


def mixer_fwd(proj, first, pos, taps, gain, prm, dims, half, part=None, filled=()):
    tok = pos.shape[0]
    nh, dk, dv = dims
    hs = nh // SPLIT
    ns = tok // SEQ
    wv = hs * dv
    steps = ns // PAIR if part is None else ns // PAIR // 2
    off = part * steps if part else 0
    row = pl.BlockSpec((ROWS, wv), lambda i: (i + off, 0))
    args = [proj, proj, proj, proj, first, pos, taps, gain, prm, *filled]
    return pl.pallas_call(
        functools.partial(fwd_kernel, dims, half),
        grid=(steps,),
        in_specs=shared_specs(dims, off) + [pl.BlockSpec(memory_space=pl.ANY)] * len(filled),
        out_specs=[
            pl.BlockSpec((ROWS, wv), lambda i: (i + off, half)),
            pl.BlockSpec((PAIR * hs, SEQ, SEQ), lambda i: (i + off, 0, 0)),
            row,
            row,
        ],
        out_shape=[
            jax.ShapeDtypeStruct((tok, nh * dv), bf16),
            jax.ShapeDtypeStruct((ns * hs, SEQ, SEQ), f32),
            jax.ShapeDtypeStruct((tok, wv), f32),
            jax.ShapeDtypeStruct((tok, wv), f32),
        ],
        input_output_aliases={9 + i: i for i in range(len(filled))},
        cost_estimate=cost(4 if part is None else 12),
        compiler_params=pltpu.CompilerParams(vmem_limit_bytes=48 << 20),
    )(*args)


def mixer_bwd(proj, first, pos, taps, gain, prm, x, u, o, dm, dims, half, part, before=None, filled=None):
    tok = pos.shape[0]
    nh, dk, dv = dims
    hs = nh // SPLIT
    ns = tok // SEQ
    wq, wv = hs * dk, hs * dv
    steps = dm.shape[0] // ROWS
    off = part * steps
    row = pl.BlockSpec((ROWS, wv), lambda i: (i + off, 0))
    lanes = pl.BlockSpec((ROWS, 128), lambda i: (i + off, 0))
    specs = shared_specs(dims, off) + [
        pl.BlockSpec((PAIR * hs, SEQ, SEQ), lambda i: (i + off, 0, 0)), row, row, pl.BlockSpec((ROWS, wv), lambda i: (i, half))]
    args = [proj, proj, proj, proj, first, pos, taps, gain, prm, x, u, o, dm]
    width = 2 * wq + 2 * wv
    if before is not None:
        args.append(before)
        specs.append(lanes)
        width += 128
    alias = {}
    if filled is not None:
        alias = {len(args): 0, len(args) + 1: 1}
        args += filled
        specs += [pl.BlockSpec(memory_space=pl.ANY)] * 2
    return pl.pallas_call(
        functools.partial(bwd_kernel, dims, half, before is not None),
        grid=(steps,),
        in_specs=specs,
        out_specs=[
            pl.BlockSpec((ROWS, width), lambda i: (i + off, 0)),
            lanes,
            pl.BlockSpec((4, 2 * wq + wv), lambda i: (0, 0)),
            pl.BlockSpec((1, dv), lambda i: (0, 0)),
            pl.BlockSpec((8, 128), lambda i: (0, 0)),
        ],
        out_shape=[
            jax.ShapeDtypeStruct((tok, width), bf16),
            jax.ShapeDtypeStruct((tok, 128), f32),
            jax.ShapeDtypeStruct((4, 2 * wq + wv), f32),
            jax.ShapeDtypeStruct((1, dv), f32),
            jax.ShapeDtypeStruct((8, 128), f32),
        ],
        input_output_aliases=alias,
        cost_estimate=cost(26),
        compiler_params=pltpu.CompilerParams(vmem_limit_bytes=56 << 20),
    )(*args)


def xor_send(value, axis, size, step):
    return lax.ppermute(value, axis, [(i, i ^ step) for i in range(size)])


def after(value, *needs):
    return lax.optimization_barrier((value, *needs))[0]


def lines(size):
    return [[low + 2 * i for i in range(size // 2)] for low in range(2)]


def gather_line(rows, size):
    return lax.all_gather(rows, "fsdp", axis=0, tiled=True, axis_index_groups=lines(size))


def gather_side(near, size, *needs):
    got = xor_send(after(near, *needs) if needs else near, "fsdp", size, 1)
    return jnp.concatenate([near, got], axis=0), got


def gather_side_first(rows, size, *needs):
    got = xor_send(after(rows, *needs), "fsdp", size, 1)
    full = gather_line(jnp.concatenate([rows, got], axis=0), size)
    width = rows.shape[1]
    return full.reshape(size // 2, 2, -1, width).swapaxes(0, 1).reshape(-1, width), full, got


def dot(left, right, dims=NN, out=f32):
    return lax.dot_general(left, right, dims, preferred_element_type=f32).astype(out)


class Summed:
    def __init__(self, left, right, size, *needs):
        self.size = size
        self.half = left.shape[1] // 2
        self.left, self.right = left, right
        self.sent = dot(left[:, self.half :], right, TN, bf16)
        self.got = xor_send(after(self.sent, *needs) if needs else self.sent, "fsdp", size, 1)

    def side(self, *needs, before=()):
        keep = dot(self.left[:, : self.half], after(self.right, *needs) if needs else self.right, TN)
        self.low = (keep + self.got.astype(f32)).astype(bf16)
        ready = after(self.low, *before) if before else self.low
        self.sum = lax.psum_scatter(ready, "fsdp", scatter_dimension=0, tiled=True, axis_index_groups=lines(self.size))

    def total(self, ranks):
        return lax.all_to_all(self.sum.reshape(ranks, -1, self.sum.shape[1]), "rep", 0, 0)


def join_tokens(rows, size):
    half = size // 2

    def around(block):
        held = {0: block}
        step = half // 2
        while step:
            for j in list(held):
                held[j ^ step] = xor_send(held[j], "rep", size, step)
            step //= 2
        return jnp.concatenate([held[j] for j in range(half)], axis=0)

    beyond = xor_send(rows, "rep", size, half)
    return around(rows), around(beyond), beyond


def sum_tokens(far, near, size, *needs, last=False):
    half = size // 2

    def around(part, *first):
        held = jnp.split(part, half, axis=0)
        step = 1
        while step < half:
            for j in range(0, half, 2 * step):
                low = held[j + step].astype(bf16)
                held[j] = held[j] + xor_send(after(low, *first) if first else low, "rep", size, step).astype(f32)
            step *= 2
        return held[0]

    beyond = around(far()).astype(bf16)
    part = near(beyond)
    if needs:
        beyond = after(beyond, *needs)
    got = xor_send(beyond, "rep", size, half)
    return around(part, *([got] if last else [])) + got.astype(f32), got


def rms(values):
    return lax.rsqrt(jnp.mean(values * values, axis=-1, keepdims=True) + 1e-06)


def norm_back(n, r, gain, dout):
    scaled = dout * gain
    return r * (scaled - n * jnp.mean(n * scaled, axis=-1, keepdims=True)), jnp.sum(dout * n, axis=0)


def make(F, R):
    both = ("fsdp", "rep")

    def on_device(tokens, segments, cotangent, gain_one, w_query, w_key, w_value, w_gate, w_beta, w_alpha, conv_q, conv_k,
                  conv_v, a_log, dt_bias, norm_gain, w_out, gain_two, w_ffgate, w_ffup, w_down):
        f = lax.axis_index("fsdp")
        r = lax.axis_index("rep")
        N = F * R
        rows_own, D = tokens.shape
        heads = a_log.shape[0]
        dk = w_query.shape[1] // heads
        dv = w_value.shape[1] // heads
        nh = heads // R
        dims = (nh, dk, dv)
        wq, wv = nh * dk, nh * dv
        hq, hv = wq // SPLIT, wv // SPLIT
        shard = D // N
        block = D // F
        ffq = w_ffgate.shape[1] // R
        tok = rows_own * R
        ns = tok // SEQ
        tiny = dv // N
        per = conv_v.shape[1] // shard

        low_bit = f & 1

        def swap(array, axis):
            half = array.shape[axis] // 2
            return jnp.concatenate(
                [lax.dynamic_slice_in_dim(array, (low_bit ^ j) * half, half, axis=axis) for j in range(2)], axis=axis)

        def mix(array, axis):
            at = [slice(None)] * array.ndim
            parts = []
            for bit in range(2):
                for i in range(F // 2):
                    at[axis] = slice((2 * i + bit) * block, (2 * i + bit + 1) * block)
                    parts.append(array[tuple(at)])
            return swap(jnp.concatenate(parts, axis=axis), axis)

        def unmix(array, axis):
            array = swap(array, axis)
            at = [slice(None)] * array.ndim
            parts = []
            for i in range(F // 2):
                for bit in range(2):
                    p = bit * (F // 2) + i
                    at[axis] = slice(p * block, (p + 1) * block)
                    parts.append(array[tuple(at)])
            return jnp.concatenate(parts, axis=axis)

        def quarter(arrays):
            return jnp.concatenate([a.reshape(shard, R, -1) for a in arrays], axis=2)

        def spread(packed, *needs):
            packed = packed.transpose(1, 0, 2)
            if needs:
                packed = after(packed, *needs)
            return lax.all_to_all(packed, "rep", 0, 0).reshape(R * shard, -1)

        extra = jnp.concatenate(
            [gain_one[:, None], gain_two[:, None], conv_q.T, conv_k.T,
             conv_v.reshape(4, shard, per).transpose(1, 0, 2).reshape(shard, 4 * per),
             jnp.pad(norm_gain, (0, shard - tiny))[:, None]], axis=1).T
        small = jnp.concatenate([w_beta.reshape(shard, R, nh), w_alpha.reshape(shard, R, nh)], axis=2)
        small = jnp.pad(small, ((0, 0), (0, 0), (0, 128 - 2 * nh)))

        def halves(array, width):
            parts = array.reshape(shard, R, SPLIT, width)
            return [parts[:, :, h] for h in range(SPLIT)]

        q_h, k_h, v_h, g_h = halves(w_query, hq), halves(w_key, hq), halves(w_value, hv), halves(w_gate, hv)
        own = mix(tokens, 1)
        part_a = spread(jnp.concatenate([q_h[0], k_h[0], v_h[0], g_h[0], small, q_h[1], k_h[1], v_h[1], g_h[1]], axis=2))
        w1 = 2 * hq + 2 * hv
        part_a = after(part_a, own)
        part_1, part_2 = part_a[:, : w1 + 128], part_a[:, w1 + 128 :]
        extra_all = lax.all_to_all(jnp.broadcast_to(after(extra, part_a)[None], (N, *extra.shape)), both, 0, 0)
        extra_all = extra_all.transpose(1, 0, 2).reshape(-1, D).astype(f32)
        line_1 = gather_line(part_1, F)
        every_near, every_far, every_got = join_tokens(own, R)
        every = jnp.concatenate([every_near, every_far], axis=0)
        ids_all = jnp.concatenate(join_tokens(segments[:, None], R)[:2], axis=0).reshape(ns, SEQ)
        part_r = spread(quarter([w_out.T, w_ffgate, w_ffup, w_down.T]), extra_all, every_got, line_1)
        gains = mix(extra_all[:2], 1)
        gain_first, gain_second = gains[0:1], gains[1:2]
        every32 = every.astype(f32)
        normed_one = (every32 * rms(every32) * gain_first).astype(bf16)
        part_r = after(part_r, normed_one)
        part_b, part_g, part_u, part_d = (
            part_r[:, :wv], part_r[:, wv : wv + ffq], part_r[:, wv + ffq : wv + 2 * ffq], part_r[:, wv + 2 * ffq :])
        line_2 = gather_line(after(part_2, extra_all), F)
        wa1, side_1 = gather_side(line_1, F)
        cot = mix(cotangent, 1)
        cot_near, cot_far, unused = join_tokens(after(cot, side_1), R)
        line_b = gather_line(part_b, F)
        line_g = gather_line(after(part_g, side_1), F)
        wu, line_u, got_u = gather_side_first(part_u, F, side_1)
        line_d = gather_line(after(part_d, side_1), F)

        cq = lax.dynamic_slice_in_dim(extra_all[2:6], r * wq, wq, axis=1)
        ck = lax.dynamic_slice_in_dim(extra_all[6:10], r * wq, wq, axis=1)
        cv = extra_all[10 : 10 + 4 * per].reshape(4, per, D).transpose(0, 2, 1).reshape(4, D * per)
        cv = lax.dynamic_slice_in_dim(cv, r * wv, wv, axis=1)
        gain_out = extra_all[10 + 4 * per].reshape(N, shard)[:, :tiny].reshape(1, dv)
        taps = [jnp.concatenate([cq[:, h * hq : (h + 1) * hq], ck[:, h * hq : (h + 1) * hq], cv[:, h * hv : (h + 1) * hv]], axis=1)
                for h in range(SPLIT)]
        prm = jnp.stack([jnp.exp(lax.dynamic_slice_in_dim(a_log, r * nh, nh)), lax.dynamic_slice_in_dim(dt_bias, r * nh, nh)])
        prm = jnp.pad(prm, ((0, 6), (nh, 128 - 2 * nh)))
        place = jnp.arange(SEQ)
        same = (ids_all[:, :, None] == ids_all[:, None, :]) & (place[:, None] >= place[None, :])[None]
        pos = (jnp.sum(same.astype(f32), axis=2) - 1.0).reshape(tok, 1)

        proj_1 = dot(after(normed_one, part_r), wa1)
        mixed, x_1, u_1, o_1 = mixer_fwd(proj_1, proj_1, pos, taps[0], gain_out, prm, dims, 0)
        wa2, side_2 = gather_side(line_2, F, side_1)
        proj_2 = dot(after(normed_one, mixed, line_b, got_u), wa2)
        mixed, *saved_2 = mixer_fwd(proj_2, proj_1, pos, taps[1], gain_out, prm, dims, 1, 1, [mixed])
        wb, side_b = gather_side(line_b, F, side_2)
        wg, side_g = gather_side(line_g, F, side_b)
        wd, side_d = gather_side(line_d, F, side_g)
        own32 = own.astype(f32)
        mid = tok // 2
        mixed = after(mixed, line_g, cot_near, cot_far)
        out_far = dot(mixed[mid:], wb, NT)
        kept = {}

        def keep(name, value):
            kept[name] = value
            return value

        def near_mixed(part):
            kept["mixed"], *kept["saved"] = mixer_fwd(
                proj_2, proj_1, after(pos, part), taps[1], gain_out, prm, dims, 1, 0, [mixed, *saved_2])
            return dot(kept["mixed"][:mid], wb, NT)

        added, unused = sum_tokens(lambda: out_far, near_mixed, R, last=True)
        mixed, saved_2 = kept["mixed"], kept["saved"]
        middle = own32 + after(added, side_g)
        r2 = rms(middle)
        n2 = middle * r2
        normed_own = (n2 * gain_second).astype(bf16)
        two = join_tokens(normed_own, R)[:2]
        gates, ups, acts, sigs, hiddens = [], [], [], [], []
        for normed in (after(two[0], line_u), two[1]):
            gates.append(dot(normed, wg))
            ups.append(dot(after(normed, gates[-1], side_d) if ups else normed, wu))
            sigs.append(jax.nn.sigmoid(gates[-1]))
            acts.append(gates[-1] * sigs[-1])
            hiddens.append((acts[-1] * ups[-1]).astype(bf16))
        hidden = jnp.concatenate(hiddens, axis=0)
        normed_two = jnp.concatenate(two, axis=0)
        cot_all = jnp.concatenate([cot_near, cot_far], axis=0)

        g_down = Summed(cot_all, hidden, F)
        dgates, dups = [None, None], [None, None]

        def back_two(t, *needs):
            dhidden = dot(after((cot_near, cot_far)[t], *needs), wd)
            dgates[t] = (dhidden * ups[t] * (sigs[t] * (1.0 + gates[t] * (1.0 - sigs[t])))).astype(bf16)
            dups[t] = (dhidden * acts[t]).astype(bf16)
            return dot(dgates[t], wg, NT) + dot(dups[t], wu, NT)

        dnormed_two, far_two = sum_tokens(lambda: back_two(1, g_down.sent), lambda part: keep("two", back_two(0, part)), R)
        g_down.side(kept["two"])
        g_gate = Summed(normed_two, after(jnp.concatenate(dgates, axis=0), g_down.low), F, g_down.got)
        dinner, dgain_second = norm_back(n2, r2, gain_second, after(dnormed_two, g_gate.sent))
        dmiddle = cot.astype(f32) + dinner
        dmiddle_own = dmiddle.astype(bf16)
        dlow = join_tokens(dmiddle_own, R)[:2]
        dm_near = dot(dlow[0], wb)
        args_2 = (proj_2, proj_1, pos, taps[1], gain_out, prm, *saved_2)
        args_1 = (proj_1, proj_1, pos, taps[0], gain_out, prm, x_1, u_1, o_1)
        dp_2, dba, dt_2, dg_2, dr_2 = mixer_bwd(*args_2, dm_near, dims, 1, 0)
        g_up = Summed(normed_two, after(jnp.concatenate(dups, axis=0), dba), F, g_gate.got)
        g_gate.side(g_up.sent)
        dp_1, dba_1, dt_1, dg_1, dr_1 = mixer_bwd(*args_1, after(dm_near, g_gate.low, g_down.sum), dims, 0, 0, dba)
        t_down = g_down.total(R)
        g_out = Summed(jnp.concatenate(dlow, axis=0), after(mixed, dba_1), F)
        dm_far = dot(after(dlow[1], dba_1), wb)
        dp_2, dba, et_2, eg_2, er_2 = mixer_bwd(*args_2, after(dm_far, g_out.sent), dims, 1, 1, None, [dp_2, dba])
        g_up.side(dba)
        g_2 = Summed(normed_one, after(dp_2, g_up.low, g_gate.sum), F)
        t_gate = g_gate.total(R)
        dp_1, dba_1, et_1, eg_1, er_1 = mixer_bwd(
            *args_1, after(dm_far, g_2.sent, t_down), dims, 0, 1, dba, [dp_1, dba_1])
        g_out.side(dp_1)
        g_1 = Summed(normed_one, after(dp_1, g_out.low), F)
        t_up = g_up.total(R)

        def back_one(lo, hi, *needs):
            return dot(after(dp_1, *needs)[lo:hi], wa1, NT) + dot(after(dp_2, *needs)[lo:hi], wa2, NT)

        t_out = g_out.total(R)

        def near_one(part):
            g_2.side(part, before=(g_out.sum,))

            keep("far", dot(after(hiddens[1], g_2.low, g_out.sum, t_up), wd, NT))
            return keep("one", back_one(0, mid, kept["far"]))

        dnormed_one, far_one = sum_tokens(lambda: back_one(mid, tok, g_1.sent, g_up.sum, t_gate), near_one, R)
        g_1.side(kept["one"], before=(g_2.sum,))
        added, unused = sum_tokens(lambda: kept["far"], lambda part: dot(after(hiddens[0], g_1.low, t_out), wd, NT), R)
        layer_out = (middle + after(added, g_1.sum)).astype(bf16)
        dprm = dr_1 + dr_2 + er_1 + er_2
        dgain_out = dg_1 + dg_2 + eg_1 + eg_2
        dtaps = [dt_1 + et_1, dt_2 + et_2]

        n1 = own32 * rms(own32)
        dfirst, dgain_first = norm_back(n1, rms(own32), gain_first, dnormed_one)
        grad_tokens = unmix(dmiddle + dfirst, 1)

        def wide(parts):
            return parts.astype(f32).transpose(1, 0, 2).reshape(shard, -1)

        def tall(parts):
            return parts.astype(f32).transpose(0, 2, 1).reshape(-1, shard)

        t_2 = g_2.total(R)
        t_1 = g_1.total(R)

        def joined(lo, width):
            return jnp.stack([t[:, :, lo : lo + width] for t in (t_1, t_2)], axis=2).astype(f32).transpose(1, 0, 2, 3).reshape(shard, -1)

        grad_query, grad_key = joined(0, hq), joined(hq, hq)
        grad_value, grad_gate_w = joined(2 * hq, hv), joined(2 * hq + hv, hv)
        grad_beta, grad_alpha = wide(t_1[:, :, w1 : w1 + nh]), wide(t_1[:, :, w1 + nh : w1 + 2 * nh])
        grad_down, grad_out = tall(t_down), tall(t_out)
        grad_gate, grad_up = wide(t_gate), wide(t_up)

        def placed(parts, total, width):
            part = jnp.concatenate(parts, axis=1)
            return lax.dynamic_update_slice(jnp.zeros((4, total), f32), part, (0, r * width))

        gq = placed([dtaps[h][:, :hq] for h in range(SPLIT)], R * wq, wq)
        gk = placed([dtaps[h][:, hq : 2 * hq] for h in range(SPLIT)], R * wq, wq)
        gv = placed([dtaps[h][:, 2 * hq :] for h in range(SPLIT)], R * wv, wv)
        heads_part = lax.dynamic_update_slice(jnp.zeros((2, heads), f32), dprm[:2, nh : 2 * nh], (0, r * nh)).reshape(1, -1)
        packed = jnp.concatenate([
            unmix(dgain_first[None], 1).reshape(N, -1),
            unmix(dgain_second[None], 1).reshape(N, -1),
            gq.reshape(4, N, -1).transpose(1, 0, 2).reshape(N, -1),
            gk.reshape(4, N, -1).transpose(1, 0, 2).reshape(N, -1),
            gv.reshape(4, N, -1).transpose(1, 0, 2).reshape(N, -1),
            dgain_out.reshape(N, tiny),
            jnp.broadcast_to(heads_part, (N, 2 * heads))], axis=1)
        summed = jnp.sum(lax.all_to_all(packed, both, 0, 0, tiled=True), axis=0)
        sizes = [shard, shard, 4 * shard, 4 * shard, 4 * shard * per, tiny, heads, heads]
        ends = [0]
        for size in sizes:
            ends.append(ends[-1] + size)
        pick = [summed[ends[i] : ends[i + 1]] for i in range(len(sizes))]
        return (
            unmix(layer_out, 1), grad_tokens, pick[0], grad_query, grad_key, grad_value, grad_gate_w, grad_beta, grad_alpha,
            pick[2].reshape(4, shard), pick[3].reshape(4, shard), pick[4].reshape(4, shard * per), pick[6], pick[7], pick[5],
            grad_out, pick[1], grad_gate, grad_up, grad_down)

    return on_device


def solution(mesh):
    rows, cols, flat = P(("fsdp", "rep"), None), P(None, ("fsdp", "rep")), P(("fsdp", "rep"))
    placed = (rows, flat, rows, flat, rows, rows, rows, rows, rows, rows, cols, cols, cols, P(), P(), flat, cols, flat, rows, rows, cols)
    made = (rows, rows, flat, rows, rows, rows, rows, rows, rows, cols, cols, cols, P(), P(), flat, cols, flat, rows, rows, cols)
    return jax.shard_map(
        make(mesh.shape["fsdp"], mesh.shape["rep"]), mesh=mesh, in_specs=placed, out_specs=made, check_vma=False)
```

```python
import functools

import jax
import jax.numpy as jnp
from jax import lax
from jax.experimental import pallas as pl
from jax.experimental.pallas import tpu as pltpu
from jax.sharding import PartitionSpec as P

SEQ = 256
SPLIT = 2
PAIR = 2
ROWS = PAIR * SEQ

f32 = jnp.float32
bf16 = jnp.bfloat16
NN = (((1,), (0,)), ((), ()))
NT = (((1,), (1,)), ((), ()))
TN = (((0,), (0,)), ((), ()))


def split(a):
    hi = a.astype(bf16)
    return hi, (a - hi.astype(f32)).astype(bf16)


def one(a, b, dims):
    return lax.dot_general(a.astype(bf16), b.astype(bf16), dims, preferred_element_type=f32)


def three(a, b, dims):
    ah, al = split(a)
    bh, bl = split(b)
    out = lax.dot_general(ah, bl, dims, preferred_element_type=f32)
    out = out + lax.dot_general(al, bh, dims, preferred_element_type=f32)
    return out + lax.dot_general(ah, bh, dims, preferred_element_type=f32)


def exact_left(a, b, dims):
    bh, bl = split(b)
    a = a.astype(bf16)
    return lax.dot_general(a, bh, dims, preferred_element_type=f32) + lax.dot_general(a, bl, dims, preferred_element_type=f32)


def exact_right(a, b, dims):
    ah, al = split(a)
    b = b.astype(bf16)
    return lax.dot_general(ah, b, dims, preferred_element_type=f32) + lax.dot_general(al, b, dims, preferred_element_type=f32)


def sigmoid(v):
    return 1.0 / (1.0 + jnp.exp(-v))


def conv(c, taps, pos):
    width = taps.shape[0]
    z = c * taps[width - 1 : width]
    for s in range(1, width):
        z = z + jnp.where(pos >= s, pltpu.roll(c, s, 0), 0.0) * taps[width - 1 - s : width - s]
    return z


def unit(c):
    r = lax.rsqrt(jnp.sum(c * c, axis=-1, keepdims=True) + 1e-6)
    return c * r, r


def inverses(n_list, iota_r, iota_c):
    size = n_list[0].shape[0]
    eye = (iota_r == iota_c).astype(f32)
    xs = None
    b = 1
    while b < size:
        mask = ((iota_r // (2 * b)) == (iota_c // (2 * b))) & ((iota_r // b) % 2 == 1) & ((iota_c // b) % 2 == 0)
        cs = [jnp.where(mask, n, 0.0) for n in n_list]
        if xs is None:
            xs = [eye - c for c in cs]
        else:
            low = [x.astype(bf16) for x in xs]
            t = [one(c, x, NN) for c, x in zip(cs, low)]
            xs = [x - one(y, z, NN) for x, y, z in zip(xs, low, t)]
        b *= 2
    left = [(eye - x) - three(n, x, NN) for n, x in zip(n_list, xs)]
    return [x + one(x, r, NN) for x, r in zip(xs, left)]


def rates(pba, prm, tri):
    beta = sigmoid(pba)
    rate = pba + prm[1:2]
    decay = -prm[0:1] * (jnp.maximum(rate, 0.0) + jnp.log1p(jnp.exp(-jnp.abs(rate))))
    return beta, rate, decay, exact_left(tri, decay, NN), exact_right(decay, tri, (((0,), (1,)), ((), ())))


class Sequence:
    def __init__(self, dims, half, refs, rows, iota_r, iota_c, tri):
        pq_ref, pk_ref, pv_ref, pg_ref, ba_ref, pos_ref, taps_ref, gain_ref, prm_ref = refs
        nh, dk, dv = dims
        hs = nh // SPLIT
        wq = hs * dk
        at = half * hs
        H = range(hs)
        self.rows = rows
        self.pos = pos_ref[rows, :]
        taps = taps_ref[...]
        self.taps = (taps[:, :wq], taps[:, wq : 2 * wq], taps[:, 2 * wq :])
        self.raw = (pq_ref[rows, :], pk_ref[rows, :], pv_ref[rows, :])
        self.beta, self.rate, self.decay, gcol, grow = rates(ba_ref[rows, :], prm_ref[...], tri)
        self.z = tuple(conv(c, t, self.pos) for c, t in zip(self.raw, self.taps))
        self.sig = tuple(sigmoid(z) for z in self.z)
        qc, kc, self.v = (z * g for z, g in zip(self.z, self.sig))
        live = (iota_c <= iota_r) & (iota_c >= iota_r - self.pos.astype(jnp.int32))
        self.bs = [self.beta[:, at + h : at + h + 1] for h in H]
        self.uq = [unit(qc[:, h * dk : (h + 1) * dk]) for h in H]
        self.uk = [unit(kc[:, h * dk : (h + 1) * dk]) for h in H]
        self.qs = [a * dk ** -0.5 for a, _ in self.uq]
        self.ks = [a for a, _ in self.uk]
        lane = nh + at
        self.ls = [
            jnp.where(live, jnp.exp(jnp.where(live, gcol[:, lane + h : lane + h + 1] - grow[lane + h : lane + h + 1, :], 0.0)), 0.0)
            for h in H]


def planes(n):
    iota_r = lax.broadcasted_iota(jnp.int32, (n, n), 0)
    iota_c = lax.broadcasted_iota(jnp.int32, (n, n), 1)
    return iota_r, iota_c, (iota_c <= iota_r).astype(f32), iota_c < iota_r


def fwd_kernel(dims, half, *refs):
    shared, (out_ref, x_ref, u_ref, o_ref) = refs[:9], refs[-4:]
    pg_ref, gain_ref = refs[3], refs[7]
    nh, dk, dv = dims
    hs = nh // SPLIT
    iota_r, iota_c, tri, strict = planes(SEQ)
    gain = gain_ref[...]
    seqs = [Sequence(dims, half, shared, slice(i * SEQ, (i + 1) * SEQ), iota_r, iota_c, tri) for i in range(out_ref.shape[0] // SEQ)]
    units = [(i, h) for i in range(len(seqs)) for h in range(hs)]
    ms = [three(seqs[i].ks[h], seqs[i].ks[h], NT) for i, h in units]
    ns = [jnp.where(strict, seqs[i].bs[h] * seqs[i].ls[h] * m, 0.0) for (i, h), m in zip(units, ms)]
    xs = inverses(ns, iota_r, iota_c)
    us = [three(x, seqs[i].bs[h] * seqs[i].v[:, h * dv : (h + 1) * dv], NN) for (i, h), x in zip(units, xs)]
    ps = [seqs[i].ls[h] * three(seqs[i].qs[h], seqs[i].ks[h], NT) for i, h in units]
    os = [three(p, u, NN) for p, u in zip(ps, us)]
    for (i, h), x, u, o in zip(units, xs, us, os):
        rows, sl = seqs[i].rows, slice(h * dv, (h + 1) * dv)
        x_ref[i * hs + h] = x
        u_ref[rows, sl] = u
        o_ref[rows, sl] = o
        r = lax.rsqrt(jnp.mean(o * o, axis=-1, keepdims=True) + 1e-5)
        pg = pg_ref[rows, sl]
        out_ref[rows, sl] = (o * r * gain * (pg * sigmoid(pg))).astype(bf16)


def bwd_kernel(dims, half, has_before, *refs):
    shared, (x_ref, u_ref, o_ref, dm_ref) = refs[:9], refs[9:13]
    dp_ref, dba_ref, dtaps_ref, dgain_ref, dprm_ref = refs[-5:]
    pg_ref, gain_ref, prm_ref = refs[3], refs[7], refs[8]
    nh, dk, dv = dims
    hs = nh // SPLIT
    wq, wv = hs * dk, hs * dv
    at = half * hs
    iota_r, iota_c, tri, strict = planes(SEQ)
    gain = gain_ref[...]
    prm = prm_ref[...]
    seqs = [Sequence(dims, half, shared, slice(i * SEQ, (i + 1) * SEQ), iota_r, iota_c, tri) for i in range(dm_ref.shape[0] // SEQ)]
    units = [(i, h) for i in range(len(seqs)) for h in range(hs)]
    dgain = jnp.zeros_like(gain)
    dos, us = [], []
    for i, h in units:
        rows, sl = seqs[i].rows, slice(h * dv, (h + 1) * dv)
        o = o_ref[rows, sl]
        pg = pg_ref[rows, sl]
        dm = dm_ref[rows, sl]
        r = lax.rsqrt(jnp.mean(o * o, axis=-1, keepdims=True) + 1e-5)
        nrm = o * r
        sg = sigmoid(pg)
        dp_ref[rows, 2 * wq + wv + h * dv : 2 * wq + wv + (h + 1) * dv] = (dm * nrm * gain * (sg * (1.0 + pg * (1.0 - sg)))).astype(bf16)
        dy = dm * (pg * sg)
        dgain = dgain + jnp.sum(dy * nrm, axis=0, keepdims=True)
        dn = dy * gain
        dos.append(r * (dn - nrm * jnp.mean(nrm * dn, axis=-1, keepdims=True)))
        us.append(u_ref[rows, sl])
    bm = [jnp.where(strict, seqs[i].ls[h] * three(seqs[i].ks[h], seqs[i].ks[h], NT), 0.0) for i, h in units]
    ps = [seqs[i].ls[h] * three(seqs[i].qs[h], seqs[i].ks[h], NT) for i, h in units]
    dps = [three(do, u, NT) for do, u in zip(dos, us)]
    dus = [three(p, do, TN) for p, do in zip(ps, dos)]
    dws = [three(x_ref[i * hs + h], du, TN) for (i, h), du in zip(units, dus)]
    das = [-three(dw, u, NT) for dw, u in zip(dws, us)]

    @pl.when(pl.program_id(0) == 0)
    def _():
        dtaps_ref[...] = jnp.zeros_like(dtaps_ref)
        dgain_ref[...] = jnp.zeros_like(dgain_ref)
        dprm_ref[...] = jnp.zeros_like(dprm_ref)

    dgain_ref[...] += dgain
    lane = lax.broadcasted_iota(jnp.int32, (SEQ, 128), 1)
    ones = jnp.ones((SEQ, 128), f32)
    sc = dk ** -0.5
    for i, q in enumerate(seqs):
        rows, pos = q.rows, q.pos
        dbeta = jnp.zeros((SEQ, 128), f32)
        dlog = jnp.zeros((SEQ, 128), f32)
        dz = ([], [], [])
        for h in range(hs):
            n = i * hs + h
            vh = q.v[:, h * dv : (h + 1) * dv]
            ab = das[n] * bm[n]
            dbeta = jnp.where(lane == at + h, jnp.sum(dws[n] * vh, axis=-1, keepdims=True) + jnp.sum(ab, axis=-1, keepdims=True), dbeta)
            e = q.bs[h] * ab + dps[n] * ps[n]
            dlog = jnp.where(lane == nh + at + h, jnp.sum(e, axis=-1, keepdims=True) - exact_right(e, ones, TN), dlog)
            ds = dps[n] * q.ls[h]
            dmm = jnp.where(strict, q.bs[h] * das[n] * q.ls[h], 0.0)
            dq = sc * three(ds, q.ks[h], NN)
            dkh = three(ds, q.qs[h], TN) + three(dmm, q.ks[h], NN) + three(dmm, q.ks[h], TN)
            qh, rq = q.uq[h]
            kh, rk = q.uk[h]
            dz[0].append(rq * (dq - qh * jnp.sum(qh * dq, axis=-1, keepdims=True)))
            dz[1].append(rk * (dkh - kh * jnp.sum(kh * dkh, axis=-1, keepdims=True)))
            dz[2].append(q.bs[h] * dws[n])
        ddecay = exact_left(tri, dlog, TN)
        drate = -prm[0:1] * ddecay * sigmoid(q.rate)
        dba = dbeta * q.beta * (1.0 - q.beta) + drate
        if has_before:
            dba = dba + refs[13][rows, :]
            dp_ref[rows, 2 * wq + 2 * wv :] = dba.astype(bf16)
        dba_ref[rows, :] = dba
        dprm_ref[0:1, :] += jnp.sum(ddecay * q.decay, axis=0, keepdims=True)
        dprm_ref[1:2, :] += jnp.sum(drate, axis=0, keepdims=True)
        to = 0
        for parts, z, sg, c, tap in zip(dz, q.z, q.sig, q.raw, q.taps):
            d = jnp.concatenate(parts, axis=1) * (sg * (1.0 + z * (1.0 - sg)))
            width = tap.shape[0]
            w = c.shape[1]
            dc = d * tap[width - 1 : width]
            dtaps_ref[width - 1 : width, to : to + w] += jnp.sum(d * c, axis=0, keepdims=True)
            for s in range(1, width):
                m = jnp.where(pos >= s, d, 0.0)
                dc = dc + pltpu.roll(m, SEQ - s, 0) * tap[width - 1 - s : width - s]
                dtaps_ref[width - 1 - s : width - s, to : to + w] += jnp.sum(m * pltpu.roll(c, s, 0), axis=0, keepdims=True)
            dp_ref[rows, to : to + w] = dc.astype(bf16)
            to += w


def shared_specs(dims, off=0):
    nh, dk, dv = dims
    wq, wv = nh // SPLIT * dk, nh // SPLIT * dv
    at = (2 * wq) // wv
    small = (2 * wq + 2 * wv) // 128
    return [
        pl.BlockSpec((ROWS, wq), lambda i: (i + off, 0)),
        pl.BlockSpec((ROWS, wq), lambda i: (i + off, 1)),
        pl.BlockSpec((ROWS, wv), lambda i: (i + off, at)),
        pl.BlockSpec((ROWS, wv), lambda i: (i + off, at + 1)),
        pl.BlockSpec((ROWS, 128), lambda i: (i + off, small)),
        pl.BlockSpec((ROWS, 1), lambda i: (i + off, 0)),
        pl.BlockSpec((4, 2 * wq + wv), lambda i: (0, 0)),
        pl.BlockSpec((1, dv), lambda i: (0, 0)),
        pl.BlockSpec((8, 128), lambda i: (0, 0)),
    ]


def cost(us):
    return pl.CostEstimate(flops=int(us * 1.1e9), bytes_accessed=int(us * 1e6), transcendentals=0)


def mixer_fwd(proj, first, pos, taps, gain, prm, dims, half, part=None, filled=()):
    tok = pos.shape[0]
    nh, dk, dv = dims
    hs = nh // SPLIT
    ns = tok // SEQ
    wv = hs * dv
    steps = ns // PAIR if part is None else ns // PAIR // 2
    off = part * steps if part else 0
    row = pl.BlockSpec((ROWS, wv), lambda i: (i + off, 0))
    args = [proj, proj, proj, proj, first, pos, taps, gain, prm, *filled]
    return pl.pallas_call(
        functools.partial(fwd_kernel, dims, half),
        grid=(steps,),
        in_specs=shared_specs(dims, off) + [pl.BlockSpec(memory_space=pl.ANY)] * len(filled),
        out_specs=[
            pl.BlockSpec((ROWS, wv), lambda i: (i + off, half)),
            pl.BlockSpec((PAIR * hs, SEQ, SEQ), lambda i: (i + off, 0, 0)),
            row,
            row,
        ],
        out_shape=[
            jax.ShapeDtypeStruct((tok, nh * dv), bf16),
            jax.ShapeDtypeStruct((ns * hs, SEQ, SEQ), f32),
            jax.ShapeDtypeStruct((tok, wv), f32),
            jax.ShapeDtypeStruct((tok, wv), f32),
        ],
        input_output_aliases={9 + i: i for i in range(len(filled))},
        cost_estimate=cost(4 if part is None else 12),
        compiler_params=pltpu.CompilerParams(vmem_limit_bytes=48 << 20),
    )(*args)


def mixer_bwd(proj, first, pos, taps, gain, prm, x, u, o, dm, dims, half, part, before=None, filled=None):
    tok = pos.shape[0]
    nh, dk, dv = dims
    hs = nh // SPLIT
    ns = tok // SEQ
    wq, wv = hs * dk, hs * dv
    steps = dm.shape[0] // ROWS
    off = part * steps
    row = pl.BlockSpec((ROWS, wv), lambda i: (i + off, 0))
    lanes = pl.BlockSpec((ROWS, 128), lambda i: (i + off, 0))
    specs = shared_specs(dims, off) + [
        pl.BlockSpec((PAIR * hs, SEQ, SEQ), lambda i: (i + off, 0, 0)), row, row, pl.BlockSpec((ROWS, wv), lambda i: (i, half))]
    args = [proj, proj, proj, proj, first, pos, taps, gain, prm, x, u, o, dm]
    width = 2 * wq + 2 * wv
    if before is not None:
        args.append(before)
        specs.append(lanes)
        width += 128
    alias = {}
    if filled is not None:
        alias = {len(args): 0, len(args) + 1: 1}
        args += filled
        specs += [pl.BlockSpec(memory_space=pl.ANY)] * 2
    return pl.pallas_call(
        functools.partial(bwd_kernel, dims, half, before is not None),
        grid=(steps,),
        in_specs=specs,
        out_specs=[
            pl.BlockSpec((ROWS, width), lambda i: (i + off, 0)),
            lanes,
            pl.BlockSpec((4, 2 * wq + wv), lambda i: (0, 0)),
            pl.BlockSpec((1, dv), lambda i: (0, 0)),
            pl.BlockSpec((8, 128), lambda i: (0, 0)),
        ],
        out_shape=[
            jax.ShapeDtypeStruct((tok, width), bf16),
            jax.ShapeDtypeStruct((tok, 128), f32),
            jax.ShapeDtypeStruct((4, 2 * wq + wv), f32),
            jax.ShapeDtypeStruct((1, dv), f32),
            jax.ShapeDtypeStruct((8, 128), f32),
        ],
        input_output_aliases=alias,
        cost_estimate=cost(26),
        compiler_params=pltpu.CompilerParams(vmem_limit_bytes=56 << 20),
    )(*args)


def xor_send(value, axis, size, step):
    return lax.ppermute(value, axis, [(i, i ^ step) for i in range(size)])


def after(value, *needs):
    return lax.optimization_barrier((value, *needs))[0]


def lines(size):
    return [[low + 2 * i for i in range(size // 2)] for low in range(2)]


def gather_line(rows, size):
    return lax.all_gather(rows, "fsdp", axis=0, tiled=True, axis_index_groups=lines(size))


def gather_side(near, size, *needs):
    got = xor_send(after(near, *needs) if needs else near, "fsdp", size, 1)
    return jnp.concatenate([near, got], axis=0), got


def gather_side_first(rows, size, *needs):
    got = xor_send(after(rows, *needs), "fsdp", size, 1)
    full = gather_line(jnp.concatenate([rows, got], axis=0), size)
    width = rows.shape[1]
    return full.reshape(size // 2, 2, -1, width).swapaxes(0, 1).reshape(-1, width), full, got


def dot(left, right, dims=NN, out=f32):
    return lax.dot_general(left, right, dims, preferred_element_type=f32).astype(out)


class Summed:
    def __init__(self, left, right, size, *needs):
        self.size = size
        self.half = left.shape[1] // 2
        self.left, self.right = left, right
        self.sent = dot(left[:, self.half :], right, TN, bf16)
        self.got = xor_send(after(self.sent, *needs) if needs else self.sent, "fsdp", size, 1)

    def side(self, *needs, before=()):
        keep = dot(self.left[:, : self.half], after(self.right, *needs) if needs else self.right, TN)
        self.low = (keep + self.got.astype(f32)).astype(bf16)
        ready = after(self.low, *before) if before else self.low
        self.sum = lax.psum_scatter(ready, "fsdp", scatter_dimension=0, tiled=True, axis_index_groups=lines(self.size))

    def total(self, ranks, *needs):
        ready = after(self.sum, *needs) if needs else self.sum
        return lax.all_to_all(ready.reshape(ranks, -1, ready.shape[1]), "rep", 0, 0)


def join_tokens(rows, size, meanwhile=None):
    half = size // 2

    def around(block):
        held = {0: block}
        step = half // 2
        while step:
            for j in list(held):
                held[j ^ step] = xor_send(held[j], "rep", size, step)
            step //= 2
        return jnp.concatenate([held[j] for j in range(half)], axis=0)

    beyond = xor_send(rows, "rep", size, half)
    near = around(rows)
    if meanwhile is not None:
        return near, around(after(beyond, meanwhile(near))), beyond
    return near, around(beyond), beyond


def sum_tokens(far, near, size, *needs, last=False):
    half = size // 2

    def around(part, *first):
        held = jnp.split(part, half, axis=0)
        step = 1
        while step < half:
            for j in range(0, half, 2 * step):
                low = held[j + step].astype(bf16)
                held[j] = held[j] + xor_send(after(low, *first) if first else low, "rep", size, step).astype(f32)
            step *= 2
        return held[0]

    beyond = around(far()).astype(bf16)
    part = near(beyond)
    if needs:
        beyond = after(beyond, *needs)
    got = xor_send(beyond, "rep", size, half)
    return around(part, *([got] if last else [])) + got.astype(f32), got


def rms(values):
    return lax.rsqrt(jnp.mean(values * values, axis=-1, keepdims=True) + 1e-06)


def norm_back(n, r, gain, dout):
    scaled = dout * gain
    return r * (scaled - n * jnp.mean(n * scaled, axis=-1, keepdims=True)), jnp.sum(dout * n, axis=0)


def make(F, R):
    both = ("fsdp", "rep")

    def on_device(tokens, segments, cotangent, gain_one, w_query, w_key, w_value, w_gate, w_beta, w_alpha, conv_q, conv_k,
                  conv_v, a_log, dt_bias, norm_gain, w_out, gain_two, w_ffgate, w_ffup, w_down):
        f = lax.axis_index("fsdp")
        r = lax.axis_index("rep")
        N = F * R
        rows_own, D = tokens.shape
        heads = a_log.shape[0]
        dk = w_query.shape[1] // heads
        dv = w_value.shape[1] // heads
        nh = heads // R
        dims = (nh, dk, dv)
        wq, wv = nh * dk, nh * dv
        hq, hv = wq // SPLIT, wv // SPLIT
        shard = D // N
        block = D // F
        ffq = w_ffgate.shape[1] // R
        tok = rows_own * R
        ns = tok // SEQ
        tiny = dv // N
        per = conv_v.shape[1] // shard

        low_bit = f & 1

        def swap(array, axis):
            half = array.shape[axis] // 2
            return jnp.concatenate(
                [lax.dynamic_slice_in_dim(array, (low_bit ^ j) * half, half, axis=axis) for j in range(2)], axis=axis)

        def mix(array, axis):
            at = [slice(None)] * array.ndim
            parts = []
            for bit in range(2):
                for i in range(F // 2):
                    at[axis] = slice((2 * i + bit) * block, (2 * i + bit + 1) * block)
                    parts.append(array[tuple(at)])
            return swap(jnp.concatenate(parts, axis=axis), axis)

        def unmix(array, axis):
            array = swap(array, axis)
            at = [slice(None)] * array.ndim
            parts = []
            for i in range(F // 2):
                for bit in range(2):
                    p = bit * (F // 2) + i
                    at[axis] = slice(p * block, (p + 1) * block)
                    parts.append(array[tuple(at)])
            return jnp.concatenate(parts, axis=axis)

        def quarter(arrays):
            return jnp.concatenate([a.reshape(shard, R, -1) for a in arrays], axis=2)

        def spread(packed, *needs):
            packed = packed.transpose(1, 0, 2)
            if needs:
                packed = after(packed, *needs)
            return lax.all_to_all(packed, "rep", 0, 0).reshape(R * shard, -1)

        extra = jnp.concatenate(
            [gain_one[:, None], gain_two[:, None], conv_q.T, conv_k.T,
             conv_v.reshape(4, shard, per).transpose(1, 0, 2).reshape(shard, 4 * per),
             jnp.pad(norm_gain, (0, shard - tiny))[:, None]], axis=1).T
        small = jnp.concatenate([w_beta.reshape(shard, R, nh), w_alpha.reshape(shard, R, nh)], axis=2)
        small = jnp.pad(small, ((0, 0), (0, 0), (0, 128 - 2 * nh)))

        def halves(array, width):
            parts = array.reshape(shard, R, SPLIT, width)
            return [parts[:, :, h] for h in range(SPLIT)]

        q_h, k_h, v_h, g_h = halves(w_query, hq), halves(w_key, hq), halves(w_value, hv), halves(w_gate, hv)
        own = mix(tokens, 1)
        part_a = spread(jnp.concatenate([q_h[0], k_h[0], v_h[0], g_h[0], small, q_h[1], k_h[1], v_h[1], g_h[1]], axis=2))
        w1 = 2 * hq + 2 * hv
        part_a = after(part_a, own)
        part_1, part_2 = part_a[:, : w1 + 128], part_a[:, w1 + 128 :]
        extra_all = lax.all_to_all(jnp.broadcast_to(after(extra, part_a)[None], (N, *extra.shape)), both, 0, 0)
        extra_all = extra_all.transpose(1, 0, 2).reshape(-1, D).astype(f32)
        line_1 = gather_line(part_1, F)
        every_near, every_far, every_got = join_tokens(own, R)
        every = jnp.concatenate([every_near, every_far], axis=0)
        ids_all = jnp.concatenate(join_tokens(segments[:, None], R)[:2], axis=0).reshape(ns, SEQ)
        part_r = spread(quarter([w_out.T, w_ffgate, w_ffup, w_down.T]), extra_all, every_got, line_1)
        gains = mix(extra_all[:2], 1)
        gain_first, gain_second = gains[0:1], gains[1:2]
        every32 = every.astype(f32)
        normed_one = (every32 * rms(every32) * gain_first).astype(bf16)
        cot = mix(cotangent, 1)
        part_r = after(part_r, normed_one, cot)
        part_b, part_g, part_u, part_d = (
            part_r[:, :wv], part_r[:, wv : wv + ffq], part_r[:, wv + ffq : wv + 2 * ffq], part_r[:, wv + 2 * ffq :])
        line_2 = gather_line(after(part_2, extra_all), F)
        wa1, side_1 = gather_side(line_1, F)
        cot_near, cot_far, unused = join_tokens(after(cot, side_1), R)
        line_b = gather_line(part_b, F)
        line_g = gather_line(after(part_g, side_1), F)
        wu, line_u, got_u = gather_side_first(part_u, F, side_1)
        line_d = gather_line(after(part_d, side_1), F)

        cq = lax.dynamic_slice_in_dim(extra_all[2:6], r * wq, wq, axis=1)
        ck = lax.dynamic_slice_in_dim(extra_all[6:10], r * wq, wq, axis=1)
        cv = extra_all[10 : 10 + 4 * per].reshape(4, per, D).transpose(0, 2, 1).reshape(4, D * per)
        cv = lax.dynamic_slice_in_dim(cv, r * wv, wv, axis=1)
        gain_out = extra_all[10 + 4 * per].reshape(N, shard)[:, :tiny].reshape(1, dv)
        taps = [jnp.concatenate([cq[:, h * hq : (h + 1) * hq], ck[:, h * hq : (h + 1) * hq], cv[:, h * hv : (h + 1) * hv]], axis=1)
                for h in range(SPLIT)]
        prm = jnp.stack([jnp.exp(lax.dynamic_slice_in_dim(a_log, r * nh, nh)), lax.dynamic_slice_in_dim(dt_bias, r * nh, nh)])
        prm = jnp.pad(prm, ((0, 6), (nh, 128 - 2 * nh)))
        place = jnp.arange(SEQ)
        same = (ids_all[:, :, None] == ids_all[:, None, :]) & (place[:, None] >= place[None, :])[None]
        pos = (jnp.sum(same.astype(f32), axis=2) - 1.0).reshape(tok, 1)

        proj_1 = dot(after(normed_one, part_r), wa1)
        mixed, x_1, u_1, o_1 = mixer_fwd(proj_1, proj_1, pos, taps[0], gain_out, prm, dims, 0)
        wa2, side_2 = gather_side(line_2, F, side_1)
        proj_2 = dot(after(normed_one, mixed, line_b, got_u), wa2)
        mixed, *saved_2 = mixer_fwd(proj_2, proj_1, pos, taps[1], gain_out, prm, dims, 1, 1, [mixed])
        wb, side_b = gather_side(line_b, F, side_2)
        wg, side_g = gather_side(line_g, F, side_b)
        side_d = xor_send(after(line_d, side_g), "fsdp", F, 1)
        own32 = own.astype(f32)
        mid = tok // 2
        mixed = after(mixed, line_g, cot_near, cot_far)
        out_far = dot(mixed[mid:], wb, NT)
        kept = {}

        def keep(name, value):
            kept[name] = value
            return value

        def near_mixed(part):
            kept["mixed"], *kept["saved"] = mixer_fwd(
                proj_2, proj_1, after(pos, part), taps[1], gain_out, prm, dims, 1, 0, [mixed, *saved_2])
            return dot(kept["mixed"][:mid], wb, NT)

        added, unused = sum_tokens(lambda: out_far, near_mixed, R, last=True)
        mixed, saved_2 = kept["mixed"], kept["saved"]
        middle = own32 + after(added, side_g, line_u, line_d)
        r2 = rms(middle)
        n2 = middle * r2
        normed_own = (n2 * gain_second).astype(bf16)
        gates, ups, acts, sigs, hiddens = [], [], [], [], []

        def gate(normed):
            gates.append(dot(normed, wg))
            return gates[-1]

        *two, beyond = join_tokens(normed_own, R, gate)
        gate(two[1])
        side_d = after(side_d, gates[1])
        wd = jnp.concatenate([after(line_d, gates[0]), side_d], axis=0)
        for t, normed in enumerate(two):
            ups.append(dot(after(normed, gates[1]) if t else after(normed, beyond), wu))
            sigs.append(jax.nn.sigmoid(gates[t]))
            acts.append(gates[t] * sigs[t])
            hiddens.append((acts[t] * ups[t]).astype(bf16))
        hidden = jnp.concatenate(hiddens, axis=0)
        normed_two = jnp.concatenate(two, axis=0)
        cot_all = jnp.concatenate([cot_near, cot_far], axis=0)

        g_down = Summed(cot_all, hidden, F)
        dgates, dups = [None, None], [None, None]

        def back_two(t, *needs):
            dhidden = dot(after((cot_near, cot_far)[t], *needs), wd)
            dgates[t] = (dhidden * ups[t] * (sigs[t] * (1.0 + gates[t] * (1.0 - sigs[t])))).astype(bf16)
            dups[t] = (dhidden * acts[t]).astype(bf16)
            return dot(dgates[t], wg, NT) + dot(dups[t], wu, NT)

        dnormed_two, far_two = sum_tokens(lambda: back_two(1, g_down.sent), lambda part: keep("two", back_two(0, part)), R)
        g_down.side(kept["two"])
        g_gate = Summed(normed_two, after(jnp.concatenate(dgates, axis=0), g_down.low), F, g_down.got)
        dinner, dgain_second = norm_back(n2, r2, gain_second, after(dnormed_two, g_gate.sent))
        dmiddle = cot.astype(f32) + dinner
        dmiddle_own = dmiddle.astype(bf16)
        dlow = join_tokens(dmiddle_own, R)[:2]
        dm_near = dot(dlow[0], wb)
        args_2 = (proj_2, proj_1, pos, taps[1], gain_out, prm, *saved_2)
        args_1 = (proj_1, proj_1, pos, taps[0], gain_out, prm, x_1, u_1, o_1)
        dp_2, dba, dt_2, dg_2, dr_2 = mixer_bwd(*args_2, dm_near, dims, 1, 0)
        g_up = Summed(normed_two, after(jnp.concatenate(dups, axis=0), dba), F, g_gate.got)
        g_gate.side(g_up.sent)
        dp_1, dba_1, dt_1, dg_1, dr_1 = mixer_bwd(*args_1, after(dm_near, g_gate.low, g_down.sum), dims, 0, 0, dba)
        t_down = g_down.total(R)
        g_out = Summed(jnp.concatenate(dlow, axis=0), after(mixed, dba_1), F)
        dm_far = dot(after(dlow[1], dba_1), wb)
        dp_2, dba, et_2, eg_2, er_2 = mixer_bwd(*args_2, after(dm_far, g_out.sent), dims, 1, 1, None, [dp_2, dba])
        g_up.side(dba)
        g_2 = Summed(normed_one, after(dp_2, g_up.low, g_gate.sum), F)
        t_gate = g_gate.total(R)
        dp_1, dba_1, et_1, eg_1, er_1 = mixer_bwd(
            *args_1, after(dm_far, g_2.sent, t_down), dims, 0, 1, dba, [dp_1, dba_1])
        g_out.side(dp_1)
        g_1 = Summed(normed_one, after(dp_1, g_out.low), F)

        def back_one(lo, hi, *needs):
            return dot(after(dp_1, *needs)[lo:hi], wa1, NT) + dot(after(dp_2, *needs)[lo:hi], wa2, NT)


        def near_one(part):
            g_2.side(part, g_out.sum)

            kept["t_up"], kept["t_out"] = g_up.total(R, g_2.low), g_out.total(R, g_2.low)
            keep("far", dot(after(hiddens[1], g_2.low, g_out.sum), wd, NT))
            return keep("one", back_one(0, mid, kept["far"], kept["t_up"]))

        dnormed_one, far_one = sum_tokens(lambda: back_one(mid, tok, g_1.sent, g_up.sum, t_gate), near_one, R)
        t_up, t_out = kept["t_up"], kept["t_out"]
        g_1.side(kept["one"], before=(g_2.sum,))
        added, unused = sum_tokens(lambda: kept["far"], lambda part: dot(after(hiddens[0], g_1.low, t_out), wd, NT), R)
        layer_out = (middle + after(added, g_1.sum)).astype(bf16)
        dprm = dr_1 + dr_2 + er_1 + er_2
        dgain_out = dg_1 + dg_2 + eg_1 + eg_2
        dtaps = [dt_1 + et_1, dt_2 + et_2]

        n1 = own32 * rms(own32)
        dfirst, dgain_first = norm_back(n1, rms(own32), gain_first, dnormed_one)
        grad_tokens = unmix(dmiddle + dfirst, 1)

        def wide(parts):
            return parts.astype(f32).transpose(1, 0, 2).reshape(shard, -1)

        def tall(parts):
            return parts.astype(f32).transpose(0, 2, 1).reshape(-1, shard)

        t_2 = g_2.total(R)
        t_1 = g_1.total(R)

        def joined(lo, width):
            return jnp.stack([t[:, :, lo : lo + width] for t in (t_1, t_2)], axis=2).astype(f32).transpose(1, 0, 2, 3).reshape(shard, -1)

        grad_query, grad_key = joined(0, hq), joined(hq, hq)
        grad_value, grad_gate_w = joined(2 * hq, hv), joined(2 * hq + hv, hv)
        grad_beta, grad_alpha = wide(t_1[:, :, w1 : w1 + nh]), wide(t_1[:, :, w1 + nh : w1 + 2 * nh])
        grad_down, grad_out = tall(t_down), tall(t_out)
        grad_gate, grad_up = wide(t_gate), wide(t_up)

        def placed(parts, total, width):
            part = jnp.concatenate(parts, axis=1)
            return lax.dynamic_update_slice(jnp.zeros((4, total), f32), part, (0, r * width))

        gq = placed([dtaps[h][:, :hq] for h in range(SPLIT)], R * wq, wq)
        gk = placed([dtaps[h][:, hq : 2 * hq] for h in range(SPLIT)], R * wq, wq)
        gv = placed([dtaps[h][:, 2 * hq :] for h in range(SPLIT)], R * wv, wv)
        heads_part = lax.dynamic_update_slice(jnp.zeros((2, heads), f32), dprm[:2, nh : 2 * nh], (0, r * nh)).reshape(1, -1)
        packed = jnp.concatenate([
            unmix(dgain_first[None], 1).reshape(N, -1),
            unmix(dgain_second[None], 1).reshape(N, -1),
            gq.reshape(4, N, -1).transpose(1, 0, 2).reshape(N, -1),
            gk.reshape(4, N, -1).transpose(1, 0, 2).reshape(N, -1),
            gv.reshape(4, N, -1).transpose(1, 0, 2).reshape(N, -1),
            dgain_out.reshape(N, tiny),
            jnp.broadcast_to(heads_part, (N, 2 * heads))], axis=1)
        summed = jnp.sum(lax.all_to_all(packed, both, 0, 0, tiled=True), axis=0)
        sizes = [shard, shard, 4 * shard, 4 * shard, 4 * shard * per, tiny, heads, heads]
        ends = [0]
        for size in sizes:
            ends.append(ends[-1] + size)
        pick = [summed[ends[i] : ends[i + 1]] for i in range(len(sizes))]
        return (
            unmix(layer_out, 1), grad_tokens, pick[0], grad_query, grad_key, grad_value, grad_gate_w, grad_beta, grad_alpha,
            pick[2].reshape(4, shard), pick[3].reshape(4, shard), pick[4].reshape(4, shard * per), pick[6], pick[7], pick[5],
            grad_out, pick[1], grad_gate, grad_up, grad_down)

    return on_device


def solution(mesh):
    rows, cols, flat = P(("fsdp", "rep"), None), P(None, ("fsdp", "rep")), P(("fsdp", "rep"))
    placed = (rows, flat, rows, flat, rows, rows, rows, rows, rows, rows, cols, cols, cols, P(), P(), flat, cols, flat, rows, rows, cols)
    made = (rows, rows, flat, rows, rows, rows, rows, rows, rows, cols, cols, cols, P(), P(), flat, cols, flat, rows, rows, cols)
    return jax.shard_map(
        make(mesh.shape["fsdp"], mesh.shape["rep"]), mesh=mesh, in_specs=placed, out_specs=made, check_vma=False)
```

```python
import functools

import jax
import jax.numpy as jnp
from jax import lax
from jax.experimental import pallas as pl
from jax.experimental.pallas import tpu as pltpu
from jax.sharding import PartitionSpec as P

SEQ = 256
SPLIT = 2
PAIR = 2
ROWS = PAIR * SEQ

f32 = jnp.float32
bf16 = jnp.bfloat16
NN = (((1,), (0,)), ((), ()))
NT = (((1,), (1,)), ((), ()))
TN = (((0,), (0,)), ((), ()))


def split(a):
    hi = a.astype(bf16)
    return hi, (a - hi.astype(f32)).astype(bf16)


def one(a, b, dims):
    return lax.dot_general(a.astype(bf16), b.astype(bf16), dims, preferred_element_type=f32)


def three(a, b, dims):
    ah, al = split(a)
    bh, bl = split(b)
    out = lax.dot_general(ah, bl, dims, preferred_element_type=f32)
    out = out + lax.dot_general(al, bh, dims, preferred_element_type=f32)
    return out + lax.dot_general(ah, bh, dims, preferred_element_type=f32)


def exact_left(a, b, dims):
    bh, bl = split(b)
    a = a.astype(bf16)
    return lax.dot_general(a, bh, dims, preferred_element_type=f32) + lax.dot_general(a, bl, dims, preferred_element_type=f32)


def exact_right(a, b, dims):
    ah, al = split(a)
    b = b.astype(bf16)
    return lax.dot_general(ah, b, dims, preferred_element_type=f32) + lax.dot_general(al, b, dims, preferred_element_type=f32)


def sigmoid(v):
    return 1.0 / (1.0 + jnp.exp(-v))


def conv(c, taps, pos):
    width = taps.shape[0]
    z = c * taps[width - 1 : width]
    for s in range(1, width):
        z = z + jnp.where(pos >= s, pltpu.roll(c, s, 0), 0.0) * taps[width - 1 - s : width - s]
    return z


def unit(c):
    r = lax.rsqrt(jnp.sum(c * c, axis=-1, keepdims=True) + 1e-6)
    return c * r, r


def inverses(n_list, iota_r, iota_c):
    size = n_list[0].shape[0]
    eye = (iota_r == iota_c).astype(f32)
    xs = None
    b = 1
    while b < size:
        mask = ((iota_r // (2 * b)) == (iota_c // (2 * b))) & ((iota_r // b) % 2 == 1) & ((iota_c // b) % 2 == 0)
        cs = [jnp.where(mask, n, 0.0) for n in n_list]
        if xs is None:
            xs = [eye - c for c in cs]
        else:
            low = [x.astype(bf16) for x in xs]
            t = [one(c, x, NN) for c, x in zip(cs, low)]
            xs = [x - one(y, z, NN) for x, y, z in zip(xs, low, t)]
        b *= 2
    left = [(eye - x) - three(n, x, NN) for n, x in zip(n_list, xs)]
    return [x + one(x, r, NN) for x, r in zip(xs, left)]


def rates(pba, prm, tri):
    beta = sigmoid(pba)
    rate = pba + prm[1:2]
    decay = -prm[0:1] * (jnp.maximum(rate, 0.0) + jnp.log1p(jnp.exp(-jnp.abs(rate))))
    return beta, rate, decay, exact_left(tri, decay, NN), exact_right(decay, tri, (((0,), (1,)), ((), ())))


class Sequence:
    def __init__(self, dims, half, refs, rows, iota_r, iota_c, tri):
        pq_ref, pk_ref, pv_ref, pg_ref, ba_ref, pos_ref, taps_ref, gain_ref, prm_ref = refs
        nh, dk, dv = dims
        hs = nh // SPLIT
        wq = hs * dk
        at = half * hs
        H = range(hs)
        self.rows = rows
        self.pos = pos_ref[rows, :]
        taps = taps_ref[...]
        self.taps = (taps[:, :wq], taps[:, wq : 2 * wq], taps[:, 2 * wq :])
        self.raw = (pq_ref[rows, :], pk_ref[rows, :], pv_ref[rows, :])
        self.beta, self.rate, self.decay, gcol, grow = rates(ba_ref[rows, :], prm_ref[...], tri)
        self.z = tuple(conv(c, t, self.pos) for c, t in zip(self.raw, self.taps))
        self.sig = tuple(sigmoid(z) for z in self.z)
        qc, kc, self.v = (z * g for z, g in zip(self.z, self.sig))
        live = (iota_c <= iota_r) & (iota_c >= iota_r - self.pos.astype(jnp.int32))
        self.bs = [self.beta[:, at + h : at + h + 1] for h in H]
        self.uq = [unit(qc[:, h * dk : (h + 1) * dk]) for h in H]
        self.uk = [unit(kc[:, h * dk : (h + 1) * dk]) for h in H]
        self.qs = [a * dk ** -0.5 for a, _ in self.uq]
        self.ks = [a for a, _ in self.uk]
        lane = nh + at
        self.ls = [
            jnp.where(live, jnp.exp(jnp.where(live, gcol[:, lane + h : lane + h + 1] - grow[lane + h : lane + h + 1, :], 0.0)), 0.0)
            for h in H]


def planes(n):
    iota_r = lax.broadcasted_iota(jnp.int32, (n, n), 0)
    iota_c = lax.broadcasted_iota(jnp.int32, (n, n), 1)
    return iota_r, iota_c, (iota_c <= iota_r).astype(f32), iota_c < iota_r


def fwd_kernel(dims, half, *refs):
    shared, (out_ref, x_ref, u_ref, o_ref) = refs[:9], refs[-4:]
    pg_ref, gain_ref = refs[3], refs[7]
    nh, dk, dv = dims
    hs = nh // SPLIT
    iota_r, iota_c, tri, strict = planes(SEQ)
    gain = gain_ref[...]
    seqs = [Sequence(dims, half, shared, slice(i * SEQ, (i + 1) * SEQ), iota_r, iota_c, tri) for i in range(out_ref.shape[0] // SEQ)]
    units = [(i, h) for i in range(len(seqs)) for h in range(hs)]
    ms = [three(seqs[i].ks[h], seqs[i].ks[h], NT) for i, h in units]
    ns = [jnp.where(strict, seqs[i].bs[h] * seqs[i].ls[h] * m, 0.0) for (i, h), m in zip(units, ms)]
    xs = inverses(ns, iota_r, iota_c)
    us = [three(x, seqs[i].bs[h] * seqs[i].v[:, h * dv : (h + 1) * dv], NN) for (i, h), x in zip(units, xs)]
    ps = [seqs[i].ls[h] * three(seqs[i].qs[h], seqs[i].ks[h], NT) for i, h in units]
    os = [three(p, u, NN) for p, u in zip(ps, us)]
    for (i, h), x, u, o in zip(units, xs, us, os):
        rows, sl = seqs[i].rows, slice(h * dv, (h + 1) * dv)
        x_ref[i * hs + h] = x
        u_ref[rows, sl] = u
        o_ref[rows, sl] = o
        r = lax.rsqrt(jnp.mean(o * o, axis=-1, keepdims=True) + 1e-5)
        pg = pg_ref[rows, sl]
        out_ref[rows, sl] = (o * r * gain * (pg * sigmoid(pg))).astype(bf16)


def bwd_kernel(dims, half, has_before, *refs):
    shared, (x_ref, u_ref, o_ref, dm_ref) = refs[:9], refs[9:13]
    dp_ref, dba_ref, dtaps_ref, dgain_ref, dprm_ref = refs[-5:]
    pg_ref, gain_ref, prm_ref = refs[3], refs[7], refs[8]
    nh, dk, dv = dims
    hs = nh // SPLIT
    wq, wv = hs * dk, hs * dv
    at = half * hs
    iota_r, iota_c, tri, strict = planes(SEQ)
    gain = gain_ref[...]
    prm = prm_ref[...]
    seqs = [Sequence(dims, half, shared, slice(i * SEQ, (i + 1) * SEQ), iota_r, iota_c, tri) for i in range(dm_ref.shape[0] // SEQ)]
    units = [(i, h) for i in range(len(seqs)) for h in range(hs)]
    dgain = jnp.zeros_like(gain)
    dos, us = [], []
    for i, h in units:
        rows, sl = seqs[i].rows, slice(h * dv, (h + 1) * dv)
        o = o_ref[rows, sl]
        pg = pg_ref[rows, sl]
        dm = dm_ref[rows, sl]
        r = lax.rsqrt(jnp.mean(o * o, axis=-1, keepdims=True) + 1e-5)
        nrm = o * r
        sg = sigmoid(pg)
        dp_ref[rows, 2 * wq + wv + h * dv : 2 * wq + wv + (h + 1) * dv] = (dm * nrm * gain * (sg * (1.0 + pg * (1.0 - sg)))).astype(bf16)
        dy = dm * (pg * sg)
        dgain = dgain + jnp.sum(dy * nrm, axis=0, keepdims=True)
        dn = dy * gain
        dos.append(r * (dn - nrm * jnp.mean(nrm * dn, axis=-1, keepdims=True)))
        us.append(u_ref[rows, sl])
    bm = [jnp.where(strict, seqs[i].ls[h] * three(seqs[i].ks[h], seqs[i].ks[h], NT), 0.0) for i, h in units]
    ps = [seqs[i].ls[h] * three(seqs[i].qs[h], seqs[i].ks[h], NT) for i, h in units]
    dps = [three(do, u, NT) for do, u in zip(dos, us)]
    dus = [three(p, do, TN) for p, do in zip(ps, dos)]
    dws = [three(x_ref[i * hs + h], du, TN) for (i, h), du in zip(units, dus)]
    das = [-three(dw, u, NT) for dw, u in zip(dws, us)]

    @pl.when(pl.program_id(0) == 0)
    def _():
        dtaps_ref[...] = jnp.zeros_like(dtaps_ref)
        dgain_ref[...] = jnp.zeros_like(dgain_ref)
        dprm_ref[...] = jnp.zeros_like(dprm_ref)

    dgain_ref[...] += dgain
    lane = lax.broadcasted_iota(jnp.int32, (SEQ, 128), 1)
    ones = jnp.ones((SEQ, 128), f32)
    sc = dk ** -0.5
    for i, q in enumerate(seqs):
        rows, pos = q.rows, q.pos
        dbeta = jnp.zeros((SEQ, 128), f32)
        dlog = jnp.zeros((SEQ, 128), f32)
        dz = ([], [], [])
        for h in range(hs):
            n = i * hs + h
            vh = q.v[:, h * dv : (h + 1) * dv]
            ab = das[n] * bm[n]
            dbeta = jnp.where(lane == at + h, jnp.sum(dws[n] * vh, axis=-1, keepdims=True) + jnp.sum(ab, axis=-1, keepdims=True), dbeta)
            e = q.bs[h] * ab + dps[n] * ps[n]
            dlog = jnp.where(lane == nh + at + h, jnp.sum(e, axis=-1, keepdims=True) - exact_right(e, ones, TN), dlog)
            ds = dps[n] * q.ls[h]
            dmm = jnp.where(strict, q.bs[h] * das[n] * q.ls[h], 0.0)
            dq = sc * three(ds, q.ks[h], NN)
            dkh = three(ds, q.qs[h], TN) + three(dmm, q.ks[h], NN) + three(dmm, q.ks[h], TN)
            qh, rq = q.uq[h]
            kh, rk = q.uk[h]
            dz[0].append(rq * (dq - qh * jnp.sum(qh * dq, axis=-1, keepdims=True)))
            dz[1].append(rk * (dkh - kh * jnp.sum(kh * dkh, axis=-1, keepdims=True)))
            dz[2].append(q.bs[h] * dws[n])
        ddecay = exact_left(tri, dlog, TN)
        drate = -prm[0:1] * ddecay * sigmoid(q.rate)
        dba = dbeta * q.beta * (1.0 - q.beta) + drate
        if has_before:
            dba = dba + refs[13][rows, :]
            dp_ref[rows, 2 * wq + 2 * wv :] = dba.astype(bf16)
        dba_ref[rows, :] = dba
        dprm_ref[0:1, :] += jnp.sum(ddecay * q.decay, axis=0, keepdims=True)
        dprm_ref[1:2, :] += jnp.sum(drate, axis=0, keepdims=True)
        to = 0
        for parts, z, sg, c, tap in zip(dz, q.z, q.sig, q.raw, q.taps):
            d = jnp.concatenate(parts, axis=1) * (sg * (1.0 + z * (1.0 - sg)))
            width = tap.shape[0]
            w = c.shape[1]
            dc = d * tap[width - 1 : width]
            dtaps_ref[width - 1 : width, to : to + w] += jnp.sum(d * c, axis=0, keepdims=True)
            for s in range(1, width):
                m = jnp.where(pos >= s, d, 0.0)
                dc = dc + pltpu.roll(m, SEQ - s, 0) * tap[width - 1 - s : width - s]
                dtaps_ref[width - 1 - s : width - s, to : to + w] += jnp.sum(m * pltpu.roll(c, s, 0), axis=0, keepdims=True)
            dp_ref[rows, to : to + w] = dc.astype(bf16)
            to += w


def shared_specs(dims, off=0):
    nh, dk, dv = dims
    wq, wv = nh // SPLIT * dk, nh // SPLIT * dv
    at = (2 * wq) // wv
    small = (2 * wq + 2 * wv) // 128
    return [
        pl.BlockSpec((ROWS, wq), lambda i: (i + off, 0)),
        pl.BlockSpec((ROWS, wq), lambda i: (i + off, 1)),
        pl.BlockSpec((ROWS, wv), lambda i: (i + off, at)),
        pl.BlockSpec((ROWS, wv), lambda i: (i + off, at + 1)),
        pl.BlockSpec((ROWS, 128), lambda i: (i + off, small)),
        pl.BlockSpec((ROWS, 1), lambda i: (i + off, 0)),
        pl.BlockSpec((4, 2 * wq + wv), lambda i: (0, 0)),
        pl.BlockSpec((1, dv), lambda i: (0, 0)),
        pl.BlockSpec((8, 128), lambda i: (0, 0)),
    ]


def cost(us):
    return pl.CostEstimate(flops=int(us * 1.1e9), bytes_accessed=int(us * 1e6), transcendentals=0)


def mixer_fwd(proj, first, pos, taps, gain, prm, dims, half, part=None, filled=()):
    tok = pos.shape[0]
    nh, dk, dv = dims
    hs = nh // SPLIT
    ns = tok // SEQ
    wv = hs * dv
    steps = ns // PAIR if part is None else ns // PAIR // 2
    off = part * steps if part else 0
    row = pl.BlockSpec((ROWS, wv), lambda i: (i + off, 0))
    args = [proj, proj, proj, proj, first, pos, taps, gain, prm, *filled]
    return pl.pallas_call(
        functools.partial(fwd_kernel, dims, half),
        grid=(steps,),
        in_specs=shared_specs(dims, off) + [pl.BlockSpec(memory_space=pl.ANY)] * len(filled),
        out_specs=[
            pl.BlockSpec((ROWS, wv), lambda i: (i + off, half)),
            pl.BlockSpec((PAIR * hs, SEQ, SEQ), lambda i: (i + off, 0, 0)),
            row,
            row,
        ],
        out_shape=[
            jax.ShapeDtypeStruct((tok, nh * dv), bf16),
            jax.ShapeDtypeStruct((ns * hs, SEQ, SEQ), f32),
            jax.ShapeDtypeStruct((tok, wv), f32),
            jax.ShapeDtypeStruct((tok, wv), f32),
        ],
        input_output_aliases={9 + i: i for i in range(len(filled))},
        cost_estimate=cost(4 if part is None else 12),
        compiler_params=pltpu.CompilerParams(vmem_limit_bytes=48 << 20),
    )(*args)


def mixer_bwd(proj, first, pos, taps, gain, prm, x, u, o, dm, dims, half, part, before=None, filled=None):
    tok = pos.shape[0]
    nh, dk, dv = dims
    hs = nh // SPLIT
    ns = tok // SEQ
    wq, wv = hs * dk, hs * dv
    steps = dm.shape[0] // ROWS
    off = part * steps
    row = pl.BlockSpec((ROWS, wv), lambda i: (i + off, 0))
    lanes = pl.BlockSpec((ROWS, 128), lambda i: (i + off, 0))
    specs = shared_specs(dims, off) + [
        pl.BlockSpec((PAIR * hs, SEQ, SEQ), lambda i: (i + off, 0, 0)), row, row, pl.BlockSpec((ROWS, wv), lambda i: (i, half))]
    args = [proj, proj, proj, proj, first, pos, taps, gain, prm, x, u, o, dm]
    width = 2 * wq + 2 * wv
    if before is not None:
        args.append(before)
        specs.append(lanes)
        width += 128
    alias = {}
    if filled is not None:
        alias = {len(args): 0, len(args) + 1: 1}
        args += filled
        specs += [pl.BlockSpec(memory_space=pl.ANY)] * 2
    return pl.pallas_call(
        functools.partial(bwd_kernel, dims, half, before is not None),
        grid=(steps,),
        in_specs=specs,
        out_specs=[
            pl.BlockSpec((ROWS, width), lambda i: (i + off, 0)),
            lanes,
            pl.BlockSpec((4, 2 * wq + wv), lambda i: (0, 0)),
            pl.BlockSpec((1, dv), lambda i: (0, 0)),
            pl.BlockSpec((8, 128), lambda i: (0, 0)),
        ],
        out_shape=[
            jax.ShapeDtypeStruct((tok, width), bf16),
            jax.ShapeDtypeStruct((tok, 128), f32),
            jax.ShapeDtypeStruct((4, 2 * wq + wv), f32),
            jax.ShapeDtypeStruct((1, dv), f32),
            jax.ShapeDtypeStruct((8, 128), f32),
        ],
        input_output_aliases=alias,
        cost_estimate=cost(26),
        compiler_params=pltpu.CompilerParams(vmem_limit_bytes=56 << 20),
    )(*args)


def xor_send(value, axis, size, step):
    return lax.ppermute(value, axis, [(i, i ^ step) for i in range(size)])


def after(value, *needs):
    return lax.optimization_barrier((value, *needs))[0]


def lines(size):
    return [[low + 2 * i for i in range(size // 2)] for low in range(2)]


def gather_line(rows, size):
    return lax.all_gather(rows, "fsdp", axis=0, tiled=True, axis_index_groups=lines(size))


def gather_side(near, size, *needs):
    got = xor_send(after(near, *needs) if needs else near, "fsdp", size, 1)
    return jnp.concatenate([near, got], axis=0), got


def gather_side_first(rows, size, *needs):
    got = xor_send(after(rows, *needs), "fsdp", size, 1)
    full = gather_line(jnp.concatenate([rows, got], axis=0), size)
    width = rows.shape[1]
    return full.reshape(size // 2, 2, -1, width).swapaxes(0, 1).reshape(-1, width), full, got


def dot(left, right, dims=NN, out=f32):
    return lax.dot_general(left, right, dims, preferred_element_type=f32).astype(out)


class Summed:
    def __init__(self, left, right, size, *needs):
        self.size = size
        self.half = left.shape[1] // 2
        self.left, self.right = left, right
        self.sent = dot(left[:, self.half :], right, TN, bf16)
        self.got = xor_send(after(self.sent, *needs) if needs else self.sent, "fsdp", size, 1)

    def side(self, *needs, before=()):
        keep = dot(self.left[:, : self.half], after(self.right, *needs) if needs else self.right, TN)
        self.low = (keep + self.got.astype(f32)).astype(bf16)
        ready = after(self.low, *before) if before else self.low
        self.sum = lax.psum_scatter(ready, "fsdp", scatter_dimension=0, tiled=True, axis_index_groups=lines(self.size))

    def total(self, ranks, *needs):
        ready = after(self.sum, *needs) if needs else self.sum
        return lax.all_to_all(ready.reshape(ranks, -1, ready.shape[1]), "rep", 0, 0)


def join_tokens(rows, size, meanwhile=None):
    half = size // 2

    def around(block):
        held = {0: block}
        step = half // 2
        while step:
            for j in list(held):
                held[j ^ step] = xor_send(held[j], "rep", size, step)
            step //= 2
        return jnp.concatenate([held[j] for j in range(half)], axis=0)

    beyond = xor_send(rows, "rep", size, half)
    near = around(rows)
    if meanwhile is not None:
        return near, around(after(beyond, meanwhile(near))), beyond
    return near, around(beyond), beyond


def sum_tokens(far, near, size, *needs, last=False):
    half = size // 2

    def around(part, *first):
        held = jnp.split(part, half, axis=0)
        step = 1
        while step < half:
            for j in range(0, half, 2 * step):
                low = held[j + step].astype(bf16)
                held[j] = held[j] + xor_send(after(low, *first) if first else low, "rep", size, step).astype(f32)
            step *= 2
        return held[0]

    beyond = around(far()).astype(bf16)
    part = near(beyond)
    if needs:
        beyond = after(beyond, *needs)
    got = xor_send(beyond, "rep", size, half)
    return around(part, *([got] if last else [])) + got.astype(f32), got


def rms(values):
    return lax.rsqrt(jnp.mean(values * values, axis=-1, keepdims=True) + 1e-06)


def norm_back(n, r, gain, dout):
    scaled = dout * gain
    return r * (scaled - n * jnp.mean(n * scaled, axis=-1, keepdims=True)), jnp.sum(dout * n, axis=0)


def make(F, R):
    both = ("fsdp", "rep")

    def on_device(tokens, segments, cotangent, gain_one, w_query, w_key, w_value, w_gate, w_beta, w_alpha, conv_q, conv_k,
                  conv_v, a_log, dt_bias, norm_gain, w_out, gain_two, w_ffgate, w_ffup, w_down):
        f = lax.axis_index("fsdp")
        r = lax.axis_index("rep")
        N = F * R
        rows_own, D = tokens.shape
        heads = a_log.shape[0]
        dk = w_query.shape[1] // heads
        dv = w_value.shape[1] // heads
        nh = heads // R
        dims = (nh, dk, dv)
        wq, wv = nh * dk, nh * dv
        hq, hv = wq // SPLIT, wv // SPLIT
        shard = D // N
        block = D // F
        ffq = w_ffgate.shape[1] // R
        tok = rows_own * R
        ns = tok // SEQ
        tiny = dv // N
        per = conv_v.shape[1] // shard

        low_bit = f & 1

        def swap(array, axis):
            half = array.shape[axis] // 2
            return jnp.concatenate(
                [lax.dynamic_slice_in_dim(array, (low_bit ^ j) * half, half, axis=axis) for j in range(2)], axis=axis)

        def mix(array, axis):
            at = [slice(None)] * array.ndim
            parts = []
            for bit in range(2):
                for i in range(F // 2):
                    at[axis] = slice((2 * i + bit) * block, (2 * i + bit + 1) * block)
                    parts.append(array[tuple(at)])
            return swap(jnp.concatenate(parts, axis=axis), axis)

        def unmix(array, axis):
            array = swap(array, axis)
            at = [slice(None)] * array.ndim
            parts = []
            for i in range(F // 2):
                for bit in range(2):
                    p = bit * (F // 2) + i
                    at[axis] = slice(p * block, (p + 1) * block)
                    parts.append(array[tuple(at)])
            return jnp.concatenate(parts, axis=axis)

        def quarter(arrays):
            return jnp.concatenate([a.reshape(shard, R, -1) for a in arrays], axis=2)

        def spread(packed, *needs):
            packed = packed.transpose(1, 0, 2)
            if needs:
                packed = after(packed, *needs)
            return lax.all_to_all(packed, "rep", 0, 0).reshape(R * shard, -1)

        extra = jnp.concatenate(
            [gain_one[:, None], gain_two[:, None], conv_q.T, conv_k.T,
             conv_v.reshape(4, shard, per).transpose(1, 0, 2).reshape(shard, 4 * per),
             jnp.pad(norm_gain, (0, shard - tiny))[:, None]], axis=1).T
        small = jnp.concatenate([w_beta.reshape(shard, R, nh), w_alpha.reshape(shard, R, nh)], axis=2)
        small = jnp.pad(small, ((0, 0), (0, 0), (0, 128 - 2 * nh)))

        def halves(array, width):
            parts = array.reshape(shard, R, SPLIT, width)
            return [parts[:, :, h] for h in range(SPLIT)]

        q_h, k_h, v_h, g_h = halves(w_query, hq), halves(w_key, hq), halves(w_value, hv), halves(w_gate, hv)
        own = mix(tokens, 1)
        part_a = spread(jnp.concatenate([q_h[0], k_h[0], v_h[0], g_h[0], small, q_h[1], k_h[1], v_h[1], g_h[1]], axis=2))
        w1 = 2 * hq + 2 * hv
        part_a = after(part_a, own)
        part_1, part_2 = part_a[:, : w1 + 128], part_a[:, w1 + 128 :]
        extra_all = lax.all_to_all(jnp.broadcast_to(after(extra, part_a)[None], (N, *extra.shape)), both, 0, 0)
        extra_all = extra_all.transpose(1, 0, 2).reshape(-1, D).astype(f32)
        line_1 = gather_line(part_1, F)
        every_near, every_far, every_got = join_tokens(own, R)
        every = jnp.concatenate([every_near, every_far], axis=0)
        ids_all = jnp.concatenate(join_tokens(segments[:, None], R)[:2], axis=0).reshape(ns, SEQ)
        part_r = spread(quarter([w_out.T, w_ffgate, w_ffup, w_down.T]), extra_all, every_got, line_1)
        gains = mix(extra_all[:2], 1)
        gain_first, gain_second = gains[0:1], gains[1:2]
        every32 = every.astype(f32)
        normed_one = (every32 * rms(every32) * gain_first).astype(bf16)
        cot = mix(cotangent, 1)
        part_r = after(part_r, normed_one, cot)
        part_b, part_g, part_u, part_d = (
            part_r[:, :wv], part_r[:, wv : wv + ffq], part_r[:, wv + ffq : wv + 2 * ffq], part_r[:, wv + 2 * ffq :])
        line_2 = gather_line(after(part_2, extra_all), F)
        wa1, side_1 = gather_side(line_1, F)
        cot_near, cot_far, unused = join_tokens(after(cot, side_1), R)
        line_b = gather_line(part_b, F)
        line_g = gather_line(after(part_g, side_1), F)
        wu, line_u, got_u = gather_side_first(part_u, F, side_1)
        line_d = gather_line(after(part_d, side_1), F)

        cq = lax.dynamic_slice_in_dim(extra_all[2:6], r * wq, wq, axis=1)
        ck = lax.dynamic_slice_in_dim(extra_all[6:10], r * wq, wq, axis=1)
        cv = extra_all[10 : 10 + 4 * per].reshape(4, per, D).transpose(0, 2, 1).reshape(4, D * per)
        cv = lax.dynamic_slice_in_dim(cv, r * wv, wv, axis=1)
        gain_out = extra_all[10 + 4 * per].reshape(N, shard)[:, :tiny].reshape(1, dv)
        taps = [jnp.concatenate([cq[:, h * hq : (h + 1) * hq], ck[:, h * hq : (h + 1) * hq], cv[:, h * hv : (h + 1) * hv]], axis=1)
                for h in range(SPLIT)]
        prm = jnp.stack([jnp.exp(lax.dynamic_slice_in_dim(a_log, r * nh, nh)), lax.dynamic_slice_in_dim(dt_bias, r * nh, nh)])
        prm = jnp.pad(prm, ((0, 6), (nh, 128 - 2 * nh)))
        place = jnp.arange(SEQ)
        same = (ids_all[:, :, None] == ids_all[:, None, :]) & (place[:, None] >= place[None, :])[None]
        pos = (jnp.sum(same.astype(f32), axis=2) - 1.0).reshape(tok, 1)

        proj_1 = dot(after(normed_one, part_r), wa1)
        mixed, x_1, u_1, o_1 = mixer_fwd(proj_1, proj_1, pos, taps[0], gain_out, prm, dims, 0)
        wa2, side_2 = gather_side(line_2, F, side_1)
        proj_2 = dot(after(normed_one, mixed, line_b, got_u), wa2)
        mixed, *saved_2 = mixer_fwd(proj_2, proj_1, pos, taps[1], gain_out, prm, dims, 1, 1, [mixed])
        wb, side_b = gather_side(line_b, F, side_2)
        wg, side_g = gather_side(line_g, F, side_b)
        side_d = xor_send(after(line_d, side_g), "fsdp", F, 1)
        own32 = own.astype(f32)
        mid = tok // 2
        mixed = after(mixed, line_g, cot_near, cot_far)
        out_far = dot(mixed[mid:], wb, NT)
        kept = {}

        def keep(name, value):
            kept[name] = value
            return value

        def near_mixed(part):
            kept["mixed"], *kept["saved"] = mixer_fwd(
                proj_2, proj_1, after(pos, part), taps[1], gain_out, prm, dims, 1, 0, [mixed, *saved_2])
            return dot(kept["mixed"][:mid], wb, NT)

        added, unused = sum_tokens(lambda: out_far, near_mixed, R, last=True)
        mixed, saved_2 = kept["mixed"], kept["saved"]
        middle = own32 + after(added, side_g, line_u, line_d)
        r2 = rms(middle)
        n2 = middle * r2
        normed_own = (n2 * gain_second).astype(bf16)
        gates, ups, acts, sigs, hiddens = [], [], [], [], []

        def gate(normed):
            gates.append(dot(normed, wg))
            return gates[-1]

        *two, beyond = join_tokens(normed_own, R, gate)
        gate(two[1])
        side_d = after(side_d, gates[1])
        wd = jnp.concatenate([after(line_d, gates[0]), side_d], axis=0)
        for t, normed in enumerate(two):
            ups.append(dot(after(normed, gates[1]) if t else after(normed, beyond), wu))
            sigs.append(jax.nn.sigmoid(gates[t]))
            acts.append(gates[t] * sigs[t])
            hiddens.append((acts[t] * ups[t]).astype(bf16))
        hidden = jnp.concatenate(hiddens, axis=0)
        normed_two = jnp.concatenate(two, axis=0)
        cot_all = jnp.concatenate([cot_near, cot_far], axis=0)

        g_down = Summed(cot_all, hidden, F)
        dgates, dups = [None, None], [None, None]

        def back_two(t, *needs):
            dhidden = dot(after((cot_near, cot_far)[t], *needs), wd)
            dgates[t] = (dhidden * ups[t] * (sigs[t] * (1.0 + gates[t] * (1.0 - sigs[t])))).astype(bf16)
            dups[t] = (dhidden * acts[t]).astype(bf16)
            return dot(dgates[t], wg, NT) + dot(dups[t], wu, NT)

        dnormed_two, far_two = sum_tokens(lambda: back_two(1, g_down.sent), lambda part: keep("two", back_two(0, part)), R)
        g_down.side(kept["two"])
        g_gate = Summed(normed_two, after(jnp.concatenate(dgates, axis=0), g_down.low), F, g_down.got)
        dinner, dgain_second = norm_back(n2, r2, gain_second, after(dnormed_two, g_gate.sent))
        dmiddle = cot.astype(f32) + dinner
        dmiddle_own = dmiddle.astype(bf16)
        dlow = join_tokens(dmiddle_own, R)[:2]
        dm_near = dot(dlow[0], wb)
        args_2 = (proj_2, proj_1, pos, taps[1], gain_out, prm, *saved_2)
        args_1 = (proj_1, proj_1, pos, taps[0], gain_out, prm, x_1, u_1, o_1)
        dp_2, dba, dt_2, dg_2, dr_2 = mixer_bwd(*args_2, dm_near, dims, 1, 0)
        g_up = Summed(normed_two, after(jnp.concatenate(dups, axis=0), dba), F, g_gate.got)
        g_gate.side(g_up.sent)
        dp_1, dba_1, dt_1, dg_1, dr_1 = mixer_bwd(*args_1, after(dm_near, g_gate.low, g_down.sum), dims, 0, 0, dba)
        t_down = g_down.total(R)
        g_out = Summed(jnp.concatenate(dlow, axis=0), after(mixed, dba_1), F)
        dm_far = dot(after(dlow[1], dba_1), wb)
        dp_2, dba, et_2, eg_2, er_2 = mixer_bwd(*args_2, after(dm_far, g_out.sent), dims, 1, 1, None, [dp_2, dba])
        g_up.side(dba)
        g_2 = Summed(normed_one, after(dp_2, g_up.low, g_gate.sum), F)
        t_gate = g_gate.total(R)
        dp_1, dba_1, et_1, eg_1, er_1 = mixer_bwd(
            *args_1, after(dm_far, g_2.sent, t_down), dims, 0, 1, dba, [dp_1, dba_1])
        g_out.side(dp_1)
        g_1 = Summed(normed_one, after(dp_1, g_out.low), F)

        def back_one(lo, hi, *needs):
            return dot(after(dp_1, *needs)[lo:hi], wa1, NT) + dot(after(dp_2, *needs)[lo:hi], wa2, NT)


        def near_one(part):
            g_2.side(part, g_out.sum)

            kept["t_up"], kept["t_out"] = g_up.total(R, g_2.low), g_out.total(R, g_2.low)
            keep("far", dot(after(hiddens[1], g_2.low, g_out.sum), wd, NT))
            return keep("one", back_one(0, mid, kept["far"]))

        dnormed_one, far_one = sum_tokens(lambda: back_one(mid, tok, g_1.sent, g_up.sum, t_gate), near_one, R)
        t_up, t_out = kept["t_up"], kept["t_out"]
        near_out = dot(after(hiddens[0], kept["one"]), wd, NT)
        g_1.side(near_out, t_up, before=(g_2.sum,))
        added, unused = sum_tokens(lambda: kept["far"], lambda part: after(near_out, t_out, g_1.low), R)
        layer_out = (middle + after(added, g_1.sum)).astype(bf16)
        dprm = dr_1 + dr_2 + er_1 + er_2
        dgain_out = dg_1 + dg_2 + eg_1 + eg_2
        dtaps = [dt_1 + et_1, dt_2 + et_2]

        n1 = own32 * rms(own32)
        dfirst, dgain_first = norm_back(n1, rms(own32), gain_first, dnormed_one)
        grad_tokens = unmix(dmiddle + dfirst, 1)

        def wide(parts):
            return parts.astype(f32).transpose(1, 0, 2).reshape(shard, -1)

        def tall(parts):
            return parts.astype(f32).transpose(0, 2, 1).reshape(-1, shard)

        t_2 = g_2.total(R)
        t_1 = g_1.total(R)

        def joined(lo, width):
            return jnp.stack([t[:, :, lo : lo + width] for t in (t_1, t_2)], axis=2).astype(f32).transpose(1, 0, 2, 3).reshape(shard, -1)

        grad_query, grad_key = joined(0, hq), joined(hq, hq)
        grad_value, grad_gate_w = joined(2 * hq, hv), joined(2 * hq + hv, hv)
        grad_beta, grad_alpha = wide(t_1[:, :, w1 : w1 + nh]), wide(t_1[:, :, w1 + nh : w1 + 2 * nh])
        grad_down, grad_out = tall(t_down), tall(t_out)
        grad_gate, grad_up = wide(t_gate), wide(t_up)

        def placed(parts, total, width):
            part = jnp.concatenate(parts, axis=1)
            return lax.dynamic_update_slice(jnp.zeros((4, total), f32), part, (0, r * width))

        gq = placed([dtaps[h][:, :hq] for h in range(SPLIT)], R * wq, wq)
        gk = placed([dtaps[h][:, hq : 2 * hq] for h in range(SPLIT)], R * wq, wq)
        gv = placed([dtaps[h][:, 2 * hq :] for h in range(SPLIT)], R * wv, wv)
        heads_part = lax.dynamic_update_slice(jnp.zeros((2, heads), f32), dprm[:2, nh : 2 * nh], (0, r * nh)).reshape(1, -1)
        packed = jnp.concatenate([
            unmix(dgain_first[None], 1).reshape(N, -1),
            unmix(dgain_second[None], 1).reshape(N, -1),
            gq.reshape(4, N, -1).transpose(1, 0, 2).reshape(N, -1),
            gk.reshape(4, N, -1).transpose(1, 0, 2).reshape(N, -1),
            gv.reshape(4, N, -1).transpose(1, 0, 2).reshape(N, -1),
            dgain_out.reshape(N, tiny),
            jnp.broadcast_to(heads_part, (N, 2 * heads))], axis=1)
        summed = jnp.sum(lax.all_to_all(packed, both, 0, 0, tiled=True), axis=0)
        sizes = [shard, shard, 4 * shard, 4 * shard, 4 * shard * per, tiny, heads, heads]
        ends = [0]
        for size in sizes:
            ends.append(ends[-1] + size)
        pick = [summed[ends[i] : ends[i + 1]] for i in range(len(sizes))]
        return (
            unmix(layer_out, 1), grad_tokens, pick[0], grad_query, grad_key, grad_value, grad_gate_w, grad_beta, grad_alpha,
            pick[2].reshape(4, shard), pick[3].reshape(4, shard), pick[4].reshape(4, shard * per), pick[6], pick[7], pick[5],
            grad_out, pick[1], grad_gate, grad_up, grad_down)

    return on_device


def solution(mesh):
    rows, cols, flat = P(("fsdp", "rep"), None), P(None, ("fsdp", "rep")), P(("fsdp", "rep"))
    placed = (rows, flat, rows, flat, rows, rows, rows, rows, rows, rows, cols, cols, cols, P(), P(), flat, cols, flat, rows, rows, cols)
    made = (rows, rows, flat, rows, rows, rows, rows, rows, rows, cols, cols, cols, P(), P(), flat, cols, flat, rows, rows, cols)
    return jax.shard_map(
        make(mesh.shape["fsdp"], mesh.shape["rep"]), mesh=mesh, in_specs=placed, out_specs=made, check_vma=False)
```
